128 devices in a mesh: ctx: 128 (over z, x, y, core).
Axes of the slice: x: 4, y: 4, z: 4, core: 2. Of those that a mesh axis runs over, the one named last changes fastest.
Arguments:
- queries: bfloat16 [65536, 2048], P('ctx'), may hold values from -13 to 13
- keys: bfloat16 [65536, 2048], P('ctx'), may hold values from -13 to 13
- values: bfloat16 [65536, 2048], P('ctx'), may hold values from -6 to 6
- chosen: int32 [128, 16, 3], P('ctx'), may hold values from 0 to 127, as said below
Outputs:
- attended: bfloat16 [65536, 2048], P('ctx')
The draws below stay inside these ranges and needn't reach their ends.
Inputs may be any that keep to these rules, and one draw needn't show every extreme that they name: chosen[b, h, :] are three different blocks, none equal to b; over the 48 entries of one query block no block appears more than 1 times, and some block appears exactly 1 times.
All inputs are finite; a program needn't handle non-finite values.
Results may differ from the reference program's by a relative error of at most 0.0049.
Values may be sent and summed in bfloat16 or wider, within the bound.
No kernel may reach another device: no remote copies, remote signals or barrier semaphores. Data moves between devices by JAX's collectives and lax.ppermute only.
A program may use at most 192 MiB of HBM per device.

```python
import math
import jax
import jax.numpy as jnp
from jax import lax

H = 16
HEAD = 128
BLOCK = 512
D = 2048
TOKENS = 65536
N_CTX = 128


def draw_queries(key, part):
    key = jax.random.fold_in(key, 1)
    result = jnp.clip(jax.random.normal(key, (TOKENS, D), jnp.float32), -6.0, 6.0)
    return result.astype(jnp.bfloat16)


def draw_keys(key, part):
    key = jax.random.fold_in(key, 2)
    result = jnp.clip(jax.random.normal(key, (TOKENS, D), jnp.float32), -6.0, 6.0)
    return result.astype(jnp.bfloat16)


def draw_chosen(key, part):
    key = jax.random.fold_in(key, 11)
    subkeys = jax.random.split(key, N_CTX)

    def one_block(subkey, block_id):
        order = jax.random.permutation(subkey, N_CTX - 1).astype(jnp.int32)
        others = order + (order >= block_id).astype(jnp.int32)
        places = jnp.arange(3 * H) % (N_CTX - 1)
        return others[places].reshape(H, 3)
    return jax.vmap(one_block)(subkeys, jnp.arange(N_CTX, dtype=jnp.int32)).astype(jnp.int32)


def levels(key, shape, cuts, smallest, top_value):
    factor_of, own = 1.0, jax.random.fold_in(key, 6)
    for axis_at, parts in cuts:
        heights = jnp.exp(jax.random.uniform(jax.random.fold_in(own, axis_at), (parts,), jnp.float32, smallest / len(cuts), top_value / len(cuts)))
        factor_of = factor_of * jnp.repeat(heights, shape[axis_at] // parts).reshape([-1 if axis == axis_at else 1 for axis in range(len(shape))])
    return factor_of


def normal_values(key, shape, deviation, reach, shards=(), kind=jnp.bfloat16):
    gain = levels(key, shape, shards, -0.22, 0.18) if shards else 1.0
    array = jax.random.normal(key, shape, jnp.float32) * deviation * gain
    return jnp.minimum(jnp.maximum(array, -reach), reach).astype(kind)


def setup_inputs(seed: int = 0) -> dict:
    key_list = jax.random.split(jax.random.key(seed), 5)
    queries = draw_queries(jax.random.fold_in(key_list[4], 71), 0)
    keys = draw_keys(jax.random.fold_in(key_list[4], 71), 0)
    values = normal_values(key_list[2], (TOKENS, D), 1.0, 6.0, ((0, 128),))
    chosen = draw_chosen(jax.random.fold_in(key_list[4], 71), 0)
    return dict(queries=queries, keys=keys, values=values, chosen=chosen)


def reference(queries, keys, values, chosen):
    query_blk = queries.reshape(N_CTX, BLOCK, H, HEAD)
    key_heads = keys.reshape(N_CTX, BLOCK, H, HEAD).transpose(0, 2, 1, 3)
    value_heads = values.reshape(N_CTX, BLOCK, H, HEAD).transpose(0, 2, 1, 3)
    head_iota = jnp.arange(H)[:, None]
    scale = 1.0 / math.sqrt(HEAD)
    row_iota = jnp.arange(BLOCK)[:, None]
    col_iota = jnp.arange(4 * BLOCK)[None, :]
    allowed = (col_iota >= BLOCK) | (col_iota <= row_iota)

    def one_block(block_id):
        query_now = lax.dynamic_index_in_dim(query_blk, block_id, 0, keepdims=False)
        own_key = lax.dynamic_index_in_dim(key_heads, block_id, 0, keepdims=False)
        own_value = lax.dynamic_index_in_dim(value_heads, block_id, 0, keepdims=False)
        picks = lax.dynamic_index_in_dim(chosen, block_id, 0, keepdims=False)
        sel_key = key_heads[picks, head_iota]
        sel_value = value_heads[picks, head_iota]
        key_all = jnp.concatenate([own_key[:, None], sel_key], axis=1).reshape(H, 4 * BLOCK, HEAD)
        value_all = jnp.concatenate([own_value[:, None], sel_value], axis=1).reshape(H, 4 * BLOCK, HEAD)
        scores = jnp.einsum('qhd,hkd->hqk', query_now.astype(jnp.float32), key_all.astype(jnp.float32)) * scale
        scores = jnp.where(allowed[None], scores, -jnp.inf)
        highest = lax.optimization_barrier(jnp.max(scores, axis=-1, keepdims=True))
        expo = jnp.exp(scores - highest)
        weights = (expo / lax.optimization_barrier(jnp.sum(expo, axis=-1, keepdims=True))).astype(jnp.bfloat16)
        output = jnp.einsum('hqk,hkd->qhd', weights.astype(jnp.float32), value_all.astype(jnp.float32))
        return output.astype(jnp.bfloat16).reshape(BLOCK, H * HEAD)
    result = lax.map(one_block, jnp.arange(N_CTX))
    return result.reshape(TOKENS, H * HEAD)
```

```python
import math

import jax
import jax.numpy as jnp
from jax import lax
from jax.experimental import pallas as pl
from jax.experimental.pallas import tpu as pltpu
from jax.sharding import PartitionSpec as P

HEAD = 128
HEADS = 16
BLOCK = 512
DEVICES = 128
CHIPS = 64
SCALE = math.log2(math.e) / math.sqrt(HEAD)

ONE = [(1, 0, 0), (3, 0, 0), (0, 1, 0), (0, 3, 0), (0, 0, 1), (0, 0, 3)]
PARTNER = 6
SHIFTS = [(0, 0, 0, 1)] * PARTNER
SHIFTS += [(*s, c) for s in ONE for c in (0, 1)]
KINDS = len(SHIFTS)
SPARE = 4
PIECE = 16
SLOT_ROWS = 2 * BLOCK + SPARE * PIECE

ROW_DIRECT = CHIPS
ROW_SPARE = ROW_DIRECT + CHIPS
ROW_FORWARD = ROW_SPARE + CHIPS
ROW_FORWARD_HEAD = ROW_FORWARD + 32
ROW_FROM = ROW_FORWARD_HEAD + 32
ROW_FROM_RANK = ROW_FROM + 8
ROW_FROM_HEAD = ROW_FROM_RANK + 8
ROW_PARTNER = ROW_FROM_HEAD + 8
ROW_LEFT = ROW_PARTNER + 1
ROWS = ROW_PARTNER + 8


def through(device, shift):
    z, x, y, c = device // 32, device // 8 % 4, device // 2 % 4, device % 2
    dz, dx, dy, dc = shift
    return (((z + dz) % 4 * 4 + (x + dx) % 4) * 4 + (y + dy) % 4) * 2 + (c ^ dc)


def shift_pairs(shift):
    return [(through(b, shift), b) for b in range(DEVICES)]


def roll_lanes(array, amount):
    amount = amount % DEVICES
    return pltpu.roll(array, amount, 1) if amount else array


def permuted(array, shift, lane, inverse=False):
    dz, dx, dy, dc = shift
    if inverse:
        dz, dx, dy = -dz % 4, -dx % 4, -dy % 4
    if dz:
        array = roll_lanes(array, -32 * dz)
    if dx:
        inside = (lane // 8) % 4 + dx < 4
        array = jnp.where(inside, roll_lanes(array, -8 * dx), roll_lanes(array, 32 - 8 * dx))
    if dy:
        inside = (lane // 2) % 4 + dy < 4
        array = jnp.where(inside, roll_lanes(array, -2 * dy), roll_lanes(array, 8 - 2 * dy))
    if dc:
        array = jnp.where(lane % 2 == 0, roll_lanes(array, -1), roll_lanes(array, 1))
    return array


def plan_kernel(chosen_ref, out_ref):
    chip = lax.broadcasted_iota(jnp.int32, (CHIPS, DEVICES), 0)
    lane = lax.broadcasted_iota(jnp.int32, (CHIPS, DEVICES), 1)
    even = jnp.zeros((CHIPS, DEVICES), jnp.int32)
    odd = jnp.zeros((CHIPS, DEVICES), jnp.int32)
    for entry in range(3 * HEADS):
        owner = chosen_ref[entry : entry + 1, :]
        even = even + jnp.where(owner == 2 * chip, entry // 3 + 1, 0)
        odd = odd + jnp.where(owner == 2 * chip + 1, entry // 3 + 1, 0)
    home = lane // 2 == chip
    partner = jnp.sum(jnp.where(home, even + odd, 0), axis=0, keepdims=True)
    even = jnp.where(home, 0, even)
    odd = jnp.where(home, 0, odd)
    waiting = jnp.where(even > 0, odd, 0)
    slot = jnp.where(even > 0, even - 1, jnp.where(odd > 0, odd + 15, 0))
    direct = jnp.where(even > 0, even, odd)
    free = jnp.where(home, 0, jnp.where(direct > 0, 0, 1))
    options = jnp.zeros((CHIPS, DEVICES), jnp.int32)
    for shift in sorted(set(SHIFTS)):
        options = options + permuted(free, shift, lane)
    score = options * 64 + (chip + 17 * lane) % 64
    big = 1 << 20
    out_ref[...] = jnp.zeros((ROWS, DEVICES), jnp.int32)
    for kind, shift in enumerate(SHIFTS):
        able = (waiting > 0) & (permuted(free, shift, lane) > 0)
        rated = jnp.where(able, score, big)
        best = jnp.min(rated, axis=0, keepdims=True)
        picked = able & (rated == best)
        head = jnp.sum(jnp.where(picked, waiting, 0), axis=0, keepdims=True)
        back = permuted(jnp.where(picked, waiting + 16, 0), shift, lane, inverse=True)
        waiting = jnp.where(picked, 0, waiting)
        slot = jnp.where(back > 0, back - 1, slot)
        free = jnp.where(back > 0, 0, free)
        forward = jnp.sum(jnp.where(back > 0, chip, 0), axis=0, keepdims=True)
        out_ref[ROW_FORWARD + kind : ROW_FORWARD + kind + 1, :] = forward
        out_ref[ROW_FORWARD_HEAD + kind : ROW_FORWARD_HEAD + kind + 1, :] = head
    before = lax.broadcasted_iota(jnp.int32, (DEVICES, DEVICES), 0)
    after = lax.broadcasted_iota(jnp.int32, (DEVICES, DEVICES), 1)
    earlier = jnp.where((before < after) & (before % 2 == after % 2), 1.0, 0.0)
    rank = jnp.dot(
        jnp.where(waiting > 0, 1.0, 0.0), earlier, preferred_element_type=jnp.float32
    ).astype(jnp.int32)
    spare = jnp.zeros((CHIPS, DEVICES), jnp.int32)
    for index in range(SPARE):
        for core in range(2):
            chosen = (rank == index) & (lane % 2 == core)
            head = jnp.sum(jnp.where(chosen, waiting, 0), axis=1, keepdims=True)
            spare = jnp.where(lane == 2 * index + core, head, spare)
    out_ref[ROW_SPARE : ROW_SPARE + CHIPS, :] = spare
    excess = jnp.where((waiting > 0) & (rank >= SPARE), 1, 0)
    for index in range(SPARE):
        best = jnp.min(jnp.where(waiting > 0, chip, big), axis=0, keepdims=True)
        picked = (waiting > 0) & (chip == best)
        out_ref[ROW_FROM + index : ROW_FROM + index + 1, :] = jnp.where(best < big, best, 0)
        out_ref[ROW_FROM_RANK + index : ROW_FROM_RANK + index + 1, :] = jnp.minimum(
            jnp.sum(jnp.where(picked, rank, 0), axis=0, keepdims=True), SPARE - 1
        )
        out_ref[ROW_FROM_HEAD + index : ROW_FROM_HEAD + index + 1, :] = jnp.sum(
            jnp.where(picked, waiting, 0), axis=0, keepdims=True
        )
        waiting = jnp.where(picked, 0, waiting)
    excess = excess + waiting
    out_ref[ROW_PARTNER : ROW_PARTNER + 1, :] = partner
    left = jnp.max(jnp.max(excess, axis=0, keepdims=True), axis=1, keepdims=True)
    out_ref[ROW_LEFT : ROW_LEFT + 1, :] = jnp.broadcast_to(left, (1, DEVICES))
    out_ref[0:CHIPS, :] = slot
    out_ref[ROW_DIRECT : ROW_DIRECT + CHIPS, :] = direct


def make_plan(chosen_all):
    return pl.pallas_call(
        plan_kernel,
        out_shape=jax.ShapeDtypeStruct((ROWS, DEVICES), jnp.int32),
        name="plan",
    )(chosen_all)


def columns(head):
    return pl.ds(pl.multiple_of(head * HEAD, HEAD), HEAD)


def pack_kernel(plan, me_ref, keys, values, other_keys, other_values, send, sem):
    me = me_ref[0]
    chip, core = me // 2, me % 2

    def one_slot(dest, carry):
        code = plan[chip, 2 * dest + core]
        head = code % 16

        @pl.when(code // 16 == core)
        def _():
            for half, source in enumerate((keys, values)):
                pltpu.make_async_copy(
                    source.at[:, columns(head)], send.at[dest, pl.ds(half * BLOCK, BLOCK)], sem
                ).start()

        @pl.when(code // 16 != core)
        def _():
            for half, source in enumerate((other_keys, other_values)):
                pltpu.make_async_copy(
                    source.at[:, columns(head)], send.at[dest, pl.ds(half * BLOCK, BLOCK)], sem
                ).start()

        return carry

    lax.fori_loop(0, CHIPS, one_slot, 0)

    def one_spare(index, carry):
        head = jnp.maximum(plan[ROW_SPARE + chip, 2 * index + core] - 1, 0)
        into = pl.ds(pl.multiple_of(2 * BLOCK + index * PIECE, PIECE), PIECE)

        def one_piece(piece, carry):
            rows = pl.ds(pl.multiple_of(piece * PIECE, PIECE), PIECE)

            @pl.when(core == 1)
            def _():
                for half, source in enumerate((keys, values)):
                    pltpu.make_async_copy(
                        source.at[rows, columns(head)], send.at[2 * piece + half, into], sem
                    ).start()

            @pl.when(core == 0)
            def _():
                for half, source in enumerate((other_keys, other_values)):
                    pltpu.make_async_copy(
                        source.at[rows, columns(head)], send.at[2 * piece + half, into], sem
                    ).start()

            return carry

        return lax.fori_loop(0, CHIPS // 2, one_piece, carry)

    lax.fori_loop(0, SPARE, one_spare, 0)
    pltpu.make_async_copy(send, send, sem).wait()


ANY = pl.BlockSpec(memory_space=pl.ANY)
SMEM = pl.BlockSpec(memory_space=pltpu.SMEM)


def tiles(count):
    return jax.ShapeDtypeStruct((count, 2 * BLOCK, HEAD), jnp.bfloat16)


def pack(plan, me, keys, values, other_keys, other_values):
    return pl.pallas_call(
        pack_kernel,
        in_specs=[SMEM, SMEM, ANY, ANY, ANY, ANY],
        out_specs=ANY,
        out_shape=jax.ShapeDtypeStruct((CHIPS, SLOT_ROWS, HEAD), jnp.bfloat16),
        scratch_shapes=[pltpu.SemaphoreType.DMA],
        name="pack",
    )(plan, me, keys, values, other_keys, other_values)


def forward_kernel(plan, me_ref, arrived, pieces, *rest):
    outs, sems = rest[:-1], rest[-1]
    me = me_ref[0]
    core = me % 2
    for kind in range(KINDS):
        out = outs[0].at[kind] if kind < PARTNER else outs[kind - PARTNER + 1].at[0]
        pltpu.make_async_copy(
            arrived.at[plan[ROW_FORWARD + kind, me], pl.ds(0, 2 * BLOCK)], out, sems.at[kind]
        ).start()

    def one_dest(dest, carry):
        for index in range(SPARE):
            chip = plan[ROW_FROM + index, 2 * dest + core]
            rank = plan[ROW_FROM_RANK + index, 2 * dest + core]
            row = pl.multiple_of(2 * BLOCK + rank * PIECE, PIECE)
            pltpu.make_async_copy(
                arrived.at[chip, pl.ds(row, PIECE)],
                pieces.at[dest, pl.ds(index * PIECE, PIECE)],
                sems.at[KINDS],
            ).start()
        return carry

    lax.fori_loop(0, CHIPS, one_dest, 0)
    pltpu.make_async_copy(pieces, pieces, sems.at[KINDS]).wait()
    for kind in range(KINDS):
        out = outs[0].at[kind] if kind < PARTNER else outs[kind - PARTNER + 1].at[0]
        pltpu.make_async_copy(arrived.at[0, pl.ds(0, 2 * BLOCK)], out, sems.at[kind]).wait()


def forward(plan, me, arrived):
    return pl.pallas_call(
        forward_kernel,
        in_specs=[SMEM, SMEM, ANY],
        out_specs=[ANY] * (KINDS - PARTNER + 2),
        out_shape=[jax.ShapeDtypeStruct((CHIPS, SPARE * PIECE, HEAD), jnp.bfloat16)]
        + [tiles(PARTNER)]
        + [tiles(1)] * (KINDS - PARTNER),
        scratch_shapes=[pltpu.SemaphoreType.DMA((KINDS + 1,))],
        name="forward",
    )(plan, me, arrived)


def scores_of(query, key):
    return lax.dot_general(
        query, key, (((1,), (1,)), ((), ())), preferred_element_type=jnp.float32
    )


def attend_kernel(
    plan, me_ref, query, own_key, own_value, other_keys, other_values, arrived, *rest
):
    count = KINDS - PARTNER + 1
    forwarded, pieces = rest[:count], rest[count]
    out = rest[count + 1]
    where, filled, key_buf, value_buf, sems = rest[count + 2 :]
    me = me_ref[0]
    step = pl.program_id(0)

    def note(head_plus, code):
        @pl.when(head_plus > 0)
        def _():
            at = filled[head_plus - 1]
            where[(head_plus - 1) * 3 + jnp.minimum(at, 2)] = code
            filled[head_plus - 1] = at + 1

    def fetch(head, slot):
        for j in range(3):
            code = where[head * 3 + j]
            into_key = key_buf.at[slot, j]
            into_value = value_buf.at[slot, j, :, pl.ds(0, HEAD)]

            def start(source_key, source_value):
                pltpu.make_async_copy(source_key, into_key, sems.at[slot, j, 0]).start()
                pltpu.make_async_copy(source_value, into_value, sems.at[slot, j, 1]).start()

            @pl.when(code < CHIPS)
            def _():
                start(arrived.at[code, pl.ds(0, BLOCK)], arrived.at[code, pl.ds(BLOCK, BLOCK)])

            @pl.when((code >= 64) & (code < 64 + PARTNER))
            def _():
                ref = forwarded[0].at[code - 64]
                start(ref.at[pl.ds(0, BLOCK)], ref.at[pl.ds(BLOCK, BLOCK)])

            for kind in range(PARTNER, KINDS):

                @pl.when(code == 64 + kind)
                def _():
                    ref = forwarded[kind - PARTNER + 1]
                    start(ref.at[0, pl.ds(0, BLOCK)], ref.at[0, pl.ds(BLOCK, BLOCK)])

            @pl.when((code >= 96) & (code < 128))
            def _():
                from_row = pl.ds(pl.multiple_of((code - 96) * PIECE, PIECE), PIECE)

                def one_piece(piece, carry):
                    rows = pl.ds(pl.multiple_of(piece * PIECE, PIECE), PIECE)
                    pltpu.make_async_copy(
                        pieces.at[2 * piece, from_row], into_key.at[rows], sems.at[slot, j, 0]
                    ).start()
                    pltpu.make_async_copy(
                        pieces.at[2 * piece + 1, from_row],
                        into_value.at[rows],
                        sems.at[slot, j, 1],
                    ).start()
                    return carry

                lax.fori_loop(0, BLOCK // PIECE, one_piece, 0)

            @pl.when(code == 128)
            def _():
                start(other_keys.at[:, columns(head)], other_values.at[:, columns(head)])

    @pl.when(step == 0)
    def _():
        for h in range(HEADS):
            filled[h] = 0
            for j in range(3):
                where[h * 3 + j] = 0
        value_buf[...] = jnp.ones(value_buf.shape, value_buf.dtype)

        def direct(chip, carry):
            note(plan[ROW_DIRECT + chip, me], chip)
            return carry

        lax.fori_loop(0, CHIPS, direct, 0)

        def moved(kind, carry):
            note(plan[ROW_FORWARD_HEAD + kind, me], 64 + kind)
            return carry

        lax.fori_loop(0, KINDS, moved, 0)

        def shared(index, carry):
            note(plan[ROW_FROM_HEAD + index, me], 96 + index)
            return carry

        lax.fori_loop(0, SPARE, shared, 0)
        note(plan[ROW_PARTNER, me], 128)
        fetch(0, 0)

    slot = step % 2

    @pl.when(step + 1 < HEADS)
    def _():
        fetch(step + 1, 1 - slot)

    for j in range(3):
        pltpu.make_async_copy(
            arrived.at[0, pl.ds(0, BLOCK)], key_buf.at[slot, j], sems.at[slot, j, 0]
        ).wait()
        pltpu.make_async_copy(
            arrived.at[0, pl.ds(BLOCK, BLOCK)],
            value_buf.at[slot, j, :, pl.ds(0, HEAD)],
            sems.at[slot, j, 1],
        ).wait()

    rows = 256
    for part in range(BLOCK // rows):
        length = (part + 1) * rows
        q = query[part * rows : length, :]
        own = scores_of(q, own_key[0:length, :])
        row_iota = lax.broadcasted_iota(jnp.int32, (rows, length), 0) + part * rows
        col_iota = lax.broadcasted_iota(jnp.int32, (rows, length), 1)
        own = jnp.where(col_iota <= row_iota, own, -jnp.inf)
        others = [scores_of(q, key_buf[slot, j]) for j in range(3)]
        highest = jnp.max(own, axis=1, keepdims=True)
        for other in others:
            highest = jnp.maximum(highest, jnp.max(other, axis=1, keepdims=True))
        weight = jnp.exp2((own - highest) * SCALE).astype(jnp.bfloat16)
        ones = jnp.ones((length, HEAD), jnp.bfloat16)
        total = jnp.dot(
            weight,
            jnp.concatenate([own_value[0:length, :], ones], axis=1),
            preferred_element_type=jnp.float32,
        )
        for j, other in enumerate(others):
            weight = jnp.exp2((other - highest) * SCALE).astype(jnp.bfloat16)
            total = total + jnp.dot(
                weight, value_buf[slot, j], preferred_element_type=jnp.float32
            )
        out[part * rows : length, :] = (total[:, :HEAD] / total[:, HEAD:]).astype(jnp.bfloat16)


def attend(plan, me, queries, keys, values, other_keys, other_values, arrived, forwarded, pieces):
    block = pl.BlockSpec((BLOCK, HEAD), lambda h: (0, h))
    return pl.pallas_call(
        attend_kernel,
        grid=(HEADS,),
        in_specs=[SMEM, SMEM, block, block, block] + [ANY] * (4 + len(forwarded)),
        out_specs=block,
        out_shape=jax.ShapeDtypeStruct((BLOCK, HEADS * HEAD), jnp.bfloat16),
        scratch_shapes=[
            pltpu.SMEM((3 * HEADS,), jnp.int32),
            pltpu.SMEM((HEADS,), jnp.int32),
            pltpu.VMEM((2, 3, BLOCK, HEAD), jnp.bfloat16),
            pltpu.VMEM((2, 3, BLOCK, 2 * HEAD), jnp.bfloat16),
            pltpu.SemaphoreType.DMA((2, 3, 2)),
        ],
        compiler_params=pltpu.CompilerParams(vmem_limit_bytes=48 * 1024 * 1024),
        name="attend",
    )(plan, me, queries, keys, values, other_keys, other_values, arrived, *forwarded, pieces)


LANES = [[2 * chip + core for chip in range(CHIPS)] for core in range(2)]
SWAP = [(device, device ^ 1) for device in range(DEVICES)]


def exchange(array):
    return lax.all_to_all(array, "ctx", 0, 0, axis_index_groups=LANES, tiled=True)


def full_attention(queries, keys, values, chosen_all, me):
    heads = jnp.arange(3 * HEADS, dtype=jnp.int32) // 3
    mine = lax.dynamic_index_in_dim(chosen_all, me, 0, keepdims=False)
    wants = chosen_all == me
    which = jnp.max(jnp.where(wants, heads[None, :], 0), axis=1)
    key_heads = keys.reshape(BLOCK, HEADS, HEAD).transpose(1, 0, 2)
    value_heads = values.reshape(BLOCK, HEADS, HEAD).transpose(1, 0, 2)
    got_key = lax.all_to_all(jnp.take(key_heads, which, axis=0), "ctx", 0, 0, tiled=True)
    got_value = lax.all_to_all(jnp.take(value_heads, which, axis=0), "ctx", 0, 0, tiled=True)
    q_heads = queries.reshape(BLOCK, HEADS, HEAD).transpose(1, 0, 2)
    allowed = jnp.arange(4 * BLOCK)[None, :] >= BLOCK
    allowed = allowed | (jnp.arange(4 * BLOCK)[None, :] <= jnp.arange(BLOCK)[:, None])

    def one_head(head):
        picks = lax.dynamic_slice(mine, (3 * head,), (3,))
        k = jnp.concatenate([key_heads[head], got_key[picks].reshape(3 * BLOCK, HEAD)], axis=0)
        v = jnp.concatenate([value_heads[head], got_value[picks].reshape(3 * BLOCK, HEAD)], axis=0)
        s = jnp.where(allowed, scores_of(q_heads[head], k), -jnp.inf)
        weight = jnp.exp2((s - jnp.max(s, axis=1, keepdims=True)) * SCALE)
        total = jnp.sum(weight, axis=1, keepdims=True)
        o = jnp.dot(weight.astype(jnp.bfloat16), v, preferred_element_type=jnp.float32)
        return (o / total).astype(jnp.bfloat16)

    out = lax.map(one_head, jnp.arange(HEADS))
    return out.transpose(1, 0, 2).reshape(BLOCK, HEADS * HEAD)


def body(queries, keys, values, chosen):
    me = lax.axis_index("ctx").astype(jnp.int32)
    me_ref = me.reshape(1)
    other_keys = lax.ppermute(keys, "ctx", SWAP)
    other_values = lax.ppermute(values, "ctx", SWAP)
    chosen_all = lax.all_gather(chosen.reshape(1, 3 * HEADS), "ctx", axis=0, tiled=True)
    plan = make_plan(chosen_all.T)
    send = pack(plan, me_ref, keys, values, other_keys, other_values)
    arrived = exchange(send)
    pieces, *outgoing = forward(plan, me_ref, arrived)
    pieces = exchange(pieces)
    forwarded = [
        lax.ppermute(array, "ctx", shift_pairs(SHIFTS[0] if n == 0 else SHIFTS[PARTNER + n - 1]))
        for n, array in enumerate(outgoing)
    ]
    out = attend(
        plan, me_ref, queries, keys, values, other_keys, other_values, arrived, forwarded, pieces
    )
    return lax.cond(
        plan[ROW_LEFT, 0] > 0,
        lambda: full_attention(queries, keys, values, chosen_all, me),
        lambda: out,
    )


def solution(mesh):
    placed = (P("ctx", None), P("ctx", None), P("ctx", None), P("ctx", None, None))
    return jax.shard_map(
        body, mesh=mesh, in_specs=placed, out_specs=P("ctx", None), check_vma=False
    )
```

```python
import math

import jax
import jax.numpy as jnp
from jax import lax
from jax.experimental import pallas as pl
from jax.experimental.pallas import tpu as pltpu
from jax.sharding import PartitionSpec as P

HEAD = 128
HEADS = 16
BLOCK = 512
DEVICES = 128
CHIPS = 64
SCALE = math.log2(math.e) / math.sqrt(HEAD)

ONE = [(1, 0, 0), (3, 0, 0), (0, 1, 0), (0, 3, 0), (0, 0, 1), (0, 0, 3)]
PARTNER = 6
SHIFTS = [(0, 0, 0, 1)] * PARTNER
SHIFTS += [(*s, c) for s in ONE for c in (0, 1)]
KINDS = len(SHIFTS)
SPARE = 4
PIECE = 16
SLOT_ROWS = 2 * BLOCK + SPARE * PIECE

ROW_DIRECT = CHIPS
ROW_SPARE = ROW_DIRECT + CHIPS
ROW_FORWARD = ROW_SPARE + CHIPS
ROW_FORWARD_HEAD = ROW_FORWARD + 32
ROW_FROM = ROW_FORWARD_HEAD + 32
ROW_FROM_RANK = ROW_FROM + 8
ROW_FROM_HEAD = ROW_FROM_RANK + 8
ROW_PARTNER = ROW_FROM_HEAD + 8
ROW_LEFT = ROW_PARTNER + 1
ROWS = ROW_PARTNER + 8


def through(device, shift):
    z, x, y, c = device // 32, device // 8 % 4, device // 2 % 4, device % 2
    dz, dx, dy, dc = shift
    return (((z + dz) % 4 * 4 + (x + dx) % 4) * 4 + (y + dy) % 4) * 2 + (c ^ dc)


def shift_pairs(shift):
    return [(through(b, shift), b) for b in range(DEVICES)]


def roll_lanes(array, amount):
    amount = amount % DEVICES
    return pltpu.roll(array, amount, 1) if amount else array


def permuted(array, shift, lane, inverse=False):
    dz, dx, dy, dc = shift
    if inverse:
        dz, dx, dy = -dz % 4, -dx % 4, -dy % 4
    if dz:
        array = roll_lanes(array, -32 * dz)
    if dx:
        inside = (lane // 8) % 4 + dx < 4
        array = jnp.where(inside, roll_lanes(array, -8 * dx), roll_lanes(array, 32 - 8 * dx))
    if dy:
        inside = (lane // 2) % 4 + dy < 4
        array = jnp.where(inside, roll_lanes(array, -2 * dy), roll_lanes(array, 8 - 2 * dy))
    if dc:
        array = jnp.where(lane % 2 == 0, roll_lanes(array, -1), roll_lanes(array, 1))
    return array


def plan_kernel(chosen_ref, out_ref):
    chip = lax.broadcasted_iota(jnp.int32, (CHIPS, DEVICES), 0)
    lane = lax.broadcasted_iota(jnp.int32, (CHIPS, DEVICES), 1)
    even = jnp.zeros((CHIPS, DEVICES), jnp.int32)
    odd = jnp.zeros((CHIPS, DEVICES), jnp.int32)
    for entry in range(3 * HEADS):
        owner = chosen_ref[entry : entry + 1, :]
        even = even + jnp.where(owner == 2 * chip, entry // 3 + 1, 0)
        odd = odd + jnp.where(owner == 2 * chip + 1, entry // 3 + 1, 0)
    home = lane // 2 == chip
    partner = jnp.sum(jnp.where(home, even + odd, 0), axis=0, keepdims=True)
    even = jnp.where(home, 0, even)
    odd = jnp.where(home, 0, odd)
    waiting = jnp.where(even > 0, odd, 0)
    slot = jnp.where(even > 0, even - 1, jnp.where(odd > 0, odd + 15, 0))
    direct = jnp.where(even > 0, even, odd)
    free = jnp.where(home, 0, jnp.where(direct > 0, 0, 1))
    options = jnp.zeros((CHIPS, DEVICES), jnp.int32)
    for shift in sorted(set(SHIFTS)):
        options = options + permuted(free, shift, lane)
    score = options * 64 + (chip + 17 * lane) % 64
    big = 1 << 20
    out_ref[...] = jnp.zeros((ROWS, DEVICES), jnp.int32)
    for kind, shift in enumerate(SHIFTS):
        able = (waiting > 0) & (permuted(free, shift, lane) > 0)
        rated = jnp.where(able, score, big)
        best = jnp.min(rated, axis=0, keepdims=True)
        picked = able & (rated == best)
        head = jnp.sum(jnp.where(picked, waiting, 0), axis=0, keepdims=True)
        back = permuted(jnp.where(picked, waiting + 16, 0), shift, lane, inverse=True)
        waiting = jnp.where(picked, 0, waiting)
        slot = jnp.where(back > 0, back - 1, slot)
        free = jnp.where(back > 0, 0, free)
        forward = jnp.sum(jnp.where(back > 0, chip, 0), axis=0, keepdims=True)
        out_ref[ROW_FORWARD + kind : ROW_FORWARD + kind + 1, :] = forward
        out_ref[ROW_FORWARD_HEAD + kind : ROW_FORWARD_HEAD + kind + 1, :] = head
    before = lax.broadcasted_iota(jnp.int32, (DEVICES, DEVICES), 0)
    after = lax.broadcasted_iota(jnp.int32, (DEVICES, DEVICES), 1)
    earlier = jnp.where((before < after) & (before % 2 == after % 2), 1.0, 0.0)
    rank = jnp.dot(
        jnp.where(waiting > 0, 1.0, 0.0), earlier, preferred_element_type=jnp.float32
    ).astype(jnp.int32)
    spare = jnp.zeros((CHIPS, DEVICES), jnp.int32)
    for index in range(SPARE):
        for core in range(2):
            chosen = (rank == index) & (lane % 2 == core)
            head = jnp.sum(jnp.where(chosen, waiting, 0), axis=1, keepdims=True)
            spare = jnp.where(lane == 2 * index + core, head, spare)
    out_ref[ROW_SPARE : ROW_SPARE + CHIPS, :] = spare
    excess = jnp.where((waiting > 0) & (rank >= SPARE), 1, 0)
    for index in range(SPARE):
        best = jnp.min(jnp.where(waiting > 0, chip, big), axis=0, keepdims=True)
        picked = (waiting > 0) & (chip == best)
        out_ref[ROW_FROM + index : ROW_FROM + index + 1, :] = jnp.where(best < big, best, 0)
        out_ref[ROW_FROM_RANK + index : ROW_FROM_RANK + index + 1, :] = jnp.minimum(
            jnp.sum(jnp.where(picked, rank, 0), axis=0, keepdims=True), SPARE - 1
        )
        out_ref[ROW_FROM_HEAD + index : ROW_FROM_HEAD + index + 1, :] = jnp.sum(
            jnp.where(picked, waiting, 0), axis=0, keepdims=True
        )
        waiting = jnp.where(picked, 0, waiting)
    excess = excess + waiting
    out_ref[ROW_PARTNER : ROW_PARTNER + 1, :] = partner
    left = jnp.max(jnp.max(excess, axis=0, keepdims=True), axis=1, keepdims=True)
    out_ref[ROW_LEFT : ROW_LEFT + 1, :] = jnp.broadcast_to(left, (1, DEVICES))
    out_ref[0:CHIPS, :] = slot
    out_ref[ROW_DIRECT : ROW_DIRECT + CHIPS, :] = direct


def make_plan(chosen_all):
    return pl.pallas_call(
        plan_kernel,
        out_shape=jax.ShapeDtypeStruct((ROWS, DEVICES), jnp.int32),
        name="plan",
    )(chosen_all)


def columns(head):
    return pl.ds(pl.multiple_of(head * HEAD, HEAD), HEAD)


def pack_kernel(plan, me_ref, keys, values, other_keys, other_values, send, sem):
    me = me_ref[0]
    chip, core = me // 2, me % 2

    def one_slot(dest, carry):
        code = plan[chip, 2 * dest + core]
        head = code % 16

        @pl.when(code // 16 == core)
        def _():
            for half, source in enumerate((keys, values)):
                pltpu.make_async_copy(
                    source.at[:, columns(head)], send.at[dest, pl.ds(half * BLOCK, BLOCK)], sem
                ).start()

        @pl.when(code // 16 != core)
        def _():
            for half, source in enumerate((other_keys, other_values)):
                pltpu.make_async_copy(
                    source.at[:, columns(head)], send.at[dest, pl.ds(half * BLOCK, BLOCK)], sem
                ).start()

        return carry

    lax.fori_loop(0, CHIPS, one_slot, 0)

    def one_spare(index, carry):
        head = jnp.maximum(plan[ROW_SPARE + chip, 2 * index + core] - 1, 0)
        into = pl.ds(pl.multiple_of(2 * BLOCK + index * PIECE, PIECE), PIECE)

        def one_piece(piece, carry):
            rows = pl.ds(pl.multiple_of(piece * PIECE, PIECE), PIECE)

            @pl.when(core == 1)
            def _():
                for half, source in enumerate((keys, values)):
                    pltpu.make_async_copy(
                        source.at[rows, columns(head)], send.at[2 * piece + half, into], sem
                    ).start()

            @pl.when(core == 0)
            def _():
                for half, source in enumerate((other_keys, other_values)):
                    pltpu.make_async_copy(
                        source.at[rows, columns(head)], send.at[2 * piece + half, into], sem
                    ).start()

            return carry

        return lax.fori_loop(0, CHIPS // 2, one_piece, carry)

    lax.fori_loop(0, SPARE, one_spare, 0)
    pltpu.make_async_copy(send, send, sem).wait()


ANY = pl.BlockSpec(memory_space=pl.ANY)
SMEM = pl.BlockSpec(memory_space=pltpu.SMEM)
VMEM = pl.BlockSpec(memory_space=pltpu.VMEM)
BIG = pltpu.CompilerParams(vmem_limit_bytes=48 * 1024 * 1024)


def tiles(count):
    return jax.ShapeDtypeStruct((count, 2 * BLOCK, HEAD), jnp.bfloat16)


def pack(plan, me, keys, values, other_keys, other_values):
    return pl.pallas_call(
        pack_kernel,
        in_specs=[SMEM, SMEM, VMEM, VMEM, VMEM, VMEM],
        out_specs=ANY,
        out_shape=jax.ShapeDtypeStruct((CHIPS, SLOT_ROWS, HEAD), jnp.bfloat16),
        scratch_shapes=[pltpu.SemaphoreType.DMA],
        compiler_params=BIG,
        name="pack",
    )(plan, me, keys, values, other_keys, other_values)


def forward_kernel(plan, me_ref, arrived, pieces, *rest):
    outs, sems = rest[:-1], rest[-1]
    me = me_ref[0]
    core = me % 2
    for kind in range(KINDS):
        out = outs[0].at[kind] if kind < PARTNER else outs[kind - PARTNER + 1].at[0]
        pltpu.make_async_copy(
            arrived.at[plan[ROW_FORWARD + kind, me], pl.ds(0, 2 * BLOCK)], out, sems.at[kind]
        ).start()

    def one_dest(dest, carry):
        for index in range(SPARE):
            chip = plan[ROW_FROM + index, 2 * dest + core]
            rank = plan[ROW_FROM_RANK + index, 2 * dest + core]
            row = pl.multiple_of(2 * BLOCK + rank * PIECE, PIECE)
            pltpu.make_async_copy(
                arrived.at[chip, pl.ds(row, PIECE)],
                pieces.at[dest, pl.ds(index * PIECE, PIECE)],
                sems.at[KINDS],
            ).start()
        return carry

    lax.fori_loop(0, CHIPS, one_dest, 0)
    pltpu.make_async_copy(pieces, pieces, sems.at[KINDS]).wait()
    for kind in range(KINDS):
        out = outs[0].at[kind] if kind < PARTNER else outs[kind - PARTNER + 1].at[0]
        pltpu.make_async_copy(arrived.at[0, pl.ds(0, 2 * BLOCK)], out, sems.at[kind]).wait()


def forward(plan, me, arrived):
    return pl.pallas_call(
        forward_kernel,
        in_specs=[SMEM, SMEM, ANY],
        out_specs=[VMEM] * (KINDS - PARTNER + 2),
        out_shape=[jax.ShapeDtypeStruct((CHIPS, SPARE * PIECE, HEAD), jnp.bfloat16)]
        + [tiles(PARTNER)]
        + [tiles(1)] * (KINDS - PARTNER),
        scratch_shapes=[pltpu.SemaphoreType.DMA((KINDS + 1,))],
        compiler_params=BIG,
        name="forward",
    )(plan, me, arrived)


def scores_of(query, key):
    return lax.dot_general(
        query, key, (((1,), (1,)), ((), ())), preferred_element_type=jnp.float32
    )


def attend_kernel(
    plan, me_ref, query, own_key, own_value, other_keys, other_values, arrived, *rest
):
    count = KINDS - PARTNER + 1
    forwarded, pieces = rest[:count], rest[count]
    out = rest[count + 1]
    where, filled, key_buf, value_buf, sems = rest[count + 2 :]
    me = me_ref[0]
    step = pl.program_id(0)

    def note(head_plus, code):
        @pl.when(head_plus > 0)
        def _():
            at = filled[head_plus - 1]
            where[(head_plus - 1) * 3 + jnp.minimum(at, 2)] = code
            filled[head_plus - 1] = at + 1

    def fetch(head, slot):
        for j in range(3):
            code = where[head * 3 + j]
            into_key = key_buf.at[slot, j]
            into_value = value_buf.at[slot, j, :, pl.ds(0, HEAD)]

            def start(source_key, source_value):
                pltpu.make_async_copy(source_key, into_key, sems.at[slot, j, 0]).start()
                pltpu.make_async_copy(source_value, into_value, sems.at[slot, j, 1]).start()

            @pl.when(code < CHIPS)
            def _():
                start(arrived.at[code, pl.ds(0, BLOCK)], arrived.at[code, pl.ds(BLOCK, BLOCK)])

            @pl.when((code >= 64) & (code < 64 + PARTNER))
            def _():
                ref = forwarded[0].at[code - 64]
                start(ref.at[pl.ds(0, BLOCK)], ref.at[pl.ds(BLOCK, BLOCK)])

            for kind in range(PARTNER, KINDS):

                @pl.when(code == 64 + kind)
                def _():
                    ref = forwarded[kind - PARTNER + 1]
                    start(ref.at[0, pl.ds(0, BLOCK)], ref.at[0, pl.ds(BLOCK, BLOCK)])

            @pl.when((code >= 96) & (code < 128))
            def _():
                from_row = pl.ds(pl.multiple_of((code - 96) * PIECE, PIECE), PIECE)

                def one_piece(piece, carry):
                    rows = pl.ds(pl.multiple_of(piece * PIECE, PIECE), PIECE)
                    pltpu.make_async_copy(
                        pieces.at[2 * piece, from_row], into_key.at[rows], sems.at[slot, j, 0]
                    ).start()
                    pltpu.make_async_copy(
                        pieces.at[2 * piece + 1, from_row],
                        into_value.at[rows],
                        sems.at[slot, j, 1],
                    ).start()
                    return carry

                lax.fori_loop(0, BLOCK // PIECE, one_piece, 0)

            @pl.when(code == 128)
            def _():
                start(other_keys.at[:, columns(head)], other_values.at[:, columns(head)])

    @pl.when(step == 0)
    def _():
        for h in range(HEADS):
            filled[h] = 0
            for j in range(3):
                where[h * 3 + j] = 0
        value_buf[...] = jnp.ones(value_buf.shape, value_buf.dtype)

        def direct(chip, carry):
            note(plan[ROW_DIRECT + chip, me], chip)
            return carry

        lax.fori_loop(0, CHIPS, direct, 0)

        def moved(kind, carry):
            note(plan[ROW_FORWARD_HEAD + kind, me], 64 + kind)
            return carry

        lax.fori_loop(0, KINDS, moved, 0)

        def shared(index, carry):
            note(plan[ROW_FROM_HEAD + index, me], 96 + index)
            return carry

        lax.fori_loop(0, SPARE, shared, 0)
        note(plan[ROW_PARTNER, me], 128)
        fetch(0, 0)

    slot = step % 2

    @pl.when(step + 1 < HEADS)
    def _():
        fetch(step + 1, 1 - slot)

    for j in range(3):
        pltpu.make_async_copy(
            arrived.at[0, pl.ds(0, BLOCK)], key_buf.at[slot, j], sems.at[slot, j, 0]
        ).wait()
        pltpu.make_async_copy(
            arrived.at[0, pl.ds(BLOCK, BLOCK)],
            value_buf.at[slot, j, :, pl.ds(0, HEAD)],
            sems.at[slot, j, 1],
        ).wait()

    rows = 256
    for part in range(BLOCK // rows):
        length = (part + 1) * rows
        q = query[part * rows : length, :]
        own = scores_of(q, own_key[0:length, :])
        row_iota = lax.broadcasted_iota(jnp.int32, (rows, length), 0) + part * rows
        col_iota = lax.broadcasted_iota(jnp.int32, (rows, length), 1)
        own = jnp.where(col_iota <= row_iota, own, -jnp.inf)
        others = [scores_of(q, key_buf[slot, j]) for j in range(3)]
        highest = jnp.max(own, axis=1, keepdims=True)
        for other in others:
            highest = jnp.maximum(highest, jnp.max(other, axis=1, keepdims=True))
        weight = jnp.exp2((own - highest) * SCALE).astype(jnp.bfloat16)
        ones = jnp.ones((length, HEAD), jnp.bfloat16)
        total = jnp.dot(
            weight,
            jnp.concatenate([own_value[0:length, :], ones], axis=1),
            preferred_element_type=jnp.float32,
        )
        for j, other in enumerate(others):
            weight = jnp.exp2((other - highest) * SCALE).astype(jnp.bfloat16)
            total = total + jnp.dot(
                weight, value_buf[slot, j], preferred_element_type=jnp.float32
            )
        out[part * rows : length, :] = (total[:, :HEAD] / total[:, HEAD:]).astype(jnp.bfloat16)


def attend(plan, me, queries, keys, values, other_keys, other_values, arrived, forwarded, pieces):
    block = pl.BlockSpec((BLOCK, HEAD), lambda h: (0, h))
    return pl.pallas_call(
        attend_kernel,
        grid=(HEADS,),
        in_specs=[SMEM, SMEM, block, block, block] + [ANY] * (4 + len(forwarded)),
        out_specs=block,
        out_shape=jax.ShapeDtypeStruct((BLOCK, HEADS * HEAD), jnp.bfloat16),
        scratch_shapes=[
            pltpu.SMEM((3 * HEADS,), jnp.int32),
            pltpu.SMEM((HEADS,), jnp.int32),
            pltpu.VMEM((2, 3, BLOCK, HEAD), jnp.bfloat16),
            pltpu.VMEM((2, 3, BLOCK, 2 * HEAD), jnp.bfloat16),
            pltpu.SemaphoreType.DMA((2, 3, 2)),
        ],
        compiler_params=BIG,
        name="attend",
    )(plan, me, queries, keys, values, other_keys, other_values, arrived, *forwarded, pieces)


LANES = [[2 * chip + core for chip in range(CHIPS)] for core in range(2)]
SWAP = [(device, device ^ 1) for device in range(DEVICES)]


def exchange(array):
    return lax.all_to_all(array, "ctx", 0, 0, axis_index_groups=LANES, tiled=True)


def full_attention(queries, keys, values, chosen_all, me):
    heads = jnp.arange(3 * HEADS, dtype=jnp.int32) // 3
    mine = lax.dynamic_index_in_dim(chosen_all, me, 0, keepdims=False)
    wants = chosen_all == me
    which = jnp.max(jnp.where(wants, heads[None, :], 0), axis=1)
    key_heads = keys.reshape(BLOCK, HEADS, HEAD).transpose(1, 0, 2)
    value_heads = values.reshape(BLOCK, HEADS, HEAD).transpose(1, 0, 2)
    got_key = lax.all_to_all(jnp.take(key_heads, which, axis=0), "ctx", 0, 0, tiled=True)
    got_value = lax.all_to_all(jnp.take(value_heads, which, axis=0), "ctx", 0, 0, tiled=True)
    q_heads = queries.reshape(BLOCK, HEADS, HEAD).transpose(1, 0, 2)
    allowed = jnp.arange(4 * BLOCK)[None, :] >= BLOCK
    allowed = allowed | (jnp.arange(4 * BLOCK)[None, :] <= jnp.arange(BLOCK)[:, None])

    def one_head(head):
        picks = lax.dynamic_slice(mine, (3 * head,), (3,))
        k = jnp.concatenate([key_heads[head], got_key[picks].reshape(3 * BLOCK, HEAD)], axis=0)
        v = jnp.concatenate([value_heads[head], got_value[picks].reshape(3 * BLOCK, HEAD)], axis=0)
        s = jnp.where(allowed, scores_of(q_heads[head], k), -jnp.inf)
        weight = jnp.exp2((s - jnp.max(s, axis=1, keepdims=True)) * SCALE)
        total = jnp.sum(weight, axis=1, keepdims=True)
        o = jnp.dot(weight.astype(jnp.bfloat16), v, preferred_element_type=jnp.float32)
        return (o / total).astype(jnp.bfloat16)

    out = lax.map(one_head, jnp.arange(HEADS))
    return out.transpose(1, 0, 2).reshape(BLOCK, HEADS * HEAD)


def body(queries, keys, values, chosen):
    me = lax.axis_index("ctx").astype(jnp.int32)
    me_ref = me.reshape(1)
    other_keys = lax.ppermute(keys, "ctx", SWAP)
    other_values = lax.ppermute(values, "ctx", SWAP)
    spread = jnp.broadcast_to(chosen.reshape(1, 3 * HEADS), (DEVICES, 3 * HEADS))
    chosen_all = lax.all_to_all(spread, "ctx", 0, 0, tiled=True)
    plan = make_plan(chosen_all.T)
    send = pack(plan, me_ref, keys, values, other_keys, other_values)
    arrived = exchange(send)
    pieces, *outgoing = forward(plan, me_ref, arrived)
    pieces = exchange(pieces)
    forwarded = [
        lax.ppermute(array, "ctx", shift_pairs(SHIFTS[0] if n == 0 else SHIFTS[PARTNER + n - 1]))
        for n, array in enumerate(outgoing)
    ]
    out = attend(
        plan, me_ref, queries, keys, values, other_keys, other_values, arrived, forwarded, pieces
    )
    return lax.cond(
        plan[ROW_LEFT, 0] > 0,
        lambda: full_attention(queries, keys, values, chosen_all, me),
        lambda: out,
    )


def solution(mesh):
    placed = (P("ctx", None), P("ctx", None), P("ctx", None), P("ctx", None, None))
    return jax.shard_map(
        body, mesh=mesh, in_specs=placed, out_specs=P("ctx", None), check_vma=False
    )
```

```python
import math

import jax
import jax.numpy as jnp
from jax import lax
from jax.experimental import pallas as pl
from jax.experimental.pallas import tpu as pltpu
from jax.sharding import PartitionSpec as P

HEAD = 128
HEADS = 16
BLOCK = 512
DEVICES = 128
CHIPS = 64
SCALE = math.log2(math.e) / math.sqrt(HEAD)

ONE = [(1, 0, 0), (3, 0, 0), (0, 1, 0), (0, 3, 0), (0, 0, 1), (0, 0, 3)]
PARTNER = 6
SHIFTS = [(0, 0, 0, 1)] * PARTNER
SHIFTS += [(*s, c) for s in ONE for c in (0, 1)]
KINDS = len(SHIFTS)
SPARE = 4
PIECE = 16
PARTS = 4
SLOT_ROWS = 2 * BLOCK + SPARE * PIECE

ROW_DIRECT = CHIPS
ROW_SPARE = ROW_DIRECT + CHIPS
ROW_FORWARD = ROW_SPARE + CHIPS
ROW_FORWARD_HEAD = ROW_FORWARD + KINDS
ROW_FROM_HEAD = ROW_FORWARD_HEAD + KINDS
ROW_FROM = ROW_FROM_HEAD + SPARE
ROW_FROM_RANK = ROW_FROM + SPARE
ROW_PARTNER = ROW_FROM_RANK + SPARE
ROW_LEFT = ROW_PARTNER + 1
ROWS = -(-(ROW_LEFT + 1) // 8) * 8


def through(device, shift):
    z, x, y, c = device // 32, device // 8 % 4, device // 2 % 4, device % 2
    dz, dx, dy, dc = shift
    return (((z + dz) % 4 * 4 + (x + dx) % 4) * 4 + (y + dy) % 4) * 2 + (c ^ dc)


def shift_pairs(shift):
    return [(through(b, shift), b) for b in range(DEVICES)]


def roll_lanes(array, amount):
    amount = amount % DEVICES
    return pltpu.roll(array, amount, 1) if amount else array


def permuted(array, shift, lane, inverse=False):
    dz, dx, dy, dc = shift
    if inverse:
        dz, dx, dy = -dz % 4, -dx % 4, -dy % 4
    if dz:
        array = roll_lanes(array, -32 * dz)
    if dx:
        inside = (lane // 8) % 4 + dx < 4
        array = jnp.where(inside, roll_lanes(array, -8 * dx), roll_lanes(array, 32 - 8 * dx))
    if dy:
        inside = (lane // 2) % 4 + dy < 4
        array = jnp.where(inside, roll_lanes(array, -2 * dy), roll_lanes(array, 8 - 2 * dy))
    if dc:
        array = jnp.where(lane % 2 == 0, roll_lanes(array, -1), roll_lanes(array, 1))
    return array


def plan_kernel(chosen_ref, out_ref):
    chip = lax.broadcasted_iota(jnp.int32, (CHIPS, DEVICES), 0)
    lane = lax.broadcasted_iota(jnp.int32, (CHIPS, DEVICES), 1)
    even = jnp.zeros((CHIPS, DEVICES), jnp.int32)
    odd = jnp.zeros((CHIPS, DEVICES), jnp.int32)
    for entry in range(3 * HEADS):
        owner = chosen_ref[entry : entry + 1, :]
        even = even + jnp.where(owner == 2 * chip, entry // 3 + 1, 0)
        odd = odd + jnp.where(owner == 2 * chip + 1, entry // 3 + 1, 0)
    home = lane // 2 == chip
    partner = jnp.sum(jnp.where(home, even + odd, 0), axis=0, keepdims=True)
    even = jnp.where(home, 0, even)
    odd = jnp.where(home, 0, odd)
    waiting = jnp.where(even > 0, odd, 0)
    slot = jnp.where(even > 0, even - 1, jnp.where(odd > 0, odd + 15, 0))
    direct = jnp.where(even > 0, even, odd)
    free = jnp.where(home, 0, jnp.where(direct > 0, 0, 1))
    options = jnp.zeros((CHIPS, DEVICES), jnp.int32)
    for shift in sorted(set(SHIFTS)):
        options = options + permuted(free, shift, lane)
    score = options * 64 + (chip + 17 * lane) % 64
    big = 1 << 20
    out_ref[...] = jnp.zeros((ROWS, DEVICES), jnp.int32)
    for kind, shift in enumerate(SHIFTS):
        able = (waiting > 0) & (permuted(free, shift, lane) > 0)
        rated = jnp.where(able, score, big)
        best = jnp.min(rated, axis=0, keepdims=True)
        picked = able & (rated == best)
        head = jnp.sum(jnp.where(picked, waiting, 0), axis=0, keepdims=True)
        back = permuted(jnp.where(picked, waiting + 16, 0), shift, lane, inverse=True)
        waiting = jnp.where(picked, 0, waiting)
        slot = jnp.where(back > 0, back - 1, slot)
        free = jnp.where(back > 0, 0, free)
        forward = jnp.sum(jnp.where(back > 0, chip, 0), axis=0, keepdims=True)
        out_ref[ROW_FORWARD + kind : ROW_FORWARD + kind + 1, :] = forward
        out_ref[ROW_FORWARD_HEAD + kind : ROW_FORWARD_HEAD + kind + 1, :] = head
    before = lax.broadcasted_iota(jnp.int32, (DEVICES, DEVICES), 0)
    after = lax.broadcasted_iota(jnp.int32, (DEVICES, DEVICES), 1)
    earlier = jnp.where((before < after) & (before % 2 == after % 2), 1.0, 0.0)
    rank = jnp.dot(
        jnp.where(waiting > 0, 1.0, 0.0), earlier, preferred_element_type=jnp.float32
    ).astype(jnp.int32)
    spare = jnp.zeros((CHIPS, DEVICES), jnp.int32)
    for index in range(SPARE):
        for core in range(2):
            chosen = (rank == index) & (lane % 2 == core)
            head = jnp.sum(jnp.where(chosen, waiting, 0), axis=1, keepdims=True)
            spare = jnp.where(lane == 2 * index + core, head, spare)
    out_ref[ROW_SPARE : ROW_SPARE + CHIPS, :] = spare
    excess = jnp.where((waiting > 0) & (rank >= SPARE), 1, 0)
    for index in range(SPARE):
        best = jnp.min(jnp.where(waiting > 0, chip, big), axis=0, keepdims=True)
        picked = (waiting > 0) & (chip == best)
        out_ref[ROW_FROM + index : ROW_FROM + index + 1, :] = jnp.where(best < big, best, 0)
        out_ref[ROW_FROM_RANK + index : ROW_FROM_RANK + index + 1, :] = jnp.minimum(
            jnp.sum(jnp.where(picked, rank, 0), axis=0, keepdims=True), SPARE - 1
        )
        out_ref[ROW_FROM_HEAD + index : ROW_FROM_HEAD + index + 1, :] = jnp.sum(
            jnp.where(picked, waiting, 0), axis=0, keepdims=True
        )
        waiting = jnp.where(picked, 0, waiting)
    excess = excess + waiting
    out_ref[ROW_PARTNER : ROW_PARTNER + 1, :] = partner
    left = jnp.max(jnp.max(excess, axis=0, keepdims=True), axis=1, keepdims=True)
    out_ref[ROW_LEFT : ROW_LEFT + 1, :] = jnp.broadcast_to(left, (1, DEVICES))
    out_ref[0:CHIPS, :] = slot
    out_ref[ROW_DIRECT : ROW_DIRECT + CHIPS, :] = direct


def make_plan(chosen_all):
    return pl.pallas_call(
        plan_kernel,
        out_shape=jax.ShapeDtypeStruct((ROWS, DEVICES), jnp.int32),
        name="plan",
    )(chosen_all)


def columns(head):
    return pl.ds(pl.multiple_of(head * HEAD, HEAD), HEAD)


def pack_kernel(plan, me_ref, keys, values, other_keys, other_values, send, sem):
    me = me_ref[0]
    chip, core = me // 2, me % 2

    def one_slot(dest, carry):
        code = plan[chip, 2 * dest + core]
        head = code % 16

        @pl.when(code // 16 == core)
        def _():
            for half, source in enumerate((keys, values)):
                pltpu.make_async_copy(
                    source.at[:, columns(head)], send.at[dest, pl.ds(half * BLOCK, BLOCK)], sem
                ).start()

        @pl.when(code // 16 != core)
        def _():
            for half, source in enumerate((other_keys, other_values)):
                pltpu.make_async_copy(
                    source.at[:, columns(head)], send.at[dest, pl.ds(half * BLOCK, BLOCK)], sem
                ).start()

        return carry

    lax.fori_loop(0, CHIPS, one_slot, 0)

    def one_spare(index, carry):
        head = jnp.maximum(plan[ROW_SPARE + chip, 2 * index + core] - 1, 0)
        into = pl.ds(pl.multiple_of(2 * BLOCK + index * PIECE, PIECE), PIECE)

        def one_piece(piece, carry):
            rows = pl.ds(pl.multiple_of(piece * PIECE, PIECE), PIECE)

            @pl.when(core == 1)
            def _():
                for half, source in enumerate((keys, values)):
                    pltpu.make_async_copy(
                        source.at[rows, columns(head)], send.at[2 * piece + half, into], sem
                    ).start()

            @pl.when(core == 0)
            def _():
                for half, source in enumerate((other_keys, other_values)):
                    pltpu.make_async_copy(
                        source.at[rows, columns(head)], send.at[2 * piece + half, into], sem
                    ).start()

            return carry

        return lax.fori_loop(0, CHIPS // 2, one_piece, carry)

    lax.fori_loop(0, SPARE, one_spare, 0)
    pltpu.make_async_copy(send, send, sem).wait()


ANY = pl.BlockSpec(memory_space=pl.ANY)
SMEM = pl.BlockSpec(memory_space=pltpu.SMEM)
VMEM = pl.BlockSpec(memory_space=pltpu.VMEM)
BIG = pltpu.CompilerParams(vmem_limit_bytes=60 * 1024 * 1024)


def tiles(count):
    return jax.ShapeDtypeStruct((count, 2 * BLOCK, HEAD), jnp.bfloat16)


def pack(plan, me, keys, values, other_keys, other_values):
    return pl.pallas_call(
        pack_kernel,
        in_specs=[SMEM, SMEM, VMEM, VMEM, VMEM, VMEM],
        out_specs=ANY,
        out_shape=jax.ShapeDtypeStruct((CHIPS, SLOT_ROWS, HEAD), jnp.bfloat16),
        scratch_shapes=[pltpu.SemaphoreType.DMA],
        compiler_params=BIG,
        name="pack",
    )(plan, me, keys, values, other_keys, other_values)


def forward_kernel(plan, me_ref, arrived, *rest):
    outs, (moving, gathered, sems, out_sems) = rest[:-4], rest[-4:]
    me = me_ref[0]
    core = me % 2
    loads, stores = [], []
    for kind in range(KINDS):
        out = outs[1].at[kind] if kind < PARTNER else outs[kind - PARTNER + 2].at[0]
        source = arrived.at[plan[ROW_FORWARD + kind, me], pl.ds(0, 2 * BLOCK)]
        loads.append(pltpu.make_async_copy(source, moving.at[kind], sems.at[kind]))
        stores.append(pltpu.make_async_copy(moving.at[kind], out, out_sems.at[kind]))
    for load in loads:
        load.start()

    def one_dest(dest, carry):
        for index in range(SPARE):
            chip = plan[ROW_FROM + index, 2 * dest + core]
            rank = plan[ROW_FROM_RANK + index, 2 * dest + core]
            row = pl.multiple_of(2 * BLOCK + rank * PIECE, PIECE)
            pltpu.make_async_copy(
                arrived.at[chip, pl.ds(row, PIECE)],
                gathered.at[dest, pl.ds(index * PIECE, PIECE)],
                sems.at[KINDS],
            ).start()
        return carry

    lax.fori_loop(0, CHIPS, one_dest, 0)
    for load, store in zip(loads, stores):
        load.wait()
        store.start()
    pltpu.make_async_copy(gathered, gathered, sems.at[KINDS]).wait()
    last = pltpu.make_async_copy(gathered, outs[0], out_sems.at[KINDS])
    last.start()
    for store in stores:
        store.wait()
    last.wait()


def forward(plan, me, arrived):
    return pl.pallas_call(
        forward_kernel,
        in_specs=[SMEM, SMEM, ANY],
        out_specs=[ANY] * (KINDS - PARTNER + 2),
        out_shape=[jax.ShapeDtypeStruct((CHIPS, SPARE * PIECE, HEAD), jnp.bfloat16)]
        + [tiles(PARTNER)]
        + [tiles(1)] * (KINDS - PARTNER),
        scratch_shapes=[
            pltpu.VMEM((KINDS, 2 * BLOCK, HEAD), jnp.bfloat16),
            pltpu.VMEM((CHIPS, SPARE * PIECE, HEAD), jnp.bfloat16),
            pltpu.SemaphoreType.DMA((KINDS + 1,)),
            pltpu.SemaphoreType.DMA((KINDS + 1,)),
        ],
        compiler_params=BIG,
        name="forward",
    )(plan, me, arrived)


def scores_of(query, key):
    return lax.dot_general(
        query, key, (((1,), (1,)), ((), ())), preferred_element_type=jnp.float32
    )


def attend_kernel(first, last, plan, me_ref, query, own_key, own_value, *rest):
    other_keys, other_values, arrived = rest[:3]
    out, state, where, filled, key_buf, value_buf, sems = rest[-7:]
    me = me_ref[0]
    step = pl.program_id(0)
    head = step + first

    def note(head_plus, code):
        @pl.when(head_plus > 0)
        def _():
            at = filled[head_plus - 1]
            where[(head_plus - 1) * 3 + jnp.minimum(at, 2)] = code
            filled[head_plus - 1] = at + 1

    def fetch(head, slot):
        for j in range(3):
            code = where[head * 3 + j]
            into_key = key_buf.at[slot, j]
            into_value = value_buf.at[slot, j, :, pl.ds(0, HEAD)]

            def start(source_key, source_value):
                pltpu.make_async_copy(source_key, into_key, sems.at[slot, j, 0]).start()
                pltpu.make_async_copy(source_value, into_value, sems.at[slot, j, 1]).start()

            @pl.when((code >= 0) & (code < CHIPS))
            def _():
                start(arrived.at[code, pl.ds(0, BLOCK)], arrived.at[code, pl.ds(BLOCK, BLOCK)])

            @pl.when(code == CHIPS)
            def _():
                start(other_keys.at[:, columns(head)], other_values.at[:, columns(head)])

    @pl.when(step == 0)
    def _():
        for h in range(HEADS):
            filled[h] = 0
            for j in range(3):
                where[h * 3 + j] = -1
        value_buf[...] = jnp.ones(value_buf.shape, value_buf.dtype)

        def direct(chip, carry):
            note(plan[ROW_DIRECT + chip, me], chip)
            return carry

        lax.fori_loop(0, CHIPS, direct, 0)
        note(plan[ROW_PARTNER, me], CHIPS)
        fetch(first, 0)

    slot = step % 2

    @pl.when(head + 1 < last)
    def _():
        fetch(head + 1, 1 - slot)

    present = jnp.minimum(filled[head], 3)
    for j in range(3):

        @pl.when(j < present)
        def _():
            pltpu.make_async_copy(
                arrived.at[0, pl.ds(0, BLOCK)], key_buf.at[slot, j], sems.at[slot, j, 0]
            ).wait()
            pltpu.make_async_copy(
                arrived.at[0, pl.ds(BLOCK, BLOCK)],
                value_buf.at[slot, j, :, pl.ds(0, HEAD)],
                sems.at[slot, j, 1],
            ).wait()

    def work(count):
        rows = 256
        for part in range(BLOCK // rows):
            length = (part + 1) * rows
            span = pl.ds(part * rows, rows)
            q = query[span, :]
            own = scores_of(q, own_key[0:length, :])
            row_iota = lax.broadcasted_iota(jnp.int32, (rows, length), 0) + part * rows
            col_iota = lax.broadcasted_iota(jnp.int32, (rows, length), 1)
            own = jnp.where(col_iota <= row_iota, own, -jnp.inf)
            others = [scores_of(q, key_buf[slot, j]) for j in range(count)]
            highest = jnp.max(own, axis=1, keepdims=True)
            for other in others:
                highest = jnp.maximum(highest, jnp.max(other, axis=1, keepdims=True))
            weight = jnp.exp2((own - highest) * SCALE).astype(jnp.bfloat16)
            ones = jnp.ones((length, HEAD), jnp.bfloat16)
            total = jnp.dot(
                weight,
                jnp.concatenate([own_value[0:length, :], ones], axis=1),
                preferred_element_type=jnp.float32,
            )
            for j, other in enumerate(others):
                weight = jnp.exp2((other - highest) * SCALE).astype(jnp.bfloat16)
                total = total + jnp.dot(
                    weight, value_buf[slot, j], preferred_element_type=jnp.float32
                )
            out[span, :] = (total[:, :HEAD] / total[:, HEAD:]).astype(jnp.bfloat16)
            if count < 3:
                state[0, span, 0 : 2 * HEAD] = total
                state[0, span, 2 * HEAD :] = jnp.broadcast_to(highest, (rows, HEAD))

    for count in range(4):

        @pl.when(present == count)
        def _():
            work(count)


def attend(first, last, before, plan, me, queries, keys, values, others, arrived):
    block = pl.BlockSpec((BLOCK, HEAD), lambda h: (0, h + first))
    count = last - first
    size = count * BLOCK * 4 * BLOCK * HEAD
    return pl.pallas_call(
        lambda *refs: attend_kernel(first, last, *refs),
        grid=(count,),
        in_specs=[SMEM, SMEM, block, block, block, ANY, ANY, ANY] + [ANY] * len(before),
        out_specs=[block, pl.BlockSpec((1, BLOCK, 3 * HEAD), lambda h: (h + first, 0, 0))],
        out_shape=[
            jax.ShapeDtypeStruct((BLOCK, HEADS * HEAD), jnp.bfloat16),
            jax.ShapeDtypeStruct((HEADS, BLOCK, 3 * HEAD), jnp.float32),
        ],
        input_output_aliases={8: 0, 9: 1} if before else {},
        scratch_shapes=[
            pltpu.SMEM((3 * HEADS,), jnp.int32),
            pltpu.SMEM((HEADS,), jnp.int32),
            pltpu.VMEM((2, 3, BLOCK, HEAD), jnp.bfloat16),
            pltpu.VMEM((2, 3, BLOCK, 2 * HEAD), jnp.bfloat16),
            pltpu.SemaphoreType.DMA((2, 3, 2)),
        ],
        cost_estimate=pl.CostEstimate(
            flops=16 * size, bytes_accessed=count * 3 * 2**20, transcendentals=size // HEAD
        ),
        compiler_params=BIG,
        name="attend",
    )(plan, me, queries, keys, values, *others, arrived, *before)


PENDING = KINDS + SPARE


def merge_kernel(plan, me_ref, query, state, out_before, pieces, *rest):
    count = KINDS - PARTNER + 1
    forwarded = rest[:count]
    out, waiting, carried, tile_buf, done_buf, state_sems, sems, done_sems = rest[count:]
    me = me_ref[0]

    def head_of(index):
        return plan[ROW_FORWARD_HEAD + index, me]

    for h in range(HEADS):
        waiting[h] = 0

    def count_one(index, carry):
        @pl.when(head_of(index) > 0)
        def _():
            waiting[head_of(index) - 1] = 1

        return carry

    lax.fori_loop(0, PENDING, count_one, 0)

    def load_state(h):
        return pltpu.make_async_copy(state.at[h], carried.at[h], state_sems.at[h])

    def store_out(h):
        return pltpu.make_async_copy(done_buf.at[h], out.at[:, columns(h)], done_sems.at[h])

    def each_waiting(action):
        def one(h, carry):
            @pl.when(waiting[h] > 0)
            def _():
                action(h)

            return carry

        lax.fori_loop(0, HEADS, one, 0)

    each_waiting(lambda h: load_state(h).start())
    for kind in range(KINDS):
        source = forwarded[0].at[kind] if kind < PARTNER else forwarded[kind - PARTNER + 1].at[0]

        @pl.when(head_of(kind) > 0)
        def _():
            pltpu.make_async_copy(source, tile_buf.at[kind], sems.at[kind]).start()

    def one_spare(index, carry):
        @pl.when(head_of(KINDS + index) > 0)
        def _():
            from_row = pl.ds(pl.multiple_of(index * PIECE, PIECE), PIECE)

            def one_piece(piece, carry):
                for half in range(2):
                    row = pl.multiple_of(half * BLOCK + piece * PIECE, PIECE)
                    pltpu.make_async_copy(
                        pieces.at[2 * piece + half, from_row],
                        tile_buf.at[KINDS + index, pl.ds(row, PIECE)],
                        sems.at[KINDS + index],
                    ).start()
                return carry

            lax.fori_loop(0, BLOCK // PIECE, one_piece, 0)

        return carry

    lax.fori_loop(0, SPARE, one_spare, 0)
    each_waiting(lambda h: load_state(h).wait())

    def one_tile(index, carry):
        @pl.when(head_of(index) > 0)
        def _():
            h = head_of(index) - 1
            pltpu.make_async_copy(tile_buf.at[0], tile_buf.at[index], sems.at[index]).wait()
            key = tile_buf[index, 0:BLOCK, :]
            ones = jnp.ones((BLOCK, HEAD), jnp.bfloat16)
            value = jnp.concatenate([tile_buf[index, BLOCK:, :], ones], axis=1)
            rows = 256
            for part in range(BLOCK // rows):
                span = pl.ds(part * rows, rows)
                scores = scores_of(query[span, columns(h)], key)
                old = carried[h, span, 2 * HEAD :]
                highest = jnp.maximum(old, jnp.max(scores, axis=1, keepdims=True))
                keep = jnp.exp2((old - highest) * SCALE)
                weight = jnp.exp2((scores - highest[:, :1]) * SCALE).astype(jnp.bfloat16)
                added = jnp.dot(weight, value, preferred_element_type=jnp.float32)
                total = carried[h, span, 0:HEAD] * keep + added[:, :HEAD]
                norm = carried[h, span, HEAD : 2 * HEAD] * keep + added[:, HEAD:]
                carried[h, span, 0:HEAD] = total
                carried[h, span, HEAD : 2 * HEAD] = norm
                carried[h, span, 2 * HEAD :] = highest
                done_buf[h, span, :] = (total / norm).astype(jnp.bfloat16)

        return carry

    lax.fori_loop(0, PENDING, one_tile, 0)
    each_waiting(lambda h: store_out(h).start())
    each_waiting(lambda h: store_out(h).wait())


def merge(plan, me, queries, state, out, pieces, forwarded):
    return pl.pallas_call(
        merge_kernel,
        in_specs=[SMEM, SMEM, VMEM, ANY, ANY, ANY] + [ANY] * len(forwarded),
        out_specs=ANY,
        out_shape=jax.ShapeDtypeStruct((BLOCK, HEADS * HEAD), jnp.bfloat16),
        input_output_aliases={4: 0},
        scratch_shapes=[
            pltpu.SMEM((HEADS,), jnp.int32),
            pltpu.VMEM((HEADS, BLOCK, 3 * HEAD), jnp.float32),
            pltpu.VMEM((PENDING, 2 * BLOCK, HEAD), jnp.bfloat16),
            pltpu.VMEM((HEADS, BLOCK, HEAD), jnp.bfloat16),
            pltpu.SemaphoreType.DMA((HEADS,)),
            pltpu.SemaphoreType.DMA((PENDING,)),
            pltpu.SemaphoreType.DMA((HEADS,)),
        ],
        compiler_params=BIG,
        name="merge",
    )(plan, me, queries, state, out, pieces, *forwarded)


LANES = [[2 * chip + core for chip in range(CHIPS)] for core in range(2)]
SWAP = [(device, device ^ 1) for device in range(DEVICES)]


def exchange(array):
    return lax.all_to_all(array, "ctx", 0, 0, axis_index_groups=LANES, tiled=True)


def full_attention(queries, keys, values, chosen_all, me):
    heads = jnp.arange(3 * HEADS, dtype=jnp.int32) // 3
    mine = lax.dynamic_index_in_dim(chosen_all, me, 0, keepdims=False)
    wants = chosen_all == me
    which = jnp.max(jnp.where(wants, heads[None, :], 0), axis=1)
    key_heads = keys.reshape(BLOCK, HEADS, HEAD).transpose(1, 0, 2)
    value_heads = values.reshape(BLOCK, HEADS, HEAD).transpose(1, 0, 2)
    got_key = lax.all_to_all(jnp.take(key_heads, which, axis=0), "ctx", 0, 0, tiled=True)
    got_value = lax.all_to_all(jnp.take(value_heads, which, axis=0), "ctx", 0, 0, tiled=True)
    q_heads = queries.reshape(BLOCK, HEADS, HEAD).transpose(1, 0, 2)
    allowed = jnp.arange(4 * BLOCK)[None, :] >= BLOCK
    allowed = allowed | (jnp.arange(4 * BLOCK)[None, :] <= jnp.arange(BLOCK)[:, None])

    def one_head(head):
        picks = lax.dynamic_slice(mine, (3 * head,), (3,))
        k = jnp.concatenate([key_heads[head], got_key[picks].reshape(3 * BLOCK, HEAD)], axis=0)
        v = jnp.concatenate([value_heads[head], got_value[picks].reshape(3 * BLOCK, HEAD)], axis=0)
        s = jnp.where(allowed, scores_of(q_heads[head], k), -jnp.inf)
        weight = jnp.exp2((s - jnp.max(s, axis=1, keepdims=True)) * SCALE)
        total = jnp.sum(weight, axis=1, keepdims=True)
        o = jnp.dot(weight.astype(jnp.bfloat16), v, preferred_element_type=jnp.float32)
        return (o / total).astype(jnp.bfloat16)

    out = lax.map(one_head, jnp.arange(HEADS))
    return out.transpose(1, 0, 2).reshape(BLOCK, HEADS * HEAD)


def body(queries, keys, values, chosen):
    me = lax.axis_index("ctx").astype(jnp.int32)
    me_ref = me.reshape(1)
    other_keys = lax.ppermute(keys, "ctx", SWAP)
    other_values = lax.ppermute(values, "ctx", SWAP)
    spread = jnp.broadcast_to(chosen.reshape(1, 3 * HEADS), (DEVICES, 3 * HEADS))
    chosen_all = lax.all_to_all(spread, "ctx", 0, 0, tiled=True)
    plan = make_plan(chosen_all.T)
    send = pack(plan, me_ref, keys, values, other_keys, other_values)
    arrived = exchange(send)
    pieces, *outgoing = forward(plan, me_ref, arrived)
    pieces = exchange(pieces)
    forwarded = [
        lax.ppermute(array, "ctx", shift_pairs(SHIFTS[0] if n == 0 else SHIFTS[PARTNER + n - 1]))
        for n, array in enumerate(outgoing)
    ]
    parts = ()
    step = HEADS // PARTS
    for first in range(0, HEADS, step):
        parts = attend(
            first,
            first + step,
            parts,
            plan,
            me_ref,
            queries,
            keys,
            values,
            (other_keys, other_values),
            arrived,
        )
    out = merge(plan, me_ref, queries, parts[1], parts[0], pieces, forwarded)
    return lax.cond(
        plan[ROW_LEFT, 0] > 0,
        lambda: full_attention(queries, keys, values, chosen_all, me),
        lambda: out,
    )


def solution(mesh):
    placed = (P("ctx", None), P("ctx", None), P("ctx", None), P("ctx", None, None))
    return jax.shard_map(
        body, mesh=mesh, in_specs=placed, out_specs=P("ctx", None), check_vma=False
    )
```

```python
import math

import jax
import jax.numpy as jnp
from jax import lax
from jax.experimental import pallas as pl
from jax.experimental.pallas import tpu as pltpu
from jax.sharding import PartitionSpec as P

HEAD = 128
HEADS = 16
BLOCK = 512
DEVICES = 128
CHIPS = 64
SCALE = math.log2(math.e) / math.sqrt(HEAD)

ONE = [(1, 0, 0), (3, 0, 0), (0, 1, 0), (0, 3, 0), (0, 0, 1), (0, 0, 3)]
PARTNER = 6
SHIFTS = [(0, 0, 0, 1)] * PARTNER
SHIFTS += [(*s, c) for s in ONE for c in (0, 1)]
KINDS = len(SHIFTS)
SPARE = 4
PIECE = 16
PARTS = 4
SLOT_ROWS = 2 * BLOCK + SPARE * PIECE

ROW_DIRECT = CHIPS
ROW_SPARE = ROW_DIRECT + CHIPS
ROW_FORWARD = ROW_SPARE + CHIPS
ROW_FORWARD_HEAD = ROW_FORWARD + KINDS
ROW_FROM_HEAD = ROW_FORWARD_HEAD + KINDS
ROW_FROM = ROW_FROM_HEAD + SPARE
ROW_FROM_RANK = ROW_FROM + SPARE
ROW_PARTNER = ROW_FROM_RANK + SPARE
ROW_LEFT = ROW_PARTNER + 1
ROWS = -(-(ROW_LEFT + 1) // 8) * 8


def through(device, shift):
    z, x, y, c = device // 32, device // 8 % 4, device // 2 % 4, device % 2
    dz, dx, dy, dc = shift
    return (((z + dz) % 4 * 4 + (x + dx) % 4) * 4 + (y + dy) % 4) * 2 + (c ^ dc)


def shift_pairs(shift):
    return [(through(b, shift), b) for b in range(DEVICES)]


def roll_lanes(array, amount):
    amount = amount % DEVICES
    return pltpu.roll(array, amount, 1) if amount else array


def permuted(array, shift, lane, inverse=False):
    dz, dx, dy, dc = shift
    if inverse:
        dz, dx, dy = -dz % 4, -dx % 4, -dy % 4
    if dz:
        array = roll_lanes(array, -32 * dz)
    if dx:
        inside = (lane // 8) % 4 + dx < 4
        array = jnp.where(inside, roll_lanes(array, -8 * dx), roll_lanes(array, 32 - 8 * dx))
    if dy:
        inside = (lane // 2) % 4 + dy < 4
        array = jnp.where(inside, roll_lanes(array, -2 * dy), roll_lanes(array, 8 - 2 * dy))
    if dc:
        array = jnp.where(lane % 2 == 0, roll_lanes(array, -1), roll_lanes(array, 1))
    return array


def plan_kernel(chosen_ref, out_ref):
    chip = lax.broadcasted_iota(jnp.int32, (CHIPS, DEVICES), 0)
    lane = lax.broadcasted_iota(jnp.int32, (CHIPS, DEVICES), 1)
    even = jnp.zeros((CHIPS, DEVICES), jnp.int32)
    odd = jnp.zeros((CHIPS, DEVICES), jnp.int32)
    for entry in range(3 * HEADS):
        owner = chosen_ref[entry : entry + 1, :]
        even = even + jnp.where(owner == 2 * chip, entry // 3 + 1, 0)
        odd = odd + jnp.where(owner == 2 * chip + 1, entry // 3 + 1, 0)
    home = lane // 2 == chip
    partner = jnp.sum(jnp.where(home, even + odd, 0), axis=0, keepdims=True)
    even = jnp.where(home, 0, even)
    odd = jnp.where(home, 0, odd)
    waiting = jnp.where(even > 0, odd, 0)
    slot = jnp.where(even > 0, even - 1, jnp.where(odd > 0, odd + 15, 0))
    direct = jnp.where(even > 0, even, odd)
    free = jnp.where(home, 0, jnp.where(direct > 0, 0, 1))
    options = jnp.zeros((CHIPS, DEVICES), jnp.int32)
    for shift in sorted(set(SHIFTS)):
        options = options + permuted(free, shift, lane)
    score = options * 64 + (chip + 17 * lane) % 64
    big = 1 << 20
    out_ref[...] = jnp.zeros((ROWS, DEVICES), jnp.int32)
    for kind, shift in enumerate(SHIFTS):
        able = (waiting > 0) & (permuted(free, shift, lane) > 0)
        rated = jnp.where(able, score, big)
        best = jnp.min(rated, axis=0, keepdims=True)
        picked = able & (rated == best)
        head = jnp.sum(jnp.where(picked, waiting, 0), axis=0, keepdims=True)
        back = permuted(jnp.where(picked, waiting + 16, 0), shift, lane, inverse=True)
        waiting = jnp.where(picked, 0, waiting)
        slot = jnp.where(back > 0, back - 1, slot)
        free = jnp.where(back > 0, 0, free)
        forward = jnp.sum(jnp.where(back > 0, chip, 0), axis=0, keepdims=True)
        out_ref[ROW_FORWARD + kind : ROW_FORWARD + kind + 1, :] = forward
        out_ref[ROW_FORWARD_HEAD + kind : ROW_FORWARD_HEAD + kind + 1, :] = head
    before = lax.broadcasted_iota(jnp.int32, (DEVICES, DEVICES), 0)
    after = lax.broadcasted_iota(jnp.int32, (DEVICES, DEVICES), 1)
    earlier = jnp.where((before < after) & (before % 2 == after % 2), 1.0, 0.0)
    rank = jnp.dot(
        jnp.where(waiting > 0, 1.0, 0.0), earlier, preferred_element_type=jnp.float32
    ).astype(jnp.int32)
    spare = jnp.zeros((CHIPS, DEVICES), jnp.int32)
    for index in range(SPARE):
        for core in range(2):
            chosen = (rank == index) & (lane % 2 == core)
            head = jnp.sum(jnp.where(chosen, waiting, 0), axis=1, keepdims=True)
            spare = jnp.where(lane == 2 * index + core, head, spare)
    out_ref[ROW_SPARE : ROW_SPARE + CHIPS, :] = spare
    excess = jnp.where((waiting > 0) & (rank >= SPARE), 1, 0)
    for index in range(SPARE):
        best = jnp.min(jnp.where(waiting > 0, chip, big), axis=0, keepdims=True)
        picked = (waiting > 0) & (chip == best)
        out_ref[ROW_FROM + index : ROW_FROM + index + 1, :] = jnp.where(best < big, best, 0)
        out_ref[ROW_FROM_RANK + index : ROW_FROM_RANK + index + 1, :] = jnp.minimum(
            jnp.sum(jnp.where(picked, rank, 0), axis=0, keepdims=True), SPARE - 1
        )
        out_ref[ROW_FROM_HEAD + index : ROW_FROM_HEAD + index + 1, :] = jnp.sum(
            jnp.where(picked, waiting, 0), axis=0, keepdims=True
        )
        waiting = jnp.where(picked, 0, waiting)
    excess = excess + waiting
    out_ref[ROW_PARTNER : ROW_PARTNER + 1, :] = partner
    left = jnp.max(jnp.max(excess, axis=0, keepdims=True), axis=1, keepdims=True)
    out_ref[ROW_LEFT : ROW_LEFT + 1, :] = jnp.broadcast_to(left, (1, DEVICES))
    out_ref[0:CHIPS, :] = slot
    out_ref[ROW_DIRECT : ROW_DIRECT + CHIPS, :] = direct


def make_plan(chosen_all):
    return pl.pallas_call(
        plan_kernel,
        out_shape=jax.ShapeDtypeStruct((ROWS, DEVICES), jnp.int32),
        name="plan",
    )(chosen_all)


def columns(head):
    return pl.ds(pl.multiple_of(head * HEAD, HEAD), HEAD)


def pack_kernel(plan, me_ref, keys, values, other_keys, other_values, send, sem):
    me = me_ref[0]
    chip, core = me // 2, me % 2

    def one_slot(dest, carry):
        code = plan[chip, 2 * dest + core]
        head = code % 16

        @pl.when(code // 16 == core)
        def _():
            for half, source in enumerate((keys, values)):
                pltpu.make_async_copy(
                    source.at[:, columns(head)], send.at[dest, pl.ds(half * BLOCK, BLOCK)], sem
                ).start()

        @pl.when(code // 16 != core)
        def _():
            for half, source in enumerate((other_keys, other_values)):
                pltpu.make_async_copy(
                    source.at[:, columns(head)], send.at[dest, pl.ds(half * BLOCK, BLOCK)], sem
                ).start()

        return carry

    lax.fori_loop(0, CHIPS, one_slot, 0)

    def one_spare(index, carry):
        head = jnp.maximum(plan[ROW_SPARE + chip, 2 * index + core] - 1, 0)
        into = pl.ds(pl.multiple_of(2 * BLOCK + index * PIECE, PIECE), PIECE)

        def one_piece(piece, carry):
            rows = pl.ds(pl.multiple_of(piece * PIECE, PIECE), PIECE)

            @pl.when(core == 1)
            def _():
                for half, source in enumerate((keys, values)):
                    pltpu.make_async_copy(
                        source.at[rows, columns(head)], send.at[2 * piece + half, into], sem
                    ).start()

            @pl.when(core == 0)
            def _():
                for half, source in enumerate((other_keys, other_values)):
                    pltpu.make_async_copy(
                        source.at[rows, columns(head)], send.at[2 * piece + half, into], sem
                    ).start()

            return carry

        return lax.fori_loop(0, CHIPS // 2, one_piece, carry)

    lax.fori_loop(0, SPARE, one_spare, 0)
    pltpu.make_async_copy(send, send, sem).wait()


ANY = pl.BlockSpec(memory_space=pl.ANY)
SMEM = pl.BlockSpec(memory_space=pltpu.SMEM)
VMEM = pl.BlockSpec(memory_space=pltpu.VMEM)
BIG = pltpu.CompilerParams(vmem_limit_bytes=60 * 1024 * 1024)


def tiles(count):
    return jax.ShapeDtypeStruct((count, 2 * BLOCK, HEAD), jnp.bfloat16)


def pack(plan, me, keys, values, other_keys, other_values):
    return pl.pallas_call(
        pack_kernel,
        in_specs=[SMEM, SMEM, VMEM, VMEM, VMEM, VMEM],
        out_specs=ANY,
        out_shape=jax.ShapeDtypeStruct((CHIPS, SLOT_ROWS, HEAD), jnp.bfloat16),
        scratch_shapes=[pltpu.SemaphoreType.DMA],
        compiler_params=BIG,
        name="pack",
    )(plan, me, keys, values, other_keys, other_values)


def forward_kernel(plan, me_ref, arrived, *rest):
    outs, (moving, gathered, sems, out_sems) = rest[:-4], rest[-4:]
    me = me_ref[0]
    core = me % 2
    loads, stores = [], []
    for kind in range(KINDS):
        out = outs[1].at[kind] if kind < PARTNER else outs[kind - PARTNER + 2].at[0]
        source = arrived.at[plan[ROW_FORWARD + kind, me], pl.ds(0, 2 * BLOCK)]
        loads.append(pltpu.make_async_copy(source, moving.at[kind], sems.at[kind]))
        stores.append(pltpu.make_async_copy(moving.at[kind], out, out_sems.at[kind]))
    for load in loads:
        load.start()

    def one_dest(dest, carry):
        for index in range(SPARE):
            chip = plan[ROW_FROM + index, 2 * dest + core]
            rank = plan[ROW_FROM_RANK + index, 2 * dest + core]
            row = pl.multiple_of(2 * BLOCK + rank * PIECE, PIECE)
            pltpu.make_async_copy(
                arrived.at[chip, pl.ds(row, PIECE)],
                gathered.at[dest, pl.ds(index * PIECE, PIECE)],
                sems.at[KINDS],
            ).start()
        return carry

    lax.fori_loop(0, CHIPS, one_dest, 0)
    for load, store in zip(loads, stores):
        load.wait()
        store.start()
    pltpu.make_async_copy(gathered, gathered, sems.at[KINDS]).wait()
    last = pltpu.make_async_copy(gathered, outs[0], out_sems.at[KINDS])
    last.start()
    for store in stores:
        store.wait()
    last.wait()


def forward(plan, me, arrived):
    return pl.pallas_call(
        forward_kernel,
        in_specs=[SMEM, SMEM, ANY],
        out_specs=[ANY] * (KINDS - PARTNER + 2),
        out_shape=[jax.ShapeDtypeStruct((CHIPS, SPARE * PIECE, HEAD), jnp.bfloat16)]
        + [tiles(PARTNER)]
        + [tiles(1)] * (KINDS - PARTNER),
        scratch_shapes=[
            pltpu.VMEM((KINDS, 2 * BLOCK, HEAD), jnp.bfloat16),
            pltpu.VMEM((CHIPS, SPARE * PIECE, HEAD), jnp.bfloat16),
            pltpu.SemaphoreType.DMA((KINDS + 1,)),
            pltpu.SemaphoreType.DMA((KINDS + 1,)),
        ],
        compiler_params=BIG,
        name="forward",
    )(plan, me, arrived)


def scores_of(query, key):
    return lax.dot_general(
        query, key, (((1,), (1,)), ((), ())), preferred_element_type=jnp.float32
    )


def attend_kernel(first, last, plan, me_ref, query, own_key, own_value, *rest):
    other_keys, other_values, arrived = rest[:3]
    out, state, where, filled, key_buf, value_buf, sems = rest[-7:]
    me = me_ref[0]
    step = pl.program_id(0)
    head = step + first

    def note(head_plus, code):
        @pl.when(head_plus > 0)
        def _():
            at = filled[head_plus - 1]
            where[(head_plus - 1) * 3 + jnp.minimum(at, 2)] = code
            filled[head_plus - 1] = at + 1

    def fetch(head, slot):
        for j in range(3):
            code = where[head * 3 + j]
            into_key = key_buf.at[slot, j]
            into_value = value_buf.at[slot, j, :, pl.ds(0, HEAD)]

            def start(source_key, source_value):
                pltpu.make_async_copy(source_key, into_key, sems.at[slot, j, 0]).start()
                pltpu.make_async_copy(source_value, into_value, sems.at[slot, j, 1]).start()

            @pl.when((code >= 0) & (code < CHIPS))
            def _():
                start(arrived.at[code, pl.ds(0, BLOCK)], arrived.at[code, pl.ds(BLOCK, BLOCK)])

            @pl.when(code == CHIPS)
            def _():
                start(other_keys.at[:, columns(head)], other_values.at[:, columns(head)])

    @pl.when(step == 0)
    def _():
        for h in range(HEADS):
            filled[h] = 0
            for j in range(3):
                where[h * 3 + j] = -1
        value_buf[...] = jnp.ones(value_buf.shape, value_buf.dtype)

        def direct(chip, carry):
            note(plan[ROW_DIRECT + chip, me], chip)
            return carry

        lax.fori_loop(0, CHIPS, direct, 0)
        note(plan[ROW_PARTNER, me], CHIPS)
        fetch(first, 0)

    slot = step % 2

    @pl.when(head + 1 < last)
    def _():
        fetch(head + 1, 1 - slot)

    present = jnp.minimum(filled[head], 3)
    for j in range(3):

        @pl.when(j < present)
        def _():
            pltpu.make_async_copy(
                arrived.at[0, pl.ds(0, BLOCK)], key_buf.at[slot, j], sems.at[slot, j, 0]
            ).wait()
            pltpu.make_async_copy(
                arrived.at[0, pl.ds(BLOCK, BLOCK)],
                value_buf.at[slot, j, :, pl.ds(0, HEAD)],
                sems.at[slot, j, 1],
            ).wait()

    def work(count):
        rows = 256
        for part in range(BLOCK // rows):
            length = (part + 1) * rows
            span = pl.ds(part * rows, rows)
            q = query[span, :]
            own = scores_of(q, own_key[0:length, :])
            row_iota = lax.broadcasted_iota(jnp.int32, (rows, length), 0) + part * rows
            col_iota = lax.broadcasted_iota(jnp.int32, (rows, length), 1)
            own = jnp.where(col_iota <= row_iota, own, -jnp.inf)
            others = [scores_of(q, key_buf[slot, j]) for j in range(count)]
            highest = jnp.max(own, axis=1, keepdims=True)
            for other in others:
                highest = jnp.maximum(highest, jnp.max(other, axis=1, keepdims=True))
            weight = jnp.exp2((own - highest) * SCALE).astype(jnp.bfloat16)
            ones = jnp.ones((length, HEAD), jnp.bfloat16)
            total = jnp.dot(
                weight,
                jnp.concatenate([own_value[0:length, :], ones], axis=1),
                preferred_element_type=jnp.float32,
            )
            for j, other in enumerate(others):
                weight = jnp.exp2((other - highest) * SCALE).astype(jnp.bfloat16)
                total = total + jnp.dot(
                    weight, value_buf[slot, j], preferred_element_type=jnp.float32
                )
            out[span, :] = (total[:, :HEAD] / total[:, HEAD:]).astype(jnp.bfloat16)
            if count < 3:
                state[0, span, 0 : 2 * HEAD] = total
                state[0, span, 2 * HEAD :] = jnp.broadcast_to(highest, (rows, HEAD))

    for count in range(4):

        @pl.when(present == count)
        def _():
            work(count)


def attend(first, last, before, plan, me, queries, keys, values, others, arrived):
    block = pl.BlockSpec((BLOCK, HEAD), lambda h: (0, h + first))
    count = last - first
    size = count * BLOCK * 4 * BLOCK * HEAD
    return pl.pallas_call(
        lambda *refs: attend_kernel(first, last, *refs),
        grid=(count,),
        in_specs=[SMEM, SMEM, block, block, block, ANY, ANY, ANY] + [ANY] * len(before),
        out_specs=[block, pl.BlockSpec((1, BLOCK, 3 * HEAD), lambda h: (h + first, 0, 0))],
        out_shape=[
            jax.ShapeDtypeStruct((BLOCK, HEADS * HEAD), jnp.bfloat16),
            jax.ShapeDtypeStruct((HEADS, BLOCK, 3 * HEAD), jnp.float32),
        ],
        input_output_aliases={8: 0, 9: 1} if before else {},
        scratch_shapes=[
            pltpu.SMEM((3 * HEADS,), jnp.int32),
            pltpu.SMEM((HEADS,), jnp.int32),
            pltpu.VMEM((2, 3, BLOCK, HEAD), jnp.bfloat16),
            pltpu.VMEM((2, 3, BLOCK, 2 * HEAD), jnp.bfloat16),
            pltpu.SemaphoreType.DMA((2, 3, 2)),
        ],
        cost_estimate=pl.CostEstimate(
            flops=16 * size, bytes_accessed=count * 3 * 2**20, transcendentals=size // HEAD
        ),
        compiler_params=BIG,
        name="attend",
    )(plan, me, queries, keys, values, *others, arrived, *before)


PENDING = KINDS + SPARE


def merge_kernel(plan, me_ref, query, state, out_before, pieces, *rest):
    count = KINDS - PARTNER + 1
    forwarded = rest[:count]
    out, waiting, carried, tile_buf, done_buf, state_sems, sems, done_sems = rest[count:]
    me = me_ref[0]

    def head_of(index):
        return plan[ROW_FORWARD_HEAD + index, me]

    for h in range(HEADS):
        waiting[h] = 0

    def count_one(index, carry):
        @pl.when(head_of(index) > 0)
        def _():
            waiting[head_of(index) - 1] = 1

        return carry

    lax.fori_loop(0, PENDING, count_one, 0)

    def load_state(h):
        return pltpu.make_async_copy(state.at[h], carried.at[h], state_sems.at[h])

    def store_out(h):
        return pltpu.make_async_copy(done_buf.at[h], out.at[:, columns(h)], done_sems.at[h])

    def each_waiting(action):
        def one(h, carry):
            @pl.when(waiting[h] > 0)
            def _():
                action(h)

            return carry

        lax.fori_loop(0, HEADS, one, 0)

    each_waiting(lambda h: load_state(h).start())
    for kind in range(KINDS):
        source = forwarded[0].at[kind] if kind < PARTNER else forwarded[kind - PARTNER + 1].at[0]

        @pl.when(head_of(kind) > 0)
        def _():
            pltpu.make_async_copy(source, tile_buf.at[kind], sems.at[kind]).start()

    def one_spare(index, carry):
        @pl.when(head_of(KINDS + index) > 0)
        def _():
            from_row = pl.ds(pl.multiple_of(index * PIECE, PIECE), PIECE)

            def one_piece(piece, carry):
                for half in range(2):
                    row = pl.multiple_of(half * BLOCK + piece * PIECE, PIECE)
                    pltpu.make_async_copy(
                        pieces.at[2 * piece + half, from_row],
                        tile_buf.at[KINDS + index, pl.ds(row, PIECE)],
                        sems.at[KINDS + index],
                    ).start()
                return carry

            lax.fori_loop(0, BLOCK // PIECE, one_piece, 0)

        return carry

    lax.fori_loop(0, SPARE, one_spare, 0)
    each_waiting(lambda h: load_state(h).wait())

    def one_tile(index, carry):
        @pl.when(head_of(index) > 0)
        def _():
            h = head_of(index) - 1
            pltpu.make_async_copy(tile_buf.at[0], tile_buf.at[index], sems.at[index]).wait()
            key = tile_buf[index, 0:BLOCK, :]
            ones = jnp.ones((BLOCK, HEAD), jnp.bfloat16)
            value = jnp.concatenate([tile_buf[index, BLOCK:, :], ones], axis=1)
            rows = 256
            for part in range(BLOCK // rows):
                span = pl.ds(part * rows, rows)
                scores = scores_of(query[span, columns(h)], key)
                old = carried[h, span, 2 * HEAD :]
                highest = jnp.maximum(old, jnp.max(scores, axis=1, keepdims=True))
                keep = jnp.exp2((old - highest) * SCALE)
                weight = jnp.exp2((scores - highest[:, :1]) * SCALE).astype(jnp.bfloat16)
                added = jnp.dot(weight, value, preferred_element_type=jnp.float32)
                total = carried[h, span, 0:HEAD] * keep + added[:, :HEAD]
                norm = carried[h, span, HEAD : 2 * HEAD] * keep + added[:, HEAD:]
                carried[h, span, 0:HEAD] = total
                carried[h, span, HEAD : 2 * HEAD] = norm
                carried[h, span, 2 * HEAD :] = highest
                done_buf[h, span, :] = (total / norm).astype(jnp.bfloat16)

        return carry

    lax.fori_loop(0, PENDING, one_tile, 0)
    each_waiting(lambda h: store_out(h).start())
    each_waiting(lambda h: store_out(h).wait())


def merge(plan, me, queries, state, out, pieces, forwarded):
    return pl.pallas_call(
        merge_kernel,
        in_specs=[SMEM, SMEM, VMEM, ANY, ANY, ANY] + [ANY] * len(forwarded),
        out_specs=ANY,
        out_shape=jax.ShapeDtypeStruct((BLOCK, HEADS * HEAD), jnp.bfloat16),
        input_output_aliases={4: 0},
        scratch_shapes=[
            pltpu.SMEM((HEADS,), jnp.int32),
            pltpu.VMEM((HEADS, BLOCK, 3 * HEAD), jnp.float32),
            pltpu.VMEM((PENDING, 2 * BLOCK, HEAD), jnp.bfloat16),
            pltpu.VMEM((HEADS, BLOCK, HEAD), jnp.bfloat16),
            pltpu.SemaphoreType.DMA((HEADS,)),
            pltpu.SemaphoreType.DMA((PENDING,)),
            pltpu.SemaphoreType.DMA((HEADS,)),
        ],
        compiler_params=BIG,
        name="merge",
    )(plan, me, queries, state, out, pieces, *forwarded)


LANES = [[2 * chip + core for chip in range(CHIPS)] for core in range(2)]
SWAP = [(device, device ^ 1) for device in range(DEVICES)]


def exchange(array):
    return lax.all_to_all(array, "ctx", 0, 0, axis_index_groups=LANES, tiled=True)


def full_attention(queries, keys, values, chosen_all, me):
    heads = jnp.arange(3 * HEADS, dtype=jnp.int32) // 3
    mine = lax.dynamic_index_in_dim(chosen_all, me, 0, keepdims=False)
    wants = chosen_all == me
    which = jnp.max(jnp.where(wants, heads[None, :], 0), axis=1)
    key_heads = keys.reshape(BLOCK, HEADS, HEAD).transpose(1, 0, 2)
    value_heads = values.reshape(BLOCK, HEADS, HEAD).transpose(1, 0, 2)
    got_key = lax.all_to_all(jnp.take(key_heads, which, axis=0), "ctx", 0, 0, tiled=True)
    got_value = lax.all_to_all(jnp.take(value_heads, which, axis=0), "ctx", 0, 0, tiled=True)
    q_heads = queries.reshape(BLOCK, HEADS, HEAD).transpose(1, 0, 2)
    allowed = jnp.arange(4 * BLOCK)[None, :] >= BLOCK
    allowed = allowed | (jnp.arange(4 * BLOCK)[None, :] <= jnp.arange(BLOCK)[:, None])

    def one_head(head):
        picks = lax.dynamic_slice(mine, (3 * head,), (3,))
        k = jnp.concatenate([key_heads[head], got_key[picks].reshape(3 * BLOCK, HEAD)], axis=0)
        v = jnp.concatenate([value_heads[head], got_value[picks].reshape(3 * BLOCK, HEAD)], axis=0)
        s = jnp.where(allowed, scores_of(q_heads[head], k), -jnp.inf)
        weight = jnp.exp2((s - jnp.max(s, axis=1, keepdims=True)) * SCALE)
        total = jnp.sum(weight, axis=1, keepdims=True)
        o = jnp.dot(weight.astype(jnp.bfloat16), v, preferred_element_type=jnp.float32)
        return (o / total).astype(jnp.bfloat16)

    out = lax.map(one_head, jnp.arange(HEADS))
    return out.transpose(1, 0, 2).reshape(BLOCK, HEADS * HEAD)


def body(queries, keys, values, chosen):
    me = lax.axis_index("ctx").astype(jnp.int32)
    me_ref = me.reshape(1)
    other_keys = lax.ppermute(keys, "ctx", SWAP)
    other_values = lax.ppermute(values, "ctx", SWAP)
    spread = jnp.broadcast_to(chosen.reshape(1, 3 * HEADS), (DEVICES, 3 * HEADS))
    chosen_all = lax.all_to_all(spread, "ctx", 0, 0, tiled=True)
    plan = make_plan(chosen_all.T)
    send = pack(plan, me_ref, keys, values, other_keys, other_values)
    held = (exchange(send), plan, queries, keys, values, other_keys, other_values, me_ref)
    held = lax.optimization_barrier(held)
    arrived, plan, queries, keys, values, other_keys, other_values, me_ref = held
    pieces, *outgoing = forward(plan, me_ref, arrived)
    pieces = exchange(pieces)
    forwarded = [
        lax.ppermute(array, "ctx", shift_pairs(SHIFTS[0] if n == 0 else SHIFTS[PARTNER + n - 1]))
        for n, array in enumerate(outgoing)
    ]
    parts = ()
    step = HEADS // PARTS
    for first in range(0, HEADS, step):
        parts = attend(
            first,
            first + step,
            parts,
            plan,
            me_ref,
            queries,
            keys,
            values,
            (other_keys, other_values),
            arrived,
        )
    out = merge(plan, me_ref, queries, parts[1], parts[0], pieces, forwarded)
    return lax.cond(
        plan[ROW_LEFT, 0] > 0,
        lambda: full_attention(queries, keys, values, chosen_all, me),
        lambda: out,
    )


def solution(mesh):
    placed = (P("ctx", None), P("ctx", None), P("ctx", None), P("ctx", None, None))
    return jax.shard_map(
        body, mesh=mesh, in_specs=placed, out_specs=P("ctx", None), check_vma=False
    )
```

```python
import math

import jax
import jax.numpy as jnp
from jax import lax
from jax.experimental import pallas as pl
from jax.experimental.pallas import tpu as pltpu
from jax.sharding import PartitionSpec as P

HEAD = 128
HEADS = 16
BLOCK = 512
DEVICES = 128
CHIPS = 64
SCALE = math.log2(math.e) / math.sqrt(HEAD)

ONE = [(1, 0, 0), (3, 0, 0), (0, 1, 0), (0, 3, 0), (0, 0, 1), (0, 0, 3)]
PARTNER = 6
SHIFTS = [(0, 0, 0, 1)] * PARTNER
SHIFTS += [(*s, c) for s in ONE for c in (0, 1)]
KINDS = len(SHIFTS)
SPARE = 5
PIECE = 16
PARTS = (0, 6, 11, 16)
HALF = BLOCK // PIECE
SLOT_PIECES = 2 * HALF + SPARE
SLOT_ROWS = SLOT_PIECES * PIECE

ROW_DIRECT = CHIPS
ROW_SPARE = ROW_DIRECT + CHIPS
ROW_FORWARD = ROW_SPARE + CHIPS
ROW_FORWARD_HEAD = ROW_FORWARD + KINDS
ROW_FROM_HEAD = ROW_FORWARD_HEAD + KINDS
ROW_FROM = ROW_FROM_HEAD + SPARE
ROW_FROM_RANK = ROW_FROM + SPARE
ROW_PARTNER = ROW_FROM_RANK + SPARE
ROW_LEFT = ROW_PARTNER + 1
ROWS = -(-(ROW_LEFT + 1) // 8) * 8


def through(device, shift):
    z, x, y, c = device // 32, device // 8 % 4, device // 2 % 4, device % 2
    dz, dx, dy, dc = shift
    return (((z + dz) % 4 * 4 + (x + dx) % 4) * 4 + (y + dy) % 4) * 2 + (c ^ dc)


def shift_pairs(shift):
    return [(through(b, shift), b) for b in range(DEVICES)]


def roll_lanes(array, amount):
    amount = amount % DEVICES
    return pltpu.roll(array, amount, 1) if amount else array


def permuted(array, shift, lane, inverse=False):
    dz, dx, dy, dc = shift
    if inverse:
        dz, dx, dy = -dz % 4, -dx % 4, -dy % 4
    if dz:
        array = roll_lanes(array, -32 * dz)
    if dx:
        inside = (lane // 8) % 4 + dx < 4
        array = jnp.where(inside, roll_lanes(array, -8 * dx), roll_lanes(array, 32 - 8 * dx))
    if dy:
        inside = (lane // 2) % 4 + dy < 4
        array = jnp.where(inside, roll_lanes(array, -2 * dy), roll_lanes(array, 8 - 2 * dy))
    if dc:
        array = jnp.where(lane % 2 == 0, roll_lanes(array, -1), roll_lanes(array, 1))
    return array


def plan_kernel(chosen_ref, out_ref):
    chip = lax.broadcasted_iota(jnp.int32, (CHIPS, DEVICES), 0)
    lane = lax.broadcasted_iota(jnp.int32, (CHIPS, DEVICES), 1)
    even = jnp.zeros((CHIPS, DEVICES), jnp.int32)
    odd = jnp.zeros((CHIPS, DEVICES), jnp.int32)
    for entry in range(3 * HEADS):
        owner = chosen_ref[entry : entry + 1, :]
        even = even + jnp.where(owner == 2 * chip, entry // 3 + 1, 0)
        odd = odd + jnp.where(owner == 2 * chip + 1, entry // 3 + 1, 0)
    home = lane // 2 == chip
    partner = jnp.sum(jnp.where(home, even + odd, 0), axis=0, keepdims=True)
    even = jnp.where(home, 0, even)
    odd = jnp.where(home, 0, odd)
    waiting = jnp.where(even > 0, odd, 0)
    slot = jnp.where(even > 0, even - 1, jnp.where(odd > 0, odd + 15, 0))
    direct = jnp.where(even > 0, even, odd)
    free = jnp.where(home, 0, jnp.where(direct > 0, 0, 1))
    options = jnp.zeros((CHIPS, DEVICES), jnp.int32)
    for shift in sorted(set(SHIFTS)):
        options = options + permuted(free, shift, lane)
    score = options * 64 + (chip + 17 * lane) % 64
    big = 1 << 20
    out_ref[...] = jnp.zeros((ROWS, DEVICES), jnp.int32)
    for kind, shift in enumerate(SHIFTS):
        able = (waiting > 0) & (permuted(free, shift, lane) > 0)
        rated = jnp.where(able, score, big)
        best = jnp.min(rated, axis=0, keepdims=True)
        picked = able & (rated == best)
        head = jnp.sum(jnp.where(picked, waiting, 0), axis=0, keepdims=True)
        back = permuted(jnp.where(picked, waiting + 16, 0), shift, lane, inverse=True)
        waiting = jnp.where(picked, 0, waiting)
        slot = jnp.where(back > 0, back - 1, slot)
        free = jnp.where(back > 0, 0, free)
        forward = jnp.sum(jnp.where(back > 0, chip, 0), axis=0, keepdims=True)
        out_ref[ROW_FORWARD + kind : ROW_FORWARD + kind + 1, :] = forward
        out_ref[ROW_FORWARD_HEAD + kind : ROW_FORWARD_HEAD + kind + 1, :] = head
    before = lax.broadcasted_iota(jnp.int32, (DEVICES, DEVICES), 0)
    after = lax.broadcasted_iota(jnp.int32, (DEVICES, DEVICES), 1)
    earlier = jnp.where((before < after) & (before % 2 == after % 2), 1.0, 0.0)
    rank = jnp.dot(
        jnp.where(waiting > 0, 1.0, 0.0), earlier, preferred_element_type=jnp.float32
    ).astype(jnp.int32)
    spare = jnp.zeros((CHIPS, DEVICES), jnp.int32)
    for index in range(SPARE):
        for core in range(2):
            chosen = (rank == index) & (lane % 2 == core)
            head = jnp.sum(jnp.where(chosen, waiting, 0), axis=1, keepdims=True)
            spare = jnp.where(lane == 2 * index + core, head, spare)
    out_ref[ROW_SPARE : ROW_SPARE + CHIPS, :] = spare
    excess = jnp.where((waiting > 0) & (rank >= SPARE), 1, 0)
    for index in range(SPARE):
        best = jnp.min(jnp.where(waiting > 0, chip, big), axis=0, keepdims=True)
        picked = (waiting > 0) & (chip == best)
        out_ref[ROW_FROM + index : ROW_FROM + index + 1, :] = jnp.where(best < big, best, 0)
        out_ref[ROW_FROM_RANK + index : ROW_FROM_RANK + index + 1, :] = jnp.minimum(
            jnp.sum(jnp.where(picked, rank, 0), axis=0, keepdims=True), SPARE - 1
        )
        out_ref[ROW_FROM_HEAD + index : ROW_FROM_HEAD + index + 1, :] = jnp.sum(
            jnp.where(picked, waiting, 0), axis=0, keepdims=True
        )
        waiting = jnp.where(picked, 0, waiting)
    excess = excess + waiting
    out_ref[ROW_PARTNER : ROW_PARTNER + 1, :] = partner
    left = jnp.max(jnp.max(excess, axis=0, keepdims=True), axis=1, keepdims=True)
    out_ref[ROW_LEFT : ROW_LEFT + 1, :] = jnp.broadcast_to(left, (1, DEVICES))
    out_ref[0:CHIPS, :] = slot
    out_ref[ROW_DIRECT : ROW_DIRECT + CHIPS, :] = direct


def make_plan(chosen_all):
    return pl.pallas_call(
        plan_kernel,
        out_shape=jax.ShapeDtypeStruct((ROWS, DEVICES), jnp.int32),
        name="plan",
    )(chosen_all)


def columns(head):
    return pl.ds(pl.multiple_of(head * HEAD, HEAD), HEAD)


def pack_kernel(plan, me_ref, keys, values, other_keys, other_values, send, sem):
    me = me_ref[0]
    chip, core = me // 2, me % 2

    def one_slot(dest, carry):
        code = plan[chip, 2 * dest + core]

        def copy(*sources):
            for half, source in enumerate(sources):
                pltpu.make_async_copy(
                    source.at[:, :, columns(code % 16)],
                    send.at[dest // 2, dest % 2, pl.ds(half * HALF, HALF)],
                    sem,
                ).start()

        @pl.when(code // 16 == core)
        def _():
            copy(keys, values)

        @pl.when(code // 16 != core)
        def _():
            copy(other_keys, other_values)

        return carry

    lax.fori_loop(0, CHIPS, one_slot, 0)

    def one_spare(index, carry):
        head = jnp.maximum(plan[ROW_SPARE + chip, 2 * index + core] - 1, 0)

        def copy(*sources):
            for half, source in enumerate(sources):
                pltpu.make_async_copy(
                    source.at[:, :, columns(head)], send.at[:, half, 2 * HALF + index], sem
                ).start()

        @pl.when(core == 1)
        def _():
            copy(keys, values)

        @pl.when(core == 0)
        def _():
            copy(other_keys, other_values)

        return carry

    lax.fori_loop(0, SPARE, one_spare, 0)
    pltpu.make_async_copy(send, send, sem).wait()


ANY = pl.BlockSpec(memory_space=pl.ANY)
SMEM = pl.BlockSpec(memory_space=pltpu.SMEM)
VMEM = pl.BlockSpec(memory_space=pltpu.VMEM)
BIG = pltpu.CompilerParams(vmem_limit_bytes=60 * 1024 * 1024)


def tiles(count):
    return jax.ShapeDtypeStruct((count, 2 * HALF, PIECE, HEAD), jnp.bfloat16)


def pack(plan, me, keys, values, other_keys, other_values):
    return pl.pallas_call(
        pack_kernel,
        in_specs=[SMEM, SMEM, VMEM, VMEM, VMEM, VMEM],
        out_specs=ANY,
        out_shape=jax.ShapeDtypeStruct((HALF, 2, SLOT_PIECES, PIECE, HEAD), jnp.bfloat16),
        scratch_shapes=[pltpu.SemaphoreType.DMA],
        compiler_params=BIG,
        name="pack",
    )(plan, me, *(a.reshape(HALF, PIECE, -1) for a in (keys, values, other_keys, other_values)))


def forward_kernel(plan, me_ref, arrived, *rest):
    outs, (where, moving, spare, gathered, sems, out_sems) = rest[:-6], rest[-6:]
    me = me_ref[0]
    core = me % 2
    loads, stores = [], []
    for kind in range(KINDS):
        out = outs[1].at[kind] if kind < PARTNER else outs[kind - PARTNER + 2].at[0]
        source = arrived.at[plan[ROW_FORWARD + kind, me], pl.ds(0, 2 * HALF)]
        loads.append(pltpu.make_async_copy(source, moving.at[kind], sems.at[kind]))
        stores.append(pltpu.make_async_copy(moving.at[kind], out, out_sems.at[kind]))
    for load in loads:
        load.start()

    load_spare = pltpu.make_async_copy(
        arrived.at[:, pl.ds(2 * HALF, SPARE)], spare, sems.at[KINDS]
    )
    load_spare.start()

    def note(head_plus, code):
        @pl.when(head_plus > 0)
        def _():
            at = where[3 * HEADS + head_plus - 1]
            where[(head_plus - 1) * 3 + jnp.minimum(at, 2)] = code
            where[3 * HEADS + head_plus - 1] = at + 1

    for entry in range(4 * HEADS):
        where[entry] = 0

    def direct(chip, carry):
        note(plan[ROW_DIRECT + chip, me], chip)
        return carry

    lax.fori_loop(0, CHIPS, direct, 0)
    note(plan[ROW_PARTNER, me], CHIPS)
    for load, store in zip(loads, stores):
        load.wait()
        store.start()
    load_spare.wait()

    def one_dest(dest, carry):
        for index in range(SPARE):
            chip = plan[ROW_FROM + index, 2 * dest + core]
            rank = plan[ROW_FROM_RANK + index, 2 * dest + core]
            gathered[dest, index] = spare[chip, rank]
        return carry

    lax.fori_loop(0, CHIPS, one_dest, 0)
    last = pltpu.make_async_copy(gathered, outs[0], out_sems.at[KINDS])
    last.start()
    for store in stores:
        store.wait()
    last.wait()


def forward(plan, me, arrived):
    return pl.pallas_call(
        forward_kernel,
        in_specs=[SMEM, SMEM, ANY],
        out_specs=[ANY] * (KINDS - PARTNER + 2) + [SMEM],
        out_shape=[jax.ShapeDtypeStruct((CHIPS, SPARE, PIECE, HEAD), jnp.bfloat16)]
        + [tiles(PARTNER)]
        + [tiles(1)] * (KINDS - PARTNER)
        + [jax.ShapeDtypeStruct((4 * HEADS,), jnp.int32)],
        scratch_shapes=[
            pltpu.VMEM((KINDS, 2 * HALF, PIECE, HEAD), jnp.bfloat16),
            pltpu.VMEM((CHIPS, SPARE, PIECE, HEAD), jnp.bfloat16),
            pltpu.VMEM((CHIPS, SPARE, PIECE, HEAD), jnp.bfloat16),
            pltpu.SemaphoreType.DMA((KINDS + 1,)),
            pltpu.SemaphoreType.DMA((KINDS + 1,)),
        ],
        compiler_params=BIG,
        name="forward",
    )(plan, me, arrived.reshape(CHIPS, SLOT_PIECES, PIECE, HEAD))


def scores_of(query, key):
    return lax.dot_general(
        query, key, (((1,), (1,)), ((), ())), preferred_element_type=jnp.float32
    )


ROWS_AT_ONCE = 256


def add_tile(query, key, value, state):
    results = []
    for start in range(0, BLOCK, ROWS_AT_ONCE):
        rows = slice(start, start + ROWS_AT_ONCE)
        scores = scores_of(query[rows, :], key)
        old = state[rows, 2 * HEAD :]
        highest = jnp.maximum(old, jnp.max(scores, axis=1, keepdims=True))
        keep = jnp.exp2((old - highest) * SCALE)
        weight = jnp.exp2((scores - highest[:, :1]) * SCALE).astype(jnp.bfloat16)
        added = jnp.dot(weight, value, preferred_element_type=jnp.float32)
        total = state[rows, 0:HEAD] * keep + added[:, :HEAD]
        norm = state[rows, HEAD : 2 * HEAD] * keep + added[:, HEAD:]
        results.append((rows, total, norm, highest))
    for rows, total, norm, highest in results:
        state[rows, 0:HEAD] = total
        state[rows, HEAD : 2 * HEAD] = norm
        state[rows, 2 * HEAD :] = highest


def attend_kernel(first, last, where, query, own_key, own_value, *rest):
    other_keys, other_values, arrived = rest[:3]
    out, state, key_buf, value_buf, sems = rest[-5:]
    step = pl.program_id(0)
    head = step + first

    def fetch(head, slot):
        for j in range(3):
            code = where[head * 3 + j]
            into_key = key_buf.at[slot, j]
            into_value = value_buf.at[slot, j, :, pl.ds(0, HEAD)]

            def start(source_key, source_value):
                pltpu.make_async_copy(source_key, into_key, sems.at[slot, j, 0]).start()
                pltpu.make_async_copy(source_value, into_value, sems.at[slot, j, 1]).start()

            @pl.when(code < CHIPS)
            def _():
                start(arrived.at[code, pl.ds(0, BLOCK)], arrived.at[code, pl.ds(BLOCK, BLOCK)])

            @pl.when(code == CHIPS)
            def _():
                start(other_keys.at[:, columns(head)], other_values.at[:, columns(head)])

    @pl.when(step == 0)
    def _():
        fetch(first, 0)
        ones = jnp.ones((BLOCK, HEAD), jnp.bfloat16)
        for pair in range(2):
            for j in range(3):
                value_buf[pair, j, :, HEAD:] = ones

    slot = step % 2

    @pl.when(head + 1 < last)
    def _():
        fetch(head + 1, 1 - slot)

    for j in range(3):
        pltpu.make_async_copy(
            arrived.at[0, pl.ds(0, BLOCK)], key_buf.at[slot, j], sems.at[slot, j, 0]
        ).wait()
        pltpu.make_async_copy(
            arrived.at[0, pl.ds(BLOCK, BLOCK)],
            value_buf.at[slot, j, :, pl.ds(0, HEAD)],
            sems.at[slot, j, 1],
        ).wait()
    present = where[3 * HEADS + head]

    for start in range(0, BLOCK, ROWS_AT_ONCE):
        stop = start + ROWS_AT_ONCE
        q = query[start:stop, :]
        own = scores_of(q, own_key[0:stop, :])
        row_iota = lax.broadcasted_iota(jnp.int32, own.shape, 0) + start
        col_iota = lax.broadcasted_iota(jnp.int32, own.shape, 1)
        own = jnp.where(col_iota <= row_iota, own, -jnp.inf)
        highest = jnp.max(own, axis=1, keepdims=True)
        weight = jnp.exp2((own - highest) * SCALE).astype(jnp.bfloat16)
        ones = jnp.ones((stop, HEAD), jnp.bfloat16)
        value = jnp.concatenate([own_value[0:stop, :], ones], axis=1)
        total = jnp.dot(weight, value, preferred_element_type=jnp.float32)
        for j in range(3):
            scores = scores_of(q, key_buf[slot, j])
            top = jnp.where(j < present, jnp.max(scores, axis=1, keepdims=True), -jnp.inf)
            top = jnp.maximum(highest, top)
            keep = jnp.exp2((highest - top) * SCALE)
            base = jnp.where(j < present, top, jnp.inf)
            weight = jnp.exp2((scores - base) * SCALE).astype(jnp.bfloat16)
            added = jnp.dot(weight, value_buf[slot, j], preferred_element_type=jnp.float32)
            total = total * keep + added
            highest = top
        out[start:stop, :] = (total[:, :HEAD] / total[:, HEAD:]).astype(jnp.bfloat16)
        state[0, start:stop, 0 : 2 * HEAD] = total
        state[0, start:stop, 2 * HEAD :] = jnp.broadcast_to(highest, (ROWS_AT_ONCE, HEAD))


def attend(first, last, before, where, queries, keys, values, others, arrived):
    block = pl.BlockSpec((BLOCK, HEAD), lambda h: (0, h + first))
    count = last - first
    size = count * BLOCK * 4 * BLOCK * HEAD
    return pl.pallas_call(
        lambda *refs: attend_kernel(first, last, *refs),
        grid=(count,),
        in_specs=[SMEM, block, block, block, ANY, ANY, ANY] + [ANY] * len(before),
        out_specs=[block, pl.BlockSpec((1, BLOCK, 3 * HEAD), lambda h: (h + first, 0, 0))],
        out_shape=[
            jax.ShapeDtypeStruct((BLOCK, HEADS * HEAD), jnp.bfloat16),
            jax.ShapeDtypeStruct((HEADS, BLOCK, 3 * HEAD), jnp.float32),
        ],
        input_output_aliases={7: 0, 8: 1} if before else {},
        scratch_shapes=[
            pltpu.VMEM((2, 3, BLOCK, HEAD), jnp.bfloat16),
            pltpu.VMEM((2, 3, BLOCK, 2 * HEAD), jnp.bfloat16),
            pltpu.SemaphoreType.DMA((2, 3, 2)),
        ],
        cost_estimate=pl.CostEstimate(
            flops=16 * size, bytes_accessed=count * 3 * 2**20, transcendentals=size // HEAD
        ),
        compiler_params=BIG,
        name="attend",
    )(where, queries, keys, values, *others, arrived, *before)


PENDING = KINDS + SPARE


def merge_kernel(plan, me_ref, query, state, out_before, pieces, *rest):
    count = KINDS - PARTNER + 1
    forwarded = rest[:count]
    out, waiting, carried, tile_buf, done_buf, state_sems, sems, done_sems = rest[count:]
    me = me_ref[0]

    def head_of(index):
        return plan[ROW_FORWARD_HEAD + index, me]

    for h in range(HEADS):
        waiting[h] = 0

    def count_one(index, carry):
        @pl.when(head_of(index) > 0)
        def _():
            waiting[head_of(index) - 1] = 1

        return carry

    lax.fori_loop(0, PENDING, count_one, 0)

    def load_state(h):
        return pltpu.make_async_copy(state.at[h], carried.at[h], state_sems.at[h])

    def store_out(h):
        return pltpu.make_async_copy(done_buf.at[h], out.at[:, columns(h)], done_sems.at[h])

    def each_waiting(action):
        def one(h, carry):
            @pl.when(waiting[h] > 0)
            def _():
                action(h)

            return carry

        lax.fori_loop(0, HEADS, one, 0)

    each_waiting(lambda h: load_state(h).start())
    for kind in range(KINDS):
        source = forwarded[0].at[kind] if kind < PARTNER else forwarded[kind - PARTNER + 1].at[0]

        @pl.when(head_of(kind) > 0)
        def _():
            pltpu.make_async_copy(source, tile_buf.at[kind], sems.at[kind]).start()

    def one_spare(index, carry):
        @pl.when(head_of(KINDS + index) > 0)
        def _():
            for half in range(2):
                pltpu.make_async_copy(
                    pieces.at[:, half, index],
                    tile_buf.at[KINDS + index, pl.ds(half * HALF, HALF)],
                    sems.at[KINDS + index],
                ).start()

        return carry

    lax.fori_loop(0, SPARE, one_spare, 0)
    each_waiting(lambda h: load_state(h).wait())

    def one_tile(index, carry):
        @pl.when(head_of(index) > 0)
        def _():
            h = head_of(index) - 1
            pltpu.make_async_copy(tile_buf.at[0], tile_buf.at[index], sems.at[index]).wait()
            key = tile_buf[index, 0:HALF].reshape(BLOCK, HEAD)
            ones = jnp.ones((BLOCK, HEAD), jnp.bfloat16)
            value = tile_buf[index, HALF : 2 * HALF].reshape(BLOCK, HEAD)
            value = jnp.concatenate([value, ones], axis=1)
            add_tile(query.at[:, columns(h)], key, value, carried.at[h])

        return carry

    lax.fori_loop(0, PENDING, one_tile, 0)

    def finish(h):
        total, norm = carried[h, :, 0:HEAD], carried[h, :, HEAD : 2 * HEAD]
        done_buf[h] = (total / norm).astype(jnp.bfloat16)
        store_out(h).start()

    each_waiting(finish)
    each_waiting(lambda h: store_out(h).wait())


def merge(plan, me, queries, state, out, pieces, forwarded):
    return pl.pallas_call(
        merge_kernel,
        in_specs=[SMEM, SMEM, VMEM, ANY, ANY, ANY] + [ANY] * len(forwarded),
        out_specs=ANY,
        out_shape=jax.ShapeDtypeStruct((BLOCK, HEADS * HEAD), jnp.bfloat16),
        input_output_aliases={4: 0},
        scratch_shapes=[
            pltpu.SMEM((HEADS,), jnp.int32),
            pltpu.VMEM((HEADS, BLOCK, 3 * HEAD), jnp.float32),
            pltpu.VMEM((PENDING, 2 * HALF, PIECE, HEAD), jnp.bfloat16),
            pltpu.VMEM((HEADS, BLOCK, HEAD), jnp.bfloat16),
            pltpu.SemaphoreType.DMA((HEADS,)),
            pltpu.SemaphoreType.DMA((PENDING,)),
            pltpu.SemaphoreType.DMA((HEADS,)),
        ],
        compiler_params=BIG,
        name="merge",
    )(plan, me, queries, state, out, pieces.reshape(HALF, 2, SPARE, PIECE, HEAD), *forwarded)


LANES = [[2 * chip + core for chip in range(CHIPS)] for core in range(2)]
SWAP = [(device, device ^ 1) for device in range(DEVICES)]


def exchange(array):
    return lax.all_to_all(array, "ctx", 0, 0, axis_index_groups=LANES, tiled=True)


def full_attention(queries, keys, values, chosen_all, me):
    heads = jnp.arange(3 * HEADS, dtype=jnp.int32) // 3
    mine = lax.dynamic_index_in_dim(chosen_all, me, 0, keepdims=False)
    wants = chosen_all == me
    which = jnp.max(jnp.where(wants, heads[None, :], 0), axis=1)
    key_heads = keys.reshape(BLOCK, HEADS, HEAD).transpose(1, 0, 2)
    value_heads = values.reshape(BLOCK, HEADS, HEAD).transpose(1, 0, 2)
    got_key = lax.all_to_all(jnp.take(key_heads, which, axis=0), "ctx", 0, 0, tiled=True)
    got_value = lax.all_to_all(jnp.take(value_heads, which, axis=0), "ctx", 0, 0, tiled=True)
    q_heads = queries.reshape(BLOCK, HEADS, HEAD).transpose(1, 0, 2)
    allowed = jnp.arange(4 * BLOCK)[None, :] >= BLOCK
    allowed = allowed | (jnp.arange(4 * BLOCK)[None, :] <= jnp.arange(BLOCK)[:, None])

    def one_head(head):
        picks = lax.dynamic_slice(mine, (3 * head,), (3,))
        k = jnp.concatenate([key_heads[head], got_key[picks].reshape(3 * BLOCK, HEAD)], axis=0)
        v = jnp.concatenate([value_heads[head], got_value[picks].reshape(3 * BLOCK, HEAD)], axis=0)
        s = jnp.where(allowed, scores_of(q_heads[head], k), -jnp.inf)
        weight = jnp.exp2((s - jnp.max(s, axis=1, keepdims=True)) * SCALE)
        total = jnp.sum(weight, axis=1, keepdims=True)
        o = jnp.dot(weight.astype(jnp.bfloat16), v, preferred_element_type=jnp.float32)
        return (o / total).astype(jnp.bfloat16)

    out = lax.map(one_head, jnp.arange(HEADS))
    return out.transpose(1, 0, 2).reshape(BLOCK, HEADS * HEAD)


def body(queries, keys, values, chosen):
    me = lax.axis_index("ctx").astype(jnp.int32)
    me_ref = me.reshape(1)
    other_keys = lax.ppermute(keys, "ctx", SWAP)
    other_values = lax.ppermute(values, "ctx", SWAP)
    spread = jnp.broadcast_to(chosen.reshape(1, 3 * HEADS), (DEVICES, 3 * HEADS))
    chosen_all = lax.all_to_all(spread, "ctx", 0, 0, tiled=True)
    plan = make_plan(chosen_all.T)
    send = pack(plan, me_ref, keys, values, other_keys, other_values)
    sent = exchange(send.reshape(CHIPS, SLOT_ROWS, HEAD))
    held = (sent, plan, queries, keys, values, other_keys, other_values, me_ref)
    held = lax.optimization_barrier(held)
    arrived, plan, queries, keys, values, other_keys, other_values, me_ref = held
    pieces, *outgoing, where = forward(plan, me_ref, arrived)
    pieces = exchange(pieces)
    forwarded = [
        lax.ppermute(array, "ctx", shift_pairs(SHIFTS[0] if n == 0 else SHIFTS[PARTNER + n - 1]))
        for n, array in enumerate(outgoing)
    ]
    parts = ()
    for first, last in zip(PARTS[:-1], PARTS[1:]):
        parts = attend(
            first,
            last,
            parts,
            where,
            queries,
            keys,
            values,
            (other_keys, other_values),
            arrived,
        )
    out = merge(plan, me_ref, queries, parts[1], parts[0], pieces, forwarded)
    return lax.cond(
        plan[ROW_LEFT, 0] > 0,
        lambda: full_attention(queries, keys, values, chosen_all, me),
        lambda: out,
    )


def solution(mesh):
    placed = (P("ctx", None), P("ctx", None), P("ctx", None), P("ctx", None, None))
    return jax.shard_map(
        body, mesh=mesh, in_specs=placed, out_specs=P("ctx", None), check_vma=False
    )
```

```python
import math

import jax
import jax.numpy as jnp
from jax import lax
from jax.experimental import pallas as pl
from jax.experimental.pallas import tpu as pltpu
from jax.sharding import PartitionSpec as P

HEAD = 128
HEADS = 16
BLOCK = 512
DEVICES = 128
CHIPS = 64
SCALE = math.log2(math.e) / math.sqrt(HEAD)

ONE = [(1, 0, 0), (3, 0, 0), (0, 1, 0), (0, 3, 0), (0, 0, 1), (0, 0, 3)]
PARTNER = 6
SHIFTS = [(0, 0, 0, 1)] * PARTNER
SHIFTS += [(*s, c) for s in ONE for c in (0, 1)]
KINDS = len(SHIFTS)
SPARE = 5
PIECE = 16
WAVES = 4
WAVE_OF = [1] * (PARTNER + 4) + [2] * 4 + [3] * 4
CODE_PARTNER = CHIPS
CODE_FORWARD = CODE_PARTNER + 1
CODE_SPARE = CODE_FORWARD + KINDS
LIST = 3 * HEADS
COUNT = LIST + WAVES * HEADS
NEED = COUNT + WAVES
TABLE = NEED + 2 * HEADS
HALF = BLOCK // PIECE
SLOT_PIECES = 2 * HALF + SPARE
SLOT_ROWS = SLOT_PIECES * PIECE

ROW_DIRECT = CHIPS
ROW_SPARE = ROW_DIRECT + CHIPS
ROW_FORWARD = ROW_SPARE + CHIPS
ROW_FORWARD_HEAD = ROW_FORWARD + KINDS
ROW_FROM_HEAD = ROW_FORWARD_HEAD + KINDS
ROW_FROM = ROW_FROM_HEAD + SPARE
ROW_FROM_RANK = ROW_FROM + SPARE
ROW_PARTNER = ROW_FROM_RANK + SPARE
ROW_LEFT = ROW_PARTNER + 1
ROWS = -(-(ROW_LEFT + 1) // 8) * 8


def through(device, shift):
    z, x, y, c = device // 32, device // 8 % 4, device // 2 % 4, device % 2
    dz, dx, dy, dc = shift
    return (((z + dz) % 4 * 4 + (x + dx) % 4) * 4 + (y + dy) % 4) * 2 + (c ^ dc)


def shift_pairs(shift):
    return [(through(b, shift), b) for b in range(DEVICES)]


def roll_lanes(array, amount):
    amount = amount % DEVICES
    return pltpu.roll(array, amount, 1) if amount else array


def permuted(array, shift, lane, inverse=False):
    dz, dx, dy, dc = shift
    if inverse:
        dz, dx, dy = -dz % 4, -dx % 4, -dy % 4
    if dz:
        array = roll_lanes(array, -32 * dz)
    if dx:
        inside = (lane // 8) % 4 + dx < 4
        array = jnp.where(inside, roll_lanes(array, -8 * dx), roll_lanes(array, 32 - 8 * dx))
    if dy:
        inside = (lane // 2) % 4 + dy < 4
        array = jnp.where(inside, roll_lanes(array, -2 * dy), roll_lanes(array, 8 - 2 * dy))
    if dc:
        array = jnp.where(lane % 2 == 0, roll_lanes(array, -1), roll_lanes(array, 1))
    return array


def plan_kernel(chosen_ref, out_ref):
    chip = lax.broadcasted_iota(jnp.int32, (CHIPS, DEVICES), 0)
    lane = lax.broadcasted_iota(jnp.int32, (CHIPS, DEVICES), 1)
    even = jnp.zeros((CHIPS, DEVICES), jnp.int32)
    odd = jnp.zeros((CHIPS, DEVICES), jnp.int32)
    for entry in range(3 * HEADS):
        owner = chosen_ref[entry : entry + 1, :]
        even = even + jnp.where(owner == 2 * chip, entry // 3 + 1, 0)
        odd = odd + jnp.where(owner == 2 * chip + 1, entry // 3 + 1, 0)
    home = lane // 2 == chip
    partner = jnp.sum(jnp.where(home, even + odd, 0), axis=0, keepdims=True)
    even = jnp.where(home, 0, even)
    odd = jnp.where(home, 0, odd)
    waiting = jnp.where(even > 0, odd, 0)
    slot = jnp.where(even > 0, even - 1, jnp.where(odd > 0, odd + 15, 0))
    direct = jnp.where(even > 0, even, odd)
    free = jnp.where(home, 0, jnp.where(direct > 0, 0, 1))
    options = jnp.zeros((CHIPS, DEVICES), jnp.int32)
    for shift in sorted(set(SHIFTS)):
        options = options + permuted(free, shift, lane)
    score = options * 64 + (chip + 17 * lane) % 64
    big = 1 << 20
    out_ref[...] = jnp.zeros((ROWS, DEVICES), jnp.int32)
    for kind, shift in enumerate(SHIFTS):
        able = (waiting > 0) & (permuted(free, shift, lane) > 0)
        rated = jnp.where(able, score, big)
        best = jnp.min(rated, axis=0, keepdims=True)
        picked = able & (rated == best)
        head = jnp.sum(jnp.where(picked, waiting, 0), axis=0, keepdims=True)
        back = permuted(jnp.where(picked, waiting + 16, 0), shift, lane, inverse=True)
        waiting = jnp.where(picked, 0, waiting)
        slot = jnp.where(back > 0, back - 1, slot)
        free = jnp.where(back > 0, 0, free)
        forward = jnp.sum(jnp.where(back > 0, chip, 0), axis=0, keepdims=True)
        out_ref[ROW_FORWARD + kind : ROW_FORWARD + kind + 1, :] = forward
        out_ref[ROW_FORWARD_HEAD + kind : ROW_FORWARD_HEAD + kind + 1, :] = head
    before = lax.broadcasted_iota(jnp.int32, (DEVICES, DEVICES), 0)
    after = lax.broadcasted_iota(jnp.int32, (DEVICES, DEVICES), 1)
    earlier = jnp.where((before < after) & (before % 2 == after % 2), 1.0, 0.0)
    rank = jnp.dot(
        jnp.where(waiting > 0, 1.0, 0.0), earlier, preferred_element_type=jnp.float32
    ).astype(jnp.int32)
    spare = jnp.zeros((CHIPS, DEVICES), jnp.int32)
    for index in range(SPARE):
        for core in range(2):
            chosen = (rank == index) & (lane % 2 == core)
            head = jnp.sum(jnp.where(chosen, waiting, 0), axis=1, keepdims=True)
            spare = jnp.where(lane == 2 * index + core, head, spare)
    out_ref[ROW_SPARE : ROW_SPARE + CHIPS, :] = spare
    excess = jnp.where((waiting > 0) & (rank >= SPARE), 1, 0)
    for index in range(SPARE):
        best = jnp.min(jnp.where(waiting > 0, chip, big), axis=0, keepdims=True)
        picked = (waiting > 0) & (chip == best)
        out_ref[ROW_FROM + index : ROW_FROM + index + 1, :] = jnp.where(best < big, best, 0)
        out_ref[ROW_FROM_RANK + index : ROW_FROM_RANK + index + 1, :] = jnp.minimum(
            jnp.sum(jnp.where(picked, rank, 0), axis=0, keepdims=True), SPARE - 1
        )
        out_ref[ROW_FROM_HEAD + index : ROW_FROM_HEAD + index + 1, :] = jnp.sum(
            jnp.where(picked, waiting, 0), axis=0, keepdims=True
        )
        waiting = jnp.where(picked, 0, waiting)
    excess = excess + waiting
    out_ref[ROW_PARTNER : ROW_PARTNER + 1, :] = partner
    left = jnp.max(jnp.max(excess, axis=0, keepdims=True), axis=1, keepdims=True)
    out_ref[ROW_LEFT : ROW_LEFT + 1, :] = jnp.broadcast_to(left, (1, DEVICES))
    out_ref[0:CHIPS, :] = slot
    out_ref[ROW_DIRECT : ROW_DIRECT + CHIPS, :] = direct


def make_plan(chosen_all):
    return pl.pallas_call(
        plan_kernel,
        out_shape=jax.ShapeDtypeStruct((ROWS, DEVICES), jnp.int32),
        name="plan",
    )(chosen_all)


def columns(head):
    return pl.ds(pl.multiple_of(head * HEAD, HEAD), HEAD)


def make_table(plan, me, table):
    for entry in range(TABLE):
        table[entry] = 0

    def note(head_plus, code, wave):
        @pl.when(head_plus > 0)
        def _():
            head = head_plus - 1
            at = table[NEED + HEADS + head]
            table[head * 3 + jnp.minimum(at, 2)] = code
            table[NEED + HEADS + head] = at + 1
            table[NEED + head] = jnp.maximum(table[NEED + head], wave)

    def direct(chip, carry):
        note(plan[ROW_DIRECT + chip, me], chip, 0)
        return carry

    lax.fori_loop(0, CHIPS, direct, 0)
    note(plan[ROW_PARTNER, me], CODE_PARTNER, 0)
    for kind in range(KINDS):
        note(plan[ROW_FORWARD_HEAD + kind, me], CODE_FORWARD + kind, WAVE_OF[kind])
    for index in range(SPARE):
        note(plan[ROW_FROM_HEAD + index, me], CODE_SPARE + index, WAVES - 1)
    for head in range(HEADS):
        wave = table[NEED + head]
        at = table[COUNT + wave]
        table[LIST + wave * HEADS + at] = head
        table[COUNT + wave] = at + 1


def pack_kernel(plan, me_ref, keys, values, other_keys, other_values, send, table, sem):
    me = me_ref[0]
    chip, core = me // 2, me % 2

    def one_slot(dest, carry):
        code = plan[chip, 2 * dest + core]

        def copy(*sources):
            for half, source in enumerate(sources):
                pltpu.make_async_copy(
                    source.at[:, :, columns(code % 16)],
                    send.at[dest // 2, dest % 2, pl.ds(half * HALF, HALF)],
                    sem,
                ).start()

        @pl.when(code // 16 == core)
        def _():
            copy(keys, values)

        @pl.when(code // 16 != core)
        def _():
            copy(other_keys, other_values)

        return carry

    lax.fori_loop(0, CHIPS, one_slot, 0)

    def one_spare(index, carry):
        head = jnp.maximum(plan[ROW_SPARE + chip, 2 * index + core] - 1, 0)

        def copy(*sources):
            for half, source in enumerate(sources):
                pltpu.make_async_copy(
                    source.at[:, :, columns(head)], send.at[:, half, 2 * HALF + index], sem
                ).start()

        @pl.when(core == 1)
        def _():
            copy(keys, values)

        @pl.when(core == 0)
        def _():
            copy(other_keys, other_values)

        return carry

    lax.fori_loop(0, SPARE, one_spare, 0)
    make_table(plan, me, table)
    pltpu.make_async_copy(send, send, sem).wait()


ANY = pl.BlockSpec(memory_space=pl.ANY)
SMEM = pl.BlockSpec(memory_space=pltpu.SMEM)
VMEM = pl.BlockSpec(memory_space=pltpu.VMEM)
BIG = pltpu.CompilerParams(vmem_limit_bytes=60 * 1024 * 1024)


def tiles(count):
    return jax.ShapeDtypeStruct((count, 2 * HALF, PIECE, HEAD), jnp.bfloat16)


def in_pieces(array):
    return array.reshape(HALF, PIECE, -1)


def pack(plan, me, keys, values, other_keys, other_values):
    return pl.pallas_call(
        pack_kernel,
        in_specs=[SMEM, SMEM, VMEM, VMEM, VMEM, VMEM],
        out_specs=[ANY, SMEM],
        out_shape=[
            jax.ShapeDtypeStruct((HALF, 2, SLOT_PIECES, PIECE, HEAD), jnp.bfloat16),
            jax.ShapeDtypeStruct((TABLE,), jnp.int32),
        ],
        scratch_shapes=[pltpu.SemaphoreType.DMA],
        compiler_params=BIG,
        name="pack",
    )(plan, me, *map(in_pieces, (keys, values, other_keys, other_values)))


def forward_kernel(plan, me_ref, arrived, *rest):
    outs, (moving, spare, gathered, sems, out_sems) = rest[:-5], rest[-5:]
    me = me_ref[0]
    core = me % 2
    loads, stores = [], []
    for kind in range(KINDS):
        out = outs[1].at[kind] if kind < PARTNER else outs[kind - PARTNER + 2].at[0]
        source = arrived.at[plan[ROW_FORWARD + kind, me], pl.ds(0, 2 * HALF)]
        loads.append(pltpu.make_async_copy(source, moving.at[kind], sems.at[kind]))
        stores.append(pltpu.make_async_copy(moving.at[kind], out, out_sems.at[kind]))
    for load in loads:
        load.start()

    load_spare = pltpu.make_async_copy(
        arrived.at[:, pl.ds(2 * HALF, SPARE)], spare, sems.at[KINDS]
    )
    load_spare.start()

    for load, store in zip(loads, stores):
        load.wait()
        store.start()
    load_spare.wait()

    def one_dest(dest, carry):
        for index in range(SPARE):
            chip = plan[ROW_FROM + index, 2 * dest + core]
            rank = plan[ROW_FROM_RANK + index, 2 * dest + core]
            gathered[dest, index] = spare[chip, rank]
        return carry

    lax.fori_loop(0, CHIPS, one_dest, 0)
    last = pltpu.make_async_copy(gathered, outs[0], out_sems.at[KINDS])
    last.start()
    for store in stores:
        store.wait()
    last.wait()


def forward(plan, me, arrived):
    return pl.pallas_call(
        forward_kernel,
        in_specs=[SMEM, SMEM, ANY],
        out_specs=[ANY] * (KINDS - PARTNER + 2),
        out_shape=[jax.ShapeDtypeStruct((CHIPS, SPARE, PIECE, HEAD), jnp.bfloat16)]
        + [tiles(PARTNER)]
        + [tiles(1)] * (KINDS - PARTNER),
        scratch_shapes=[
            pltpu.VMEM((KINDS, 2 * HALF, PIECE, HEAD), jnp.bfloat16),
            pltpu.VMEM((CHIPS, SPARE, PIECE, HEAD), jnp.bfloat16),
            pltpu.VMEM((CHIPS, SPARE, PIECE, HEAD), jnp.bfloat16),
            pltpu.SemaphoreType.DMA((KINDS + 1,)),
            pltpu.SemaphoreType.DMA((KINDS + 1,)),
        ],
        compiler_params=BIG,
        name="forward",
    )(plan, me, arrived)


ROWS_AT_ONCE = 256


def scores_of(query, key):
    return lax.dot_general(
        query, key, (((1,), (1,)), ((), ())), preferred_element_type=jnp.float32
    )


ROWS_AT_ONCE = 256


def attend_kernel(wave, kinds, table, queries, keys, values, *rest):
    other_keys, other_values, arrived = rest[:3]
    forwarded = dict(zip(kinds, rest[3 : 3 + len(kinds)]))
    pieces = rest[3 + len(kinds)] if wave == WAVES - 1 else None
    out, query_buf, key_buf, value_buf, out_buf, sems, out_sems = rest[-7:]
    count = table[COUNT + wave]

    def head_at(index):
        return table[LIST + wave * HEADS + index]

    def load(index, slot):
        head = head_at(index)

        def start(j, source_key, source_value):
            into_value = value_buf.at[slot, j, :, :, pl.ds(0, HEAD)]
            pltpu.make_async_copy(source_key, key_buf.at[slot, j], sems.at[slot, 2 * j]).start()
            pltpu.make_async_copy(source_value, into_value, sems.at[slot, 2 * j + 1]).start()

        cut = columns(head)
        pltpu.make_async_copy(queries.at[:, :, cut], query_buf.at[slot], sems.at[slot, 8]).start()
        start(3, keys.at[:, :, cut], values.at[:, :, cut])
        for j in range(3):
            code = table[head * 3 + j]

            @pl.when(code < CHIPS)
            def _():
                start(j, arrived.at[code, pl.ds(0, HALF)], arrived.at[code, pl.ds(HALF, HALF)])

            @pl.when(code >= CHIPS)
            def _():
                @pl.when(code == CODE_PARTNER)
                def _():
                    start(j, other_keys.at[:, :, cut], other_values.at[:, :, cut])

                for kind, ref in forwarded.items():
                    last = kind + (PARTNER if kind == 0 else 1)

                    @pl.when((code >= CODE_FORWARD + kind) & (code < CODE_FORWARD + last))
                    def _():
                        tile = ref.at[code - CODE_FORWARD - kind]
                        start(j, tile.at[pl.ds(0, HALF)], tile.at[pl.ds(HALF, HALF)])

                if pieces is not None:

                    @pl.when(code >= CODE_SPARE)
                    def _():
                        start(j, pieces.at[:, 0, code - CODE_SPARE], pieces.at[:, 1, code - CODE_SPARE])

    def store(index, slot):
        return pltpu.make_async_copy(
            out_buf.at[slot], out.at[:, :, columns(head_at(index))], out_sems.at[slot]
        )

    @pl.when(count > 0)
    def _():
        load(0, 0)
        ones = jnp.ones((HALF, PIECE, HEAD), jnp.bfloat16)
        for slot in range(2):
            for j in range(4):
                value_buf[slot, j, :, :, HEAD:] = ones

    def one_head(index, carry):
        slot = index % 2

        @pl.when(index + 1 < count)
        def _():
            load(index + 1, 1 - slot)

        for j in range(4):
            into_value = value_buf.at[slot, j, :, :, pl.ds(0, HEAD)]
            tile = arrived.at[0, pl.ds(0, HALF)]
            pltpu.make_async_copy(tile, key_buf.at[slot, j], sems.at[slot, 2 * j]).wait()
            pltpu.make_async_copy(tile, into_value, sems.at[slot, 2 * j + 1]).wait()
        pltpu.make_async_copy(tile, query_buf.at[slot], sems.at[slot, 8]).wait()

        @pl.when(index >= 2)
        def _():
            store(index - 2, slot).wait()

        query = query_buf[slot].reshape(BLOCK, HEAD)
        for start in range(0, BLOCK, ROWS_AT_ONCE):
            stop = start + ROWS_AT_ONCE
            q = query[start:stop, :]
            total = highest = None
            for j in (3, 0, 1, 2):
                seen = stop if j == 3 else BLOCK
                scores = scores_of(q, key_buf[slot, j, 0 : seen // PIECE].reshape(seen, HEAD))
                if j == 3:
                    row_iota = lax.broadcasted_iota(jnp.int32, scores.shape, 0) + start
                    col_iota = lax.broadcasted_iota(jnp.int32, scores.shape, 1)
                    scores = jnp.where(col_iota <= row_iota, scores, -jnp.inf)
                top = jnp.max(scores, axis=1, keepdims=True)
                if highest is not None:
                    top = jnp.maximum(highest, top)
                weight = jnp.exp2((scores - top) * SCALE).astype(jnp.bfloat16)
                value = value_buf[slot, j, 0 : seen // PIECE].reshape(seen, 2 * HEAD)
                added = jnp.dot(weight, value, preferred_element_type=jnp.float32)
                if highest is None:
                    total = added
                else:
                    total = total * jnp.exp2((highest - top) * SCALE) + added
                highest = top
            result = (total[:, :HEAD] / total[:, HEAD:]).astype(jnp.bfloat16)
            span = slice(start // PIECE, stop // PIECE)
            out_buf[slot, span] = result.reshape(ROWS_AT_ONCE // PIECE, PIECE, HEAD)
        store(index, slot).start()
        return carry

    lax.fori_loop(0, count, one_head, 0)

    @pl.when(count >= 2)
    def _():
        store(count - 2, count % 2).wait()

    @pl.when(count >= 1)
    def _():
        store(count - 1, (count - 1) % 2).wait()


HEADS_EXPECTED = (9, 4, 2, 2)


def attend(wave, before, table, queries, keys, values, others, arrived, forwarded, pieces):
    kinds = [kind for kind in forwarded if WAVE_OF[kind] <= wave]
    operands = [table, *map(in_pieces, (queries, keys, values, *others)), arrived]
    operands += [forwarded[kind] for kind in kinds]
    if wave == WAVES - 1:
        operands.append(pieces.reshape(HALF, 2, SPARE, PIECE, HEAD))
    if before is not None:
        operands.append(before)
    size = HEADS_EXPECTED[wave] * BLOCK * 4 * BLOCK * HEAD
    return pl.pallas_call(
        lambda *refs: attend_kernel(wave, kinds, *refs),
        in_specs=[SMEM] + [ANY] * (len(operands) - 1),
        out_specs=ANY,
        out_shape=jax.ShapeDtypeStruct((HALF, PIECE, HEADS * HEAD), jnp.bfloat16),
        input_output_aliases={} if before is None else {len(operands) - 1: 0},
        scratch_shapes=[
            pltpu.VMEM((2, HALF, PIECE, HEAD), jnp.bfloat16),
            pltpu.VMEM((2, 4, HALF, PIECE, HEAD), jnp.bfloat16),
            pltpu.VMEM((2, 4, HALF, PIECE, 2 * HEAD), jnp.bfloat16),
            pltpu.VMEM((2, HALF, PIECE, HEAD), jnp.bfloat16),
            pltpu.SemaphoreType.DMA((2, 9)),
            pltpu.SemaphoreType.DMA((2,)),
        ],
        cost_estimate=pl.CostEstimate(
            flops=16 * size, bytes_accessed=3 * 2**20, transcendentals=size // HEAD
        ),
        compiler_params=BIG,
        name="attend",
    )(*operands)


LANES = [[2 * chip + core for chip in range(CHIPS)] for core in range(2)]
SWAP = [(device, device ^ 1) for device in range(DEVICES)]


def exchange(array):
    return lax.all_to_all(array, "ctx", 0, 0, axis_index_groups=LANES, tiled=True)


def full_attention(queries, keys, values, chosen_all, me):
    heads = jnp.arange(3 * HEADS, dtype=jnp.int32) // 3
    mine = lax.dynamic_index_in_dim(chosen_all, me, 0, keepdims=False)
    wants = chosen_all == me
    which = jnp.max(jnp.where(wants, heads[None, :], 0), axis=1)
    key_heads = keys.reshape(BLOCK, HEADS, HEAD).transpose(1, 0, 2)
    value_heads = values.reshape(BLOCK, HEADS, HEAD).transpose(1, 0, 2)
    got_key = lax.all_to_all(jnp.take(key_heads, which, axis=0), "ctx", 0, 0, tiled=True)
    got_value = lax.all_to_all(jnp.take(value_heads, which, axis=0), "ctx", 0, 0, tiled=True)
    q_heads = queries.reshape(BLOCK, HEADS, HEAD).transpose(1, 0, 2)
    allowed = jnp.arange(4 * BLOCK)[None, :] >= BLOCK
    allowed = allowed | (jnp.arange(4 * BLOCK)[None, :] <= jnp.arange(BLOCK)[:, None])

    def one_head(head):
        picks = lax.dynamic_slice(mine, (3 * head,), (3,))
        k = jnp.concatenate([key_heads[head], got_key[picks].reshape(3 * BLOCK, HEAD)], axis=0)
        v = jnp.concatenate([value_heads[head], got_value[picks].reshape(3 * BLOCK, HEAD)], axis=0)
        s = jnp.where(allowed, scores_of(q_heads[head], k), -jnp.inf)
        weight = jnp.exp2((s - jnp.max(s, axis=1, keepdims=True)) * SCALE)
        total = jnp.sum(weight, axis=1, keepdims=True)
        o = jnp.dot(weight.astype(jnp.bfloat16), v, preferred_element_type=jnp.float32)
        return (o / total).astype(jnp.bfloat16)

    out = lax.map(one_head, jnp.arange(HEADS))
    return out.transpose(1, 0, 2).reshape(BLOCK, HEADS * HEAD)


def body(queries, keys, values, chosen):
    me = lax.axis_index("ctx").astype(jnp.int32)
    me_ref = me.reshape(1)
    other_keys = lax.ppermute(keys, "ctx", SWAP)
    other_values = lax.ppermute(values, "ctx", SWAP)
    spread = jnp.broadcast_to(chosen.reshape(1, 3 * HEADS), (DEVICES, 3 * HEADS))
    chosen_all = lax.all_to_all(spread, "ctx", 0, 0, tiled=True)
    plan = make_plan(chosen_all.T)
    send, table = pack(plan, me_ref, keys, values, other_keys, other_values)
    sent = exchange(send.reshape(CHIPS, SLOT_ROWS, HEAD))
    held = (sent, plan, table, queries, keys, values, other_keys, other_values, me_ref)
    held = lax.optimization_barrier(held)
    arrived, plan, table, queries, keys, values, other_keys, other_values, me_ref = held
    arrived = arrived.reshape(CHIPS, SLOT_PIECES, PIECE, HEAD)
    pieces, *outgoing = forward(plan, me_ref, arrived)
    outgoing = dict(zip([0, *range(PARTNER, KINDS)], outgoing))
    forwarded = {}
    out = None
    for wave in range(WAVES):
        if wave:
            for kind in [kind for kind in outgoing if WAVE_OF[kind] == wave]:
                forwarded[kind] = lax.ppermute(outgoing[kind], "ctx", shift_pairs(SHIFTS[kind]))
        if wave == 1:
            pieces, out = lax.optimization_barrier((pieces, out))
            pieces = exchange(pieces)
        out = attend(
            wave,
            out,
            table,
            queries,
            keys,
            values,
            (other_keys, other_values),
            arrived,
            forwarded,
            pieces,
        )
    out = out.reshape(BLOCK, HEADS * HEAD)
    return lax.cond(
        plan[ROW_LEFT, 0] > 0,
        lambda: full_attention(queries, keys, values, chosen_all, me),
        lambda: out,
    )


def solution(mesh):
    placed = (P("ctx", None), P("ctx", None), P("ctx", None), P("ctx", None, None))
    return jax.shard_map(
        body, mesh=mesh, in_specs=placed, out_specs=P("ctx", None), check_vma=False
    )
```

```python
import math

import jax
import jax.numpy as jnp
from jax import lax
from jax.experimental import pallas as pl
from jax.experimental.pallas import tpu as pltpu
from jax.sharding import PartitionSpec as P

HEAD = 128
HEADS = 16
BLOCK = 512
DEVICES = 128
CHIPS = 64
SCALE = math.log2(math.e) / math.sqrt(HEAD)

ONE = [(1, 0, 0), (3, 0, 0), (0, 1, 0), (0, 3, 0), (0, 0, 1), (0, 0, 3)]
PARTNER = 6
SHIFTS = [(0, 0, 0, 1)] * PARTNER
SHIFTS += [(*s, c) for s in ONE for c in (0, 1)]
KINDS = len(SHIFTS)
SPARE = 5
PIECE = 16
WAVES = 4
WAVE_OF = [1] * (PARTNER + 4) + [2] * 4 + [3] * 4
CODE_PARTNER = CHIPS
CODE_FORWARD = CODE_PARTNER + 1
CODE_SPARE = CODE_FORWARD + KINDS
LIST = 3 * HEADS
COUNT = LIST + WAVES * HEADS
NEED = COUNT + WAVES
TABLE = NEED + 2 * HEADS
HALF = BLOCK // PIECE
SLOT_PIECES = 2 * HALF + SPARE
SLOT_ROWS = SLOT_PIECES * PIECE

ROW_DIRECT = CHIPS
ROW_SPARE = ROW_DIRECT + CHIPS
ROW_FORWARD = ROW_SPARE + CHIPS
ROW_FORWARD_HEAD = ROW_FORWARD + KINDS
ROW_FROM_HEAD = ROW_FORWARD_HEAD + KINDS
ROW_FROM = ROW_FROM_HEAD + SPARE
ROW_FROM_RANK = ROW_FROM + SPARE
ROW_PARTNER = ROW_FROM_RANK + SPARE
ROW_LEFT = ROW_PARTNER + 1
ROWS = -(-(ROW_LEFT + 1) // 8) * 8


def place(chip):
    return chip % 4 * 16 + chip // 4 % 4 * 4 + chip // 16


def through(device, shift):
    z, x, y, c = device // 32, device // 8 % 4, device // 2 % 4, device % 2
    dz, dx, dy, dc = shift
    return (((z + dz) % 4 * 4 + (x + dx) % 4) * 4 + (y + dy) % 4) * 2 + (c ^ dc)


def shift_pairs(shift):
    return [(through(b, shift), b) for b in range(DEVICES)]


def roll_lanes(array, amount):
    amount = amount % DEVICES
    return pltpu.roll(array, amount, 1) if amount else array


def permuted(array, shift, lane, inverse=False):
    dz, dx, dy, dc = shift
    if inverse:
        dz, dx, dy = -dz % 4, -dx % 4, -dy % 4
    if dz:
        array = roll_lanes(array, -32 * dz)
    if dx:
        inside = (lane // 8) % 4 + dx < 4
        array = jnp.where(inside, roll_lanes(array, -8 * dx), roll_lanes(array, 32 - 8 * dx))
    if dy:
        inside = (lane // 2) % 4 + dy < 4
        array = jnp.where(inside, roll_lanes(array, -2 * dy), roll_lanes(array, 8 - 2 * dy))
    if dc:
        array = jnp.where(lane % 2 == 0, roll_lanes(array, -1), roll_lanes(array, 1))
    return array


def plan_kernel(chosen_ref, out_ref):
    chip = lax.broadcasted_iota(jnp.int32, (CHIPS, DEVICES), 0)
    lane = lax.broadcasted_iota(jnp.int32, (CHIPS, DEVICES), 1)
    even = jnp.zeros((CHIPS, DEVICES), jnp.int32)
    odd = jnp.zeros((CHIPS, DEVICES), jnp.int32)
    for entry in range(3 * HEADS):
        owner = chosen_ref[entry : entry + 1, :]
        even = even + jnp.where(owner == 2 * chip, entry // 3 + 1, 0)
        odd = odd + jnp.where(owner == 2 * chip + 1, entry // 3 + 1, 0)
    home = lane // 2 == chip
    partner = jnp.sum(jnp.where(home, even + odd, 0), axis=0, keepdims=True)
    even = jnp.where(home, 0, even)
    odd = jnp.where(home, 0, odd)
    waiting = jnp.where(even > 0, odd, 0)
    slot = jnp.where(even > 0, even - 1, jnp.where(odd > 0, odd + 15, 0))
    direct = jnp.where(even > 0, even, odd)
    free = jnp.where(home, 0, jnp.where(direct > 0, 0, 1))
    options = jnp.zeros((CHIPS, DEVICES), jnp.int32)
    for shift in sorted(set(SHIFTS)):
        options = options + permuted(free, shift, lane)
    score = options * 64 + (chip + 17 * lane) % 64
    big = 1 << 20
    out_ref[...] = jnp.zeros((ROWS, DEVICES), jnp.int32)
    for kind, shift in enumerate(SHIFTS):
        able = (waiting > 0) & (permuted(free, shift, lane) > 0)
        rated = jnp.where(able, score, big)
        best = jnp.min(rated, axis=0, keepdims=True)
        picked = able & (rated == best)
        head = jnp.sum(jnp.where(picked, waiting, 0), axis=0, keepdims=True)
        back = permuted(jnp.where(picked, waiting + 16, 0), shift, lane, inverse=True)
        waiting = jnp.where(picked, 0, waiting)
        slot = jnp.where(back > 0, back - 1, slot)
        free = jnp.where(back > 0, 0, free)
        forward = jnp.sum(jnp.where(back > 0, chip, 0), axis=0, keepdims=True)
        out_ref[ROW_FORWARD + kind : ROW_FORWARD + kind + 1, :] = forward
        out_ref[ROW_FORWARD_HEAD + kind : ROW_FORWARD_HEAD + kind + 1, :] = head
    before = lax.broadcasted_iota(jnp.int32, (DEVICES, DEVICES), 0)
    after = lax.broadcasted_iota(jnp.int32, (DEVICES, DEVICES), 1)
    earlier = jnp.where((before < after) & (before % 2 == after % 2), 1.0, 0.0)
    rank = jnp.dot(
        jnp.where(waiting > 0, 1.0, 0.0), earlier, preferred_element_type=jnp.float32
    ).astype(jnp.int32)
    spare = jnp.zeros((CHIPS, DEVICES), jnp.int32)
    for index in range(SPARE):
        for core in range(2):
            chosen = (rank == index) & (lane % 2 == core)
            head = jnp.sum(jnp.where(chosen, waiting, 0), axis=1, keepdims=True)
            spare = jnp.where(lane == 2 * index + core, head, spare)
    out_ref[ROW_SPARE : ROW_SPARE + CHIPS, :] = spare
    excess = jnp.where((waiting > 0) & (rank >= SPARE), 1, 0)
    for index in range(SPARE):
        best = jnp.min(jnp.where(waiting > 0, chip, big), axis=0, keepdims=True)
        picked = (waiting > 0) & (chip == best)
        out_ref[ROW_FROM + index : ROW_FROM + index + 1, :] = jnp.where(best < big, best, 0)
        out_ref[ROW_FROM_RANK + index : ROW_FROM_RANK + index + 1, :] = jnp.minimum(
            jnp.sum(jnp.where(picked, rank, 0), axis=0, keepdims=True), SPARE - 1
        )
        out_ref[ROW_FROM_HEAD + index : ROW_FROM_HEAD + index + 1, :] = jnp.sum(
            jnp.where(picked, waiting, 0), axis=0, keepdims=True
        )
        waiting = jnp.where(picked, 0, waiting)
    excess = excess + waiting
    out_ref[ROW_PARTNER : ROW_PARTNER + 1, :] = partner
    left = jnp.max(jnp.max(excess, axis=0, keepdims=True), axis=1, keepdims=True)
    out_ref[ROW_LEFT : ROW_LEFT + 1, :] = jnp.broadcast_to(left, (1, DEVICES))
    out_ref[0:CHIPS, :] = slot
    out_ref[ROW_DIRECT : ROW_DIRECT + CHIPS, :] = direct


def make_plan(chosen_all):
    return pl.pallas_call(
        plan_kernel,
        out_shape=jax.ShapeDtypeStruct((ROWS, DEVICES), jnp.int32),
        name="plan",
    )(chosen_all)


def columns(head):
    return pl.ds(pl.multiple_of(head * HEAD, HEAD), HEAD)


def make_table(plan, me, table):
    for entry in range(TABLE):
        table[entry] = 0

    def note(head_plus, code, wave):
        @pl.when(head_plus > 0)
        def _():
            head = head_plus - 1
            at = table[NEED + HEADS + head]
            table[head * 3 + jnp.minimum(at, 2)] = code
            table[NEED + HEADS + head] = at + 1
            table[NEED + head] = jnp.maximum(table[NEED + head], wave)

    def direct(chip, carry):
        note(plan[ROW_DIRECT + chip, me], place(chip), 0)
        return carry

    lax.fori_loop(0, CHIPS, direct, 0)
    note(plan[ROW_PARTNER, me], CODE_PARTNER, 0)
    for kind in range(KINDS):
        note(plan[ROW_FORWARD_HEAD + kind, me], CODE_FORWARD + kind, WAVE_OF[kind])
    for index in range(SPARE):
        note(plan[ROW_FROM_HEAD + index, me], CODE_SPARE + index, WAVES - 1)
    for head in range(HEADS):
        wave = table[NEED + head]
        at = table[COUNT + wave]
        table[LIST + wave * HEADS + at] = head
        table[COUNT + wave] = at + 1


def pack_kernel(plan, me_ref, keys, values, other_keys, other_values, send, table, sem):
    me = me_ref[0]
    chip, core = me // 2, me % 2

    def one_slot(dest, carry):
        code = plan[chip, 2 * dest + core]
        at = place(dest)

        def copy(*sources):
            for half, source in enumerate(sources):
                pltpu.make_async_copy(
                    source.at[:, :, columns(code % 16)],
                    send.at[at // 2, at % 2, pl.ds(half * HALF, HALF)],
                    sem,
                ).start()

        @pl.when(code // 16 == core)
        def _():
            copy(keys, values)

        @pl.when(code // 16 != core)
        def _():
            copy(other_keys, other_values)

        return carry

    lax.fori_loop(0, CHIPS, one_slot, 0)

    def one_spare(index, carry):
        head = jnp.maximum(plan[ROW_SPARE + chip, 2 * index + core] - 1, 0)

        def copy(*sources):
            for half, source in enumerate(sources):
                pltpu.make_async_copy(
                    source.at[:, :, columns(head)], send.at[:, half, 2 * HALF + index], sem
                ).start()

        @pl.when(core == 1)
        def _():
            copy(keys, values)

        @pl.when(core == 0)
        def _():
            copy(other_keys, other_values)

        return carry

    lax.fori_loop(0, SPARE, one_spare, 0)
    make_table(plan, me, table)
    pltpu.make_async_copy(send, send, sem).wait()


ANY = pl.BlockSpec(memory_space=pl.ANY)
SMEM = pl.BlockSpec(memory_space=pltpu.SMEM)
VMEM = pl.BlockSpec(memory_space=pltpu.VMEM)
BIG = pltpu.CompilerParams(vmem_limit_bytes=60 * 1024 * 1024)


def tiles(count):
    return jax.ShapeDtypeStruct((count, 2 * HALF, PIECE, HEAD), jnp.bfloat16)


def in_pieces(array):
    return array.reshape(HALF, PIECE, -1)


def pack(plan, me, keys, values, other_keys, other_values):
    return pl.pallas_call(
        pack_kernel,
        in_specs=[SMEM, SMEM, VMEM, VMEM, VMEM, VMEM],
        out_specs=[ANY, SMEM],
        out_shape=[
            jax.ShapeDtypeStruct((HALF, 2, SLOT_PIECES, PIECE, HEAD), jnp.bfloat16),
            jax.ShapeDtypeStruct((TABLE,), jnp.int32),
        ],
        scratch_shapes=[pltpu.SemaphoreType.DMA],
        compiler_params=BIG,
        name="pack",
    )(plan, me, *map(in_pieces, (keys, values, other_keys, other_values)))


def forward_kernel(plan, me_ref, arrived, *rest):
    outs, (moving, spare, gathered, sems, out_sems) = rest[:-5], rest[-5:]
    me = me_ref[0]
    core = me % 2
    loads, stores = [], []
    for kind in range(KINDS):
        out = outs[1].at[kind] if kind < PARTNER else outs[kind - PARTNER + 2].at[0]
        source = arrived.at[place(plan[ROW_FORWARD + kind, me]), pl.ds(0, 2 * HALF)]
        loads.append(pltpu.make_async_copy(source, moving.at[kind], sems.at[kind]))
        stores.append(pltpu.make_async_copy(moving.at[kind], out, out_sems.at[kind]))
    for load in loads:
        load.start()

    load_spare = pltpu.make_async_copy(
        arrived.at[:, pl.ds(2 * HALF, SPARE)], spare, sems.at[KINDS]
    )
    load_spare.start()

    for load, store in zip(loads, stores):
        load.wait()
        store.start()
    load_spare.wait()

    def one_dest(dest, carry):
        for index in range(SPARE):
            chip = plan[ROW_FROM + index, 2 * dest + core]
            rank = plan[ROW_FROM_RANK + index, 2 * dest + core]
            gathered[place(dest), index] = spare[place(chip), rank]
        return carry

    lax.fori_loop(0, CHIPS, one_dest, 0)
    last = pltpu.make_async_copy(gathered, outs[0], out_sems.at[KINDS])
    last.start()
    for store in stores:
        store.wait()
    last.wait()


def forward(plan, me, arrived):
    return pl.pallas_call(
        forward_kernel,
        in_specs=[SMEM, SMEM, ANY],
        out_specs=[ANY] * (KINDS - PARTNER + 2),
        out_shape=[jax.ShapeDtypeStruct((CHIPS, SPARE, PIECE, HEAD), jnp.bfloat16)]
        + [tiles(PARTNER)]
        + [tiles(1)] * (KINDS - PARTNER),
        scratch_shapes=[
            pltpu.VMEM((KINDS, 2 * HALF, PIECE, HEAD), jnp.bfloat16),
            pltpu.VMEM((CHIPS, SPARE, PIECE, HEAD), jnp.bfloat16),
            pltpu.VMEM((CHIPS, SPARE, PIECE, HEAD), jnp.bfloat16),
            pltpu.SemaphoreType.DMA((KINDS + 1,)),
            pltpu.SemaphoreType.DMA((KINDS + 1,)),
        ],
        compiler_params=BIG,
        name="forward",
    )(plan, me, arrived)


ROWS_AT_ONCE = 256


def scores_of(query, key):
    return lax.dot_general(
        query, key, (((1,), (1,)), ((), ())), preferred_element_type=jnp.float32
    )


ROWS_AT_ONCE = 256


def attend_kernel(wave, kinds, table, queries, keys, values, *rest):
    other_keys, other_values, arrived = rest[:3]
    forwarded = dict(zip(kinds, rest[3 : 3 + len(kinds)]))
    pieces = rest[3 + len(kinds)] if wave == WAVES - 1 else None
    out, query_buf, key_buf, value_buf, out_buf, sems, out_sems = rest[-7:]
    count = table[COUNT + wave]

    def head_at(index):
        return table[LIST + wave * HEADS + index]

    def load(index, slot):
        head = head_at(index)

        def start(j, source_key, source_value):
            into_value = value_buf.at[slot, j, :, :, pl.ds(0, HEAD)]
            pltpu.make_async_copy(source_key, key_buf.at[slot, j], sems.at[slot, 2 * j]).start()
            pltpu.make_async_copy(source_value, into_value, sems.at[slot, 2 * j + 1]).start()

        cut = columns(head)
        pltpu.make_async_copy(queries.at[:, :, cut], query_buf.at[slot], sems.at[slot, 8]).start()
        start(3, keys.at[:, :, cut], values.at[:, :, cut])
        for j in range(3):
            code = table[head * 3 + j]

            @pl.when(code < CHIPS)
            def _():
                start(j, arrived.at[code, pl.ds(0, HALF)], arrived.at[code, pl.ds(HALF, HALF)])

            @pl.when(code >= CHIPS)
            def _():
                @pl.when(code == CODE_PARTNER)
                def _():
                    start(j, other_keys.at[:, :, cut], other_values.at[:, :, cut])

                for kind, ref in forwarded.items():
                    last = kind + (PARTNER if kind == 0 else 1)

                    @pl.when((code >= CODE_FORWARD + kind) & (code < CODE_FORWARD + last))
                    def _():
                        tile = ref.at[code - CODE_FORWARD - kind]
                        start(j, tile.at[pl.ds(0, HALF)], tile.at[pl.ds(HALF, HALF)])

                if pieces is not None:

                    @pl.when(code >= CODE_SPARE)
                    def _():
                        start(j, pieces.at[:, 0, code - CODE_SPARE], pieces.at[:, 1, code - CODE_SPARE])

    def store(index, slot):
        return pltpu.make_async_copy(
            out_buf.at[slot], out.at[:, :, columns(head_at(index))], out_sems.at[slot]
        )

    @pl.when(count > 0)
    def _():
        load(0, 0)
        ones = jnp.ones((HALF, PIECE, HEAD), jnp.bfloat16)
        for slot in range(2):
            for j in range(4):
                value_buf[slot, j, :, :, HEAD:] = ones

    def one_head(index, carry):
        slot = index % 2

        @pl.when(index + 1 < count)
        def _():
            load(index + 1, 1 - slot)

        for j in range(4):
            into_value = value_buf.at[slot, j, :, :, pl.ds(0, HEAD)]
            tile = arrived.at[0, pl.ds(0, HALF)]
            pltpu.make_async_copy(tile, key_buf.at[slot, j], sems.at[slot, 2 * j]).wait()
            pltpu.make_async_copy(tile, into_value, sems.at[slot, 2 * j + 1]).wait()
        pltpu.make_async_copy(tile, query_buf.at[slot], sems.at[slot, 8]).wait()

        @pl.when(index >= 2)
        def _():
            store(index - 2, slot).wait()

        query = query_buf[slot].reshape(BLOCK, HEAD)
        for start in range(0, BLOCK, ROWS_AT_ONCE):
            stop = start + ROWS_AT_ONCE
            q = query[start:stop, :]
            total = highest = None
            for j in (3, 0, 1, 2):
                seen = stop if j == 3 else BLOCK
                scores = scores_of(q, key_buf[slot, j, 0 : seen // PIECE].reshape(seen, HEAD))
                if j == 3:
                    row_iota = lax.broadcasted_iota(jnp.int32, scores.shape, 0) + start
                    col_iota = lax.broadcasted_iota(jnp.int32, scores.shape, 1)
                    scores = jnp.where(col_iota <= row_iota, scores, -jnp.inf)
                top = jnp.max(scores, axis=1, keepdims=True)
                if highest is not None:
                    top = jnp.maximum(highest, top)
                weight = jnp.exp2((scores - top) * SCALE).astype(jnp.bfloat16)
                value = value_buf[slot, j, 0 : seen // PIECE].reshape(seen, 2 * HEAD)
                added = jnp.dot(weight, value, preferred_element_type=jnp.float32)
                if highest is None:
                    total = added
                else:
                    total = total * jnp.exp2((highest - top) * SCALE) + added
                highest = top
            result = (total[:, :HEAD] / total[:, HEAD:]).astype(jnp.bfloat16)
            span = slice(start // PIECE, stop // PIECE)
            out_buf[slot, span] = result.reshape(ROWS_AT_ONCE // PIECE, PIECE, HEAD)
        store(index, slot).start()
        return carry

    lax.fori_loop(0, count, one_head, 0)

    @pl.when(count >= 2)
    def _():
        store(count - 2, count % 2).wait()

    @pl.when(count >= 1)
    def _():
        store(count - 1, (count - 1) % 2).wait()


HEADS_EXPECTED = (9, 4, 2, 2)


def attend(wave, before, table, queries, keys, values, others, arrived, forwarded, pieces):
    kinds = [kind for kind in forwarded if WAVE_OF[kind] <= wave]
    operands = [table, *map(in_pieces, (queries, keys, values, *others)), arrived]
    operands += [forwarded[kind] for kind in kinds]
    if wave == WAVES - 1:
        operands.append(pieces.reshape(HALF, 2, SPARE, PIECE, HEAD))
    if before is not None:
        operands.append(before)
    size = HEADS_EXPECTED[wave] * BLOCK * 4 * BLOCK * HEAD
    return pl.pallas_call(
        lambda *refs: attend_kernel(wave, kinds, *refs),
        in_specs=[SMEM] + [ANY] * (len(operands) - 1),
        out_specs=ANY,
        out_shape=jax.ShapeDtypeStruct((HALF, PIECE, HEADS * HEAD), jnp.bfloat16),
        input_output_aliases={} if before is None else {len(operands) - 1: 0},
        scratch_shapes=[
            pltpu.VMEM((2, HALF, PIECE, HEAD), jnp.bfloat16),
            pltpu.VMEM((2, 4, HALF, PIECE, HEAD), jnp.bfloat16),
            pltpu.VMEM((2, 4, HALF, PIECE, 2 * HEAD), jnp.bfloat16),
            pltpu.VMEM((2, HALF, PIECE, HEAD), jnp.bfloat16),
            pltpu.SemaphoreType.DMA((2, 9)),
            pltpu.SemaphoreType.DMA((2,)),
        ],
        cost_estimate=pl.CostEstimate(
            flops=16 * size, bytes_accessed=3 * 2**20, transcendentals=size // HEAD
        ),
        compiler_params=BIG,
        name="attend",
    )(*operands)


LANES = [[2 * place(at) + core for at in range(CHIPS)] for core in range(2)]
SWAP = [(device, device ^ 1) for device in range(DEVICES)]


def exchange(array):
    return lax.all_to_all(array, "ctx", 0, 0, axis_index_groups=LANES, tiled=True)


def full_attention(queries, keys, values, chosen_all, me):
    heads = jnp.arange(3 * HEADS, dtype=jnp.int32) // 3
    mine = lax.dynamic_index_in_dim(chosen_all, me, 0, keepdims=False)
    wants = chosen_all == me
    which = jnp.max(jnp.where(wants, heads[None, :], 0), axis=1)
    key_heads = keys.reshape(BLOCK, HEADS, HEAD).transpose(1, 0, 2)
    value_heads = values.reshape(BLOCK, HEADS, HEAD).transpose(1, 0, 2)
    got_key = lax.all_to_all(jnp.take(key_heads, which, axis=0), "ctx", 0, 0, tiled=True)
    got_value = lax.all_to_all(jnp.take(value_heads, which, axis=0), "ctx", 0, 0, tiled=True)
    q_heads = queries.reshape(BLOCK, HEADS, HEAD).transpose(1, 0, 2)
    allowed = jnp.arange(4 * BLOCK)[None, :] >= BLOCK
    allowed = allowed | (jnp.arange(4 * BLOCK)[None, :] <= jnp.arange(BLOCK)[:, None])

    def one_head(head):
        picks = lax.dynamic_slice(mine, (3 * head,), (3,))
        k = jnp.concatenate([key_heads[head], got_key[picks].reshape(3 * BLOCK, HEAD)], axis=0)
        v = jnp.concatenate([value_heads[head], got_value[picks].reshape(3 * BLOCK, HEAD)], axis=0)
        s = jnp.where(allowed, scores_of(q_heads[head], k), -jnp.inf)
        weight = jnp.exp2((s - jnp.max(s, axis=1, keepdims=True)) * SCALE)
        total = jnp.sum(weight, axis=1, keepdims=True)
        o = jnp.dot(weight.astype(jnp.bfloat16), v, preferred_element_type=jnp.float32)
        return (o / total).astype(jnp.bfloat16)

    out = lax.map(one_head, jnp.arange(HEADS))
    return out.transpose(1, 0, 2).reshape(BLOCK, HEADS * HEAD)


def body(queries, keys, values, chosen):
    me = lax.axis_index("ctx").astype(jnp.int32)
    me_ref = me.reshape(1)
    other_keys = lax.ppermute(keys, "ctx", SWAP)
    other_values = lax.ppermute(values, "ctx", SWAP)
    spread = jnp.broadcast_to(chosen.reshape(1, 3 * HEADS), (DEVICES, 3 * HEADS))
    chosen_all = lax.all_to_all(spread, "ctx", 0, 0, tiled=True)
    plan = make_plan(chosen_all.T)
    send, table = pack(plan, me_ref, keys, values, other_keys, other_values)
    sent = exchange(send.reshape(CHIPS, SLOT_ROWS, HEAD))
    held = (sent, plan, table, queries, keys, values, other_keys, other_values, me_ref)
    held = lax.optimization_barrier(held)
    arrived, plan, table, queries, keys, values, other_keys, other_values, me_ref = held
    arrived = arrived.reshape(CHIPS, SLOT_PIECES, PIECE, HEAD)
    pieces, *outgoing = forward(plan, me_ref, arrived)
    pieces = exchange(pieces)
    outgoing = dict(zip([0, *range(PARTNER, KINDS)], outgoing))
    forwarded = {}
    out = None
    for wave in range(WAVES):
        if wave:
            for kind in [kind for kind in outgoing if WAVE_OF[kind] == wave]:
                forwarded[kind] = lax.ppermute(outgoing[kind], "ctx", shift_pairs(SHIFTS[kind]))
        out = attend(
            wave,
            out,
            table,
            queries,
            keys,
            values,
            (other_keys, other_values),
            arrived,
            forwarded,
            pieces,
        )
    out = out.reshape(BLOCK, HEADS * HEAD)
    return lax.cond(
        plan[ROW_LEFT, 0] > 0,
        lambda: full_attention(queries, keys, values, chosen_all, me),
        lambda: out,
    )


def solution(mesh):
    placed = (P("ctx", None), P("ctx", None), P("ctx", None), P("ctx", None, None))
    return jax.shard_map(
        body, mesh=mesh, in_specs=placed, out_specs=P("ctx", None), check_vma=False
    )
```

```python
import math

import jax
import jax.numpy as jnp
from jax import lax
from jax.experimental import pallas as pl
from jax.experimental.pallas import tpu as pltpu
from jax.sharding import PartitionSpec as P

HEAD = 128
HEADS = 16
BLOCK = 512
DEVICES = 128
CHIPS = 64
SCALE = math.log2(math.e) / math.sqrt(HEAD)

ONE = [(1, 0, 0), (3, 0, 0), (0, 1, 0), (0, 3, 0), (0, 0, 1), (0, 0, 3)]
PARTNER = 6
SHIFTS = [(0, 0, 0, 1)] * PARTNER
SHIFTS += [(*s, c) for s in ONE for c in (0, 1)]
KINDS = len(SHIFTS)
SPARE = 5
PIECE = 16
WAVES = 4
WAVE_OF = [1] * (PARTNER + 4) + [2] * 4 + [3] * 4
CODE_PARTNER = CHIPS
CODE_FORWARD = CODE_PARTNER + 1
CODE_SPARE = CODE_FORWARD + KINDS
LIST = 3 * HEADS
COUNT = LIST + WAVES * HEADS
NEED = COUNT + WAVES
TABLE = NEED + 2 * HEADS
HALF = BLOCK // PIECE
SLOT_PIECES = 2 * HALF + SPARE
SLOT_ROWS = SLOT_PIECES * PIECE

ROW_DIRECT = CHIPS
ROW_SPARE = ROW_DIRECT + CHIPS
ROW_FORWARD = ROW_SPARE + CHIPS
ROW_FORWARD_HEAD = ROW_FORWARD + KINDS
ROW_FROM_HEAD = ROW_FORWARD_HEAD + KINDS
ROW_FROM = ROW_FROM_HEAD + SPARE
ROW_FROM_RANK = ROW_FROM + SPARE
ROW_PARTNER = ROW_FROM_RANK + SPARE
ROW_LEFT = ROW_PARTNER + 1
ROWS = -(-(ROW_LEFT + 1) // 8) * 8


def place(chip):
    return ((chip & 3) << 4) | (chip & 12) | (chip >> 4)


def through(device, shift):
    z, x, y, c = device // 32, device // 8 % 4, device // 2 % 4, device % 2
    dz, dx, dy, dc = shift
    return (((z + dz) % 4 * 4 + (x + dx) % 4) * 4 + (y + dy) % 4) * 2 + (c ^ dc)


def shift_pairs(shift):
    return [(through(b, shift), b) for b in range(DEVICES)]


def roll_lanes(array, amount):
    amount = amount % DEVICES
    return pltpu.roll(array, amount, 1) if amount else array


def permuted(array, shift, lane, inverse=False):
    dz, dx, dy, dc = shift
    if inverse:
        dz, dx, dy = -dz % 4, -dx % 4, -dy % 4
    if dz:
        array = roll_lanes(array, -32 * dz)
    if dx:
        inside = (lane // 8) % 4 + dx < 4
        array = jnp.where(inside, roll_lanes(array, -8 * dx), roll_lanes(array, 32 - 8 * dx))
    if dy:
        inside = (lane // 2) % 4 + dy < 4
        array = jnp.where(inside, roll_lanes(array, -2 * dy), roll_lanes(array, 8 - 2 * dy))
    if dc:
        array = jnp.where(lane % 2 == 0, roll_lanes(array, -1), roll_lanes(array, 1))
    return array


def make_plan(chosen_ref, out_ref):
    chip = lax.broadcasted_iota(jnp.int32, (CHIPS, DEVICES), 0)
    lane = lax.broadcasted_iota(jnp.int32, (CHIPS, DEVICES), 1)
    even = jnp.zeros((CHIPS, DEVICES), jnp.int32)
    odd = jnp.zeros((CHIPS, DEVICES), jnp.int32)
    for entry in range(3 * HEADS):
        owner = chosen_ref[entry : entry + 1, :]
        even = even + jnp.where(owner == 2 * chip, entry // 3 + 1, 0)
        odd = odd + jnp.where(owner == 2 * chip + 1, entry // 3 + 1, 0)
    home = lane // 2 == chip
    partner = jnp.sum(jnp.where(home, even + odd, 0), axis=0, keepdims=True)
    even = jnp.where(home, 0, even)
    odd = jnp.where(home, 0, odd)
    waiting = jnp.where(even > 0, odd, 0)
    slot = jnp.where(even > 0, even - 1, jnp.where(odd > 0, odd + 15, -1))
    direct = jnp.where(even > 0, even, odd)
    free = jnp.where(home, 0, jnp.where(direct > 0, 0, 1))
    options = jnp.zeros((CHIPS, DEVICES), jnp.int32)
    for shift in sorted(set(SHIFTS)):
        options = options + permuted(free, shift, lane)
    score = options * 64 + (chip + 17 * lane) % 64
    big = 1 << 20
    out_ref[...] = jnp.zeros((ROWS, DEVICES), jnp.int32)
    for kind, shift in enumerate(SHIFTS):
        able = (waiting > 0) & (permuted(free, shift, lane) > 0)
        rated = jnp.where(able, score, big)
        best = jnp.min(rated, axis=0, keepdims=True)
        picked = able & (rated == best)
        head = jnp.sum(jnp.where(picked, waiting, 0), axis=0, keepdims=True)
        back = permuted(jnp.where(picked, waiting + 16, 0), shift, lane, inverse=True)
        waiting = jnp.where(picked, 0, waiting)
        slot = jnp.where(back > 0, back - 1, slot)
        free = jnp.where(back > 0, 0, free)
        forward = jnp.sum(jnp.where(back > 0, chip + 1, 0), axis=0, keepdims=True)
        out_ref[ROW_FORWARD + kind : ROW_FORWARD + kind + 1, :] = forward
        out_ref[ROW_FORWARD_HEAD + kind : ROW_FORWARD_HEAD + kind + 1, :] = head
    before = lax.broadcasted_iota(jnp.int32, (DEVICES, DEVICES), 0)
    after = lax.broadcasted_iota(jnp.int32, (DEVICES, DEVICES), 1)
    earlier = jnp.where((before < after) & (before % 2 == after % 2), 1.0, 0.0)
    rank = jnp.dot(
        jnp.where(waiting > 0, 1.0, 0.0), earlier, preferred_element_type=jnp.float32
    ).astype(jnp.int32)
    spare = jnp.zeros((CHIPS, DEVICES), jnp.int32)
    for index in range(SPARE):
        for core in range(2):
            chosen = (rank == index) & (lane % 2 == core)
            head = jnp.sum(jnp.where(chosen, waiting, 0), axis=1, keepdims=True)
            spare = jnp.where(lane == 2 * index + core, head, spare)
    out_ref[ROW_SPARE : ROW_SPARE + CHIPS, :] = spare
    excess = jnp.where((waiting > 0) & (rank >= SPARE), 1, 0)
    for index in range(SPARE):
        best = jnp.min(jnp.where(waiting > 0, chip, big), axis=0, keepdims=True)
        picked = (waiting > 0) & (chip == best)
        out_ref[ROW_FROM + index : ROW_FROM + index + 1, :] = jnp.where(best < big, best, 0)
        out_ref[ROW_FROM_RANK + index : ROW_FROM_RANK + index + 1, :] = jnp.minimum(
            jnp.sum(jnp.where(picked, rank, 0), axis=0, keepdims=True), SPARE - 1
        )
        out_ref[ROW_FROM_HEAD + index : ROW_FROM_HEAD + index + 1, :] = jnp.sum(
            jnp.where(picked, waiting, 0), axis=0, keepdims=True
        )
        waiting = jnp.where(picked, 0, waiting)
    excess = excess + waiting
    out_ref[ROW_PARTNER : ROW_PARTNER + 1, :] = partner
    left = jnp.max(jnp.max(excess, axis=0, keepdims=True), axis=1, keepdims=True)
    out_ref[ROW_LEFT : ROW_LEFT + 1, :] = jnp.broadcast_to(left, (1, DEVICES))
    out_ref[0:CHIPS, :] = slot
    out_ref[ROW_DIRECT : ROW_DIRECT + CHIPS, :] = direct


def columns(head):
    return pl.ds(pl.multiple_of(head * HEAD, HEAD), HEAD)


def make_table(plan, me, table):
    for entry in range(TABLE):
        table[entry] = 0

    def note(head_plus, code, wave):
        @pl.when(head_plus > 0)
        def _():
            head = head_plus - 1
            at = table[NEED + HEADS + head]
            table[head * 3 + jnp.minimum(at, 2)] = code
            table[NEED + HEADS + head] = at + 1
            table[NEED + head] = jnp.maximum(table[NEED + head], wave)

    def direct(chip, carry):
        note(plan[ROW_DIRECT + chip, me], place(chip), 0)
        return carry

    lax.fori_loop(0, CHIPS, direct, 0)
    note(plan[ROW_PARTNER, me], CODE_PARTNER, 0)
    for kind in range(KINDS):
        note(plan[ROW_FORWARD_HEAD + kind, me], CODE_FORWARD + kind, WAVE_OF[kind])
    for index in range(SPARE):
        note(plan[ROW_FROM_HEAD + index, me], CODE_SPARE + index, WAVES - 1)
    for head in range(HEADS):
        wave = table[NEED + head]
        at = table[COUNT + wave]
        table[LIST + wave * HEADS + at] = head
        table[COUNT + wave] = at + 1


def pack_kernel(chosen, me_ref, keys_in, values_in, other_keys_in, other_values_in, *rest):
    plan_out, send, table, plan, keys, values, other_keys, other_values, sem, sems = rest
    loads = []
    pairs = zip(
        (keys_in, values_in, other_keys_in, other_values_in),
        (keys, values, other_keys, other_values),
    )
    for n, (source, into) in enumerate(pairs):
        loads.append(pltpu.make_async_copy(source, into, sems.at[n]))
        loads[-1].start()
    make_plan(chosen, plan_out)
    to_scalars = pltpu.make_async_copy(plan_out, plan, sems.at[4])
    to_scalars.start()
    to_scalars.wait()
    me = me_ref[0]
    chip, core = me >> 1, me & 1
    for load in loads:
        load.wait()

    def one_slot(dest, carry):
        code = plan[chip, 2 * dest + core]
        at = place(dest)
        cut = columns(jnp.maximum(code, 0) & 15)

        def copy(*sources):
            for half, source in enumerate(sources):
                pltpu.make_async_copy(
                    source.at[:, :, cut],
                    send.at[at >> 1, at & 1, pl.ds(half * HALF, HALF)],
                    sem,
                ).start()

        @pl.when(code >> 4 == core)
        def _():
            copy(keys, values)

        @pl.when(code >> 4 == 1 - core)
        def _():
            copy(other_keys, other_values)

        return carry + jnp.where(code >= 0, 2, 0)

    def one_spare(index, started):
        head = plan[ROW_SPARE + chip, 2 * index + core] - 1
        cut = columns(jnp.maximum(head, 0))

        def copy(*sources):
            for half, source in enumerate(sources):
                pltpu.make_async_copy(
                    source.at[:, :, cut], send.at[:, half, 2 * HALF + index], sem
                ).start()

        @pl.when((head >= 0) & (core == 1))
        def _():
            copy(keys, values)

        @pl.when((head >= 0) & (core == 0))
        def _():
            copy(other_keys, other_values)

        return started + jnp.where(head >= 0, 2, 0)

    started = lax.fori_loop(0, CHIPS, one_slot, 0)
    started = lax.fori_loop(0, SPARE, one_spare, started)
    make_table(plan, me, table)

    def wait_one(index, carry):
        pltpu.make_async_copy(
            keys.at[:, :, pl.ds(0, HEAD)], send.at[0, 0, pl.ds(0, HALF)], sem
        ).wait()
        return carry

    lax.fori_loop(0, started, wait_one, 0)


ANY = pl.BlockSpec(memory_space=pl.ANY)
SMEM = pl.BlockSpec(memory_space=pltpu.SMEM)
VMEM = pl.BlockSpec(memory_space=pltpu.VMEM)
BIG = pltpu.CompilerParams(vmem_limit_bytes=60 * 1024 * 1024)


def tiles(count):
    return jax.ShapeDtypeStruct((count, 2 * HALF, PIECE, HEAD), jnp.bfloat16)


def in_pieces(array):
    return array.reshape(HALF, PIECE, -1)


def pack(chosen_all, me, keys, values, other_keys, other_values):
    whole = pltpu.VMEM((HALF, PIECE, HEADS * HEAD), jnp.bfloat16)
    return pl.pallas_call(
        pack_kernel,
        in_specs=[VMEM, SMEM, ANY, ANY, ANY, ANY],
        out_specs=[VMEM, ANY, SMEM],
        out_shape=[
            jax.ShapeDtypeStruct((ROWS, DEVICES), jnp.int32),
            jax.ShapeDtypeStruct((HALF, 2, SLOT_PIECES, PIECE, HEAD), jnp.bfloat16),
            jax.ShapeDtypeStruct((TABLE,), jnp.int32),
        ],
        scratch_shapes=[pltpu.SMEM((ROWS, DEVICES), jnp.int32)]
        + [whole] * 4
        + [pltpu.SemaphoreType.DMA, pltpu.SemaphoreType.DMA((5,))],
        compiler_params=BIG,
        name="pack",
    )(chosen_all, me, *map(in_pieces, (keys, values, other_keys, other_values)))


def forward_kernel(plan, me_ref, arrived, *rest):
    outs, (moving, spare, gathered, sems, out_sems) = rest[:-5], rest[-5:]
    me = me_ref[0]
    core = me & 1
    load_spare = pltpu.make_async_copy(
        arrived.at[:, pl.ds(2 * HALF, SPARE)], spare, sems.at[KINDS]
    )
    load_spare.start()
    steps = []
    for kind in range(KINDS):
        out = outs[1].at[kind] if kind < PARTNER else outs[kind - PARTNER + 2].at[0]
        chip = plan[ROW_FORWARD + kind, me] - 1
        source = arrived.at[place(jnp.maximum(chip, 0)), pl.ds(0, 2 * HALF)]
        load = pltpu.make_async_copy(source, moving.at[kind], sems.at[kind])
        store = pltpu.make_async_copy(moving.at[kind], out, out_sems.at[kind])
        steps.append((chip >= 0, load, store))
    for used, load, _ in steps:

        @pl.when(used)
        def _():
            load.start()

    load_spare.wait()

    def one_dest(dest, carry):
        device = 2 * dest + core

        def move(index):
            @pl.when(plan[ROW_FROM_HEAD + index, device] > 0)
            def _():
                chip = plan[ROW_FROM + index, device]
                rank = plan[ROW_FROM_RANK + index, device]
                gathered[place(dest), index] = spare[place(chip), rank]
                if index + 1 < SPARE:
                    move(index + 1)

        move(0)
        return carry

    lax.fori_loop(0, CHIPS, one_dest, 0)
    last = pltpu.make_async_copy(gathered, outs[0], out_sems.at[KINDS])
    last.start()
    for used, load, store in steps:

        @pl.when(used)
        def _():
            load.wait()
            store.start()

    for used, _, store in steps:

        @pl.when(used)
        def _():
            store.wait()

    last.wait()


def forward(plan, me, arrived):
    return pl.pallas_call(
        forward_kernel,
        in_specs=[SMEM, SMEM, ANY],
        out_specs=[ANY] * (KINDS - PARTNER + 2),
        out_shape=[jax.ShapeDtypeStruct((CHIPS, SPARE, PIECE, HEAD), jnp.bfloat16)]
        + [tiles(PARTNER)]
        + [tiles(1)] * (KINDS - PARTNER),
        scratch_shapes=[
            pltpu.VMEM((KINDS, 2 * HALF, PIECE, HEAD), jnp.bfloat16),
            pltpu.VMEM((CHIPS, SPARE, PIECE, HEAD), jnp.bfloat16),
            pltpu.VMEM((CHIPS, SPARE, PIECE, HEAD), jnp.bfloat16),
            pltpu.SemaphoreType.DMA((KINDS + 1,)),
            pltpu.SemaphoreType.DMA((KINDS + 1,)),
        ],
        compiler_params=BIG,
        name="forward",
    )(plan, me, arrived)


ROWS_AT_ONCE = 256


def scores_of(query, key):
    return lax.dot_general(
        query, key, (((1,), (1,)), ((), ())), preferred_element_type=jnp.float32
    )


def attend_kernel(wave, kinds, table, queries, keys, values, *rest):
    other_keys, other_values, arrived = rest[:3]
    forwarded = dict(zip(kinds, rest[3 : 3 + len(kinds)]))
    pieces = rest[3 + len(kinds)] if wave == WAVES - 1 else None
    out, query_buf, key_buf, value_buf, out_buf, sems, out_sems = rest[-7:]
    count = table[COUNT + wave]

    def head_at(index):
        return table[LIST + wave * HEADS + index]

    def load(index, slot):
        head = head_at(index)

        def start(j, source_key, source_value):
            into_value = value_buf.at[slot, j, :, :, pl.ds(0, HEAD)]
            pltpu.make_async_copy(source_key, key_buf.at[slot, j], sems.at[slot, 2 * j]).start()
            pltpu.make_async_copy(source_value, into_value, sems.at[slot, 2 * j + 1]).start()

        cut = columns(head)
        pltpu.make_async_copy(queries.at[:, :, cut], query_buf.at[slot], sems.at[slot, 8]).start()
        start(3, keys.at[:, :, cut], values.at[:, :, cut])
        for j in range(3):
            code = table[head * 3 + j]

            @pl.when(code < CHIPS)
            def _():
                start(j, arrived.at[code, pl.ds(0, HALF)], arrived.at[code, pl.ds(HALF, HALF)])

            @pl.when(code >= CHIPS)
            def _():
                @pl.when(code == CODE_PARTNER)
                def _():
                    start(j, other_keys.at[:, :, cut], other_values.at[:, :, cut])

                for kind, ref in forwarded.items():
                    last = kind + (PARTNER if kind == 0 else 1)

                    @pl.when((code >= CODE_FORWARD + kind) & (code < CODE_FORWARD + last))
                    def _():
                        tile = ref.at[code - CODE_FORWARD - kind]
                        start(j, tile.at[pl.ds(0, HALF)], tile.at[pl.ds(HALF, HALF)])

                if pieces is not None:

                    @pl.when(code >= CODE_SPARE)
                    def _():
                        start(j, pieces.at[:, 0, code - CODE_SPARE], pieces.at[:, 1, code - CODE_SPARE])

    def store(index, slot):
        return pltpu.make_async_copy(
            out_buf.at[slot], out.at[:, :, columns(head_at(index))], out_sems.at[slot]
        )

    @pl.when(count > 0)
    def _():
        load(0, 0)
        ones = jnp.ones((HALF, PIECE, HEAD), jnp.bfloat16)
        for slot in range(2):
            for j in range(4):
                value_buf[slot, j, :, :, HEAD:] = ones

    def one_head(index, carry):
        slot = index % 2

        @pl.when(index + 1 < count)
        def _():
            load(index + 1, 1 - slot)

        for j in range(4):
            into_value = value_buf.at[slot, j, :, :, pl.ds(0, HEAD)]
            tile = arrived.at[0, pl.ds(0, HALF)]
            pltpu.make_async_copy(tile, key_buf.at[slot, j], sems.at[slot, 2 * j]).wait()
            pltpu.make_async_copy(tile, into_value, sems.at[slot, 2 * j + 1]).wait()
        pltpu.make_async_copy(tile, query_buf.at[slot], sems.at[slot, 8]).wait()

        @pl.when(index >= 2)
        def _():
            store(index - 2, slot).wait()

        query = query_buf[slot].reshape(BLOCK, HEAD)
        for start in range(0, BLOCK, ROWS_AT_ONCE):
            stop = start + ROWS_AT_ONCE
            q = query[start:stop, :]
            total = highest = None
            for j in (3, 0, 1, 2):
                seen = stop if j == 3 else BLOCK
                scores = scores_of(q, key_buf[slot, j, 0 : seen // PIECE].reshape(seen, HEAD))
                if j == 3:
                    row_iota = lax.broadcasted_iota(jnp.int32, scores.shape, 0) + start
                    col_iota = lax.broadcasted_iota(jnp.int32, scores.shape, 1)
                    scores = jnp.where(col_iota <= row_iota, scores, -jnp.inf)
                top = jnp.max(scores, axis=1, keepdims=True)
                if highest is not None:
                    top = jnp.maximum(highest, top)
                weight = jnp.exp2((scores - top) * SCALE).astype(jnp.bfloat16)
                value = value_buf[slot, j, 0 : seen // PIECE].reshape(seen, 2 * HEAD)
                added = jnp.dot(weight, value, preferred_element_type=jnp.float32)
                if highest is None:
                    total = added
                else:
                    total = total * jnp.exp2((highest - top) * SCALE) + added
                highest = top
            result = (total[:, :HEAD] / total[:, HEAD:]).astype(jnp.bfloat16)
            span = slice(start // PIECE, stop // PIECE)
            out_buf[slot, span] = result.reshape(ROWS_AT_ONCE // PIECE, PIECE, HEAD)
        store(index, slot).start()
        return carry

    lax.fori_loop(0, count, one_head, 0)

    @pl.when(count >= 2)
    def _():
        store(count - 2, count % 2).wait()

    @pl.when(count >= 1)
    def _():
        store(count - 1, (count - 1) % 2).wait()


HEADS_EXPECTED = (9, 4, 2, 2)


def attend(wave, before, table, queries, keys, values, others, arrived, forwarded, pieces):
    kinds = [kind for kind in forwarded if WAVE_OF[kind] <= wave]
    operands = [table, *map(in_pieces, (queries, keys, values, *others)), arrived]
    operands += [forwarded[kind] for kind in kinds]
    if wave == WAVES - 1:
        operands.append(pieces.reshape(HALF, 2, SPARE, PIECE, HEAD))
    if before is not None:
        operands.append(before)
    size = HEADS_EXPECTED[wave] * BLOCK * 4 * BLOCK * HEAD
    return pl.pallas_call(
        lambda *refs: attend_kernel(wave, kinds, *refs),
        in_specs=[SMEM] + [ANY] * (len(operands) - 1),
        out_specs=ANY,
        out_shape=jax.ShapeDtypeStruct((HALF, PIECE, HEADS * HEAD), jnp.bfloat16),
        input_output_aliases={} if before is None else {len(operands) - 1: 0},
        scratch_shapes=[
            pltpu.VMEM((2, HALF, PIECE, HEAD), jnp.bfloat16),
            pltpu.VMEM((2, 4, HALF, PIECE, HEAD), jnp.bfloat16),
            pltpu.VMEM((2, 4, HALF, PIECE, 2 * HEAD), jnp.bfloat16),
            pltpu.VMEM((2, HALF, PIECE, HEAD), jnp.bfloat16),
            pltpu.SemaphoreType.DMA((2, 9)),
            pltpu.SemaphoreType.DMA((2,)),
        ],
        cost_estimate=pl.CostEstimate(
            flops=16 * size, bytes_accessed=3 * 2**20, transcendentals=size // HEAD
        ),
        compiler_params=BIG,
        name="attend",
    )(*operands)


LANES = [[2 * place(at) + core for at in range(CHIPS)] for core in range(2)]
SWAP = [(device, device ^ 1) for device in range(DEVICES)]


def exchange(array):
    return lax.all_to_all(array, "ctx", 0, 0, axis_index_groups=LANES, tiled=True)


def full_attention(queries, keys, values, chosen_all, me):
    heads = jnp.arange(3 * HEADS, dtype=jnp.int32) // 3
    mine = lax.dynamic_index_in_dim(chosen_all, me, 0, keepdims=False)
    wants = chosen_all == me
    which = jnp.max(jnp.where(wants, heads[None, :], 0), axis=1)
    key_heads = keys.reshape(BLOCK, HEADS, HEAD).transpose(1, 0, 2)
    value_heads = values.reshape(BLOCK, HEADS, HEAD).transpose(1, 0, 2)
    got_key = lax.all_to_all(jnp.take(key_heads, which, axis=0), "ctx", 0, 0, tiled=True)
    got_value = lax.all_to_all(jnp.take(value_heads, which, axis=0), "ctx", 0, 0, tiled=True)
    q_heads = queries.reshape(BLOCK, HEADS, HEAD).transpose(1, 0, 2)
    allowed = jnp.arange(4 * BLOCK)[None, :] >= BLOCK
    allowed = allowed | (jnp.arange(4 * BLOCK)[None, :] <= jnp.arange(BLOCK)[:, None])

    def one_head(head):
        picks = lax.dynamic_slice(mine, (3 * head,), (3,))
        k = jnp.concatenate([key_heads[head], got_key[picks].reshape(3 * BLOCK, HEAD)], axis=0)
        v = jnp.concatenate([value_heads[head], got_value[picks].reshape(3 * BLOCK, HEAD)], axis=0)
        s = jnp.where(allowed, scores_of(q_heads[head], k), -jnp.inf)
        weight = jnp.exp2((s - jnp.max(s, axis=1, keepdims=True)) * SCALE)
        total = jnp.sum(weight, axis=1, keepdims=True)
        o = jnp.dot(weight.astype(jnp.bfloat16), v, preferred_element_type=jnp.float32)
        return (o / total).astype(jnp.bfloat16)

    out = lax.map(one_head, jnp.arange(HEADS))
    return out.transpose(1, 0, 2).reshape(BLOCK, HEADS * HEAD)


def body(queries, keys, values, chosen):
    me = lax.axis_index("ctx").astype(jnp.int32)
    me_ref = me.reshape(1)
    other_keys = lax.ppermute(keys, "ctx", SWAP)
    other_values = lax.ppermute(values, "ctx", SWAP)
    spread = jnp.broadcast_to(chosen.reshape(1, 3 * HEADS), (DEVICES, 3 * HEADS))
    chosen_all = lax.all_to_all(spread, "ctx", 0, 0, tiled=True)
    plan, send, table = pack(chosen_all.T, me_ref, keys, values, other_keys, other_values)
    sent = exchange(send.reshape(CHIPS, SLOT_ROWS, HEAD))
    held = (sent, plan, table, queries, keys, values, other_keys, other_values, me_ref)
    held = lax.optimization_barrier(held)
    arrived, plan, table, queries, keys, values, other_keys, other_values, me_ref = held
    arrived = arrived.reshape(CHIPS, SLOT_PIECES, PIECE, HEAD)
    pieces, *outgoing = forward(plan, me_ref, arrived)
    pieces = exchange(pieces)
    outgoing = dict(zip([0, *range(PARTNER, KINDS)], outgoing))
    forwarded = {}
    out = None
    for wave in range(WAVES):
        if wave:
            for kind in [kind for kind in outgoing if WAVE_OF[kind] == wave]:
                forwarded[kind] = lax.ppermute(outgoing[kind], "ctx", shift_pairs(SHIFTS[kind]))
        out = attend(
            wave,
            out,
            table,
            queries,
            keys,
            values,
            (other_keys, other_values),
            arrived,
            forwarded,
            pieces,
        )
    out = out.reshape(BLOCK, HEADS * HEAD)
    return lax.cond(
        plan[ROW_LEFT, 0] > 0,
        lambda: full_attention(queries, keys, values, chosen_all, me),
        lambda: out,
    )


def solution(mesh):
    placed = (P("ctx", None), P("ctx", None), P("ctx", None), P("ctx", None, None))
    return jax.shard_map(
        body, mesh=mesh, in_specs=placed, out_specs=P("ctx", None), check_vma=False
    )
```

```python
import math

import jax
import jax.numpy as jnp
from jax import lax
from jax.experimental import pallas as pl
from jax.experimental.pallas import tpu as pltpu
from jax.sharding import PartitionSpec as P

HEAD = 128
HEADS = 16
BLOCK = 512
DEVICES = 128
CHIPS = 64
SCALE = math.log2(math.e) / math.sqrt(HEAD)

ONE = [(1, 0, 0), (3, 0, 0), (0, 1, 0), (0, 3, 0), (0, 0, 1), (0, 0, 3)]
PARTNER = 6
SHIFTS = [(0, 0, 0, 1)] * PARTNER
SHIFTS += [(*s, c) for s in ONE for c in (0, 1)]
KINDS = len(SHIFTS)
SPARE = 5
PIECE = 16
WAVES = 4
UP_TO = (8, 12, 15)
WAVE_OF = [1] * (PARTNER + 4) + [2] * 4 + [3] * 4
CODE_PARTNER = CHIPS
CODE_FORWARD = CODE_PARTNER + 1
CODE_SPARE = CODE_FORWARD + KINDS
LIST = 3 * HEADS
COUNT = LIST + WAVES * HEADS
NEED = COUNT + WAVES
TABLE = NEED + 2 * HEADS
HALF = BLOCK // PIECE
SLOT_PIECES = 2 * HALF + SPARE
SLOT_ROWS = SLOT_PIECES * PIECE

ROW_DIRECT = CHIPS
ROW_SPARE = ROW_DIRECT + CHIPS
ROW_FORWARD = ROW_SPARE + CHIPS
ROW_FORWARD_HEAD = ROW_FORWARD + KINDS
ROW_FROM_HEAD = ROW_FORWARD_HEAD + KINDS
ROW_FROM = ROW_FROM_HEAD + SPARE
ROW_FROM_RANK = ROW_FROM + SPARE
ROW_PARTNER = ROW_FROM_RANK + SPARE
ROW_LEFT = ROW_PARTNER + 1
ROWS = -(-(ROW_LEFT + 1) // 8) * 8


def place(chip):
    return ((chip & 3) << 4) | (chip & 12) | (chip >> 4)


def through(device, shift):
    z, x, y, c = device // 32, device // 8 % 4, device // 2 % 4, device % 2
    dz, dx, dy, dc = shift
    return (((z + dz) % 4 * 4 + (x + dx) % 4) * 4 + (y + dy) % 4) * 2 + (c ^ dc)


def shift_pairs(shift):
    return [(through(b, shift), b) for b in range(DEVICES)]


def roll_lanes(array, amount):
    amount = amount % DEVICES
    return pltpu.roll(array, amount, 1) if amount else array


def permuted(array, shift, lane, inverse=False):
    dz, dx, dy, dc = shift
    if inverse:
        dz, dx, dy = -dz % 4, -dx % 4, -dy % 4
    if dz:
        array = roll_lanes(array, -32 * dz)
    if dx:
        inside = (lane // 8) % 4 + dx < 4
        array = jnp.where(inside, roll_lanes(array, -8 * dx), roll_lanes(array, 32 - 8 * dx))
    if dy:
        inside = (lane // 2) % 4 + dy < 4
        array = jnp.where(inside, roll_lanes(array, -2 * dy), roll_lanes(array, 8 - 2 * dy))
    if dc:
        array = jnp.where(lane % 2 == 0, roll_lanes(array, -1), roll_lanes(array, 1))
    return array


def make_plan(chosen_ref, out_ref):
    chip = lax.broadcasted_iota(jnp.int32, (CHIPS, DEVICES), 0)
    lane = lax.broadcasted_iota(jnp.int32, (CHIPS, DEVICES), 1)
    even = jnp.zeros((CHIPS, DEVICES), jnp.int32)
    odd = jnp.zeros((CHIPS, DEVICES), jnp.int32)
    for entry in range(3 * HEADS):
        owner = chosen_ref[entry : entry + 1, :]
        even = even + jnp.where(owner == 2 * chip, entry // 3 + 1, 0)
        odd = odd + jnp.where(owner == 2 * chip + 1, entry // 3 + 1, 0)
    home = lane // 2 == chip
    partner = jnp.sum(jnp.where(home, even + odd, 0), axis=0, keepdims=True)
    even = jnp.where(home, 0, even)
    odd = jnp.where(home, 0, odd)
    waiting = jnp.where(even > 0, odd, 0)
    slot = jnp.where(even > 0, even - 1, jnp.where(odd > 0, odd + 15, -1))
    direct = jnp.where(even > 0, even, odd)
    free = jnp.where(home, 0, jnp.where(direct > 0, 0, 1))
    options = jnp.zeros((CHIPS, DEVICES), jnp.int32)
    for shift in sorted(set(SHIFTS)):
        options = options + permuted(free, shift, lane)
    score = options * 64 + (chip + 17 * lane) % 64
    big = 1 << 20
    out_ref[...] = jnp.zeros((ROWS, DEVICES), jnp.int32)
    for kind, shift in enumerate(SHIFTS):
        able = (waiting > 0) & (permuted(free, shift, lane) > 0)
        rated = jnp.where(able, score, big)
        best = jnp.min(rated, axis=0, keepdims=True)
        picked = able & (rated == best)
        head = jnp.sum(jnp.where(picked, waiting, 0), axis=0, keepdims=True)
        back = permuted(jnp.where(picked, waiting + 16, 0), shift, lane, inverse=True)
        waiting = jnp.where(picked, 0, waiting)
        slot = jnp.where(back > 0, back - 1, slot)
        free = jnp.where(back > 0, 0, free)
        forward = jnp.sum(jnp.where(back > 0, chip + 1, 0), axis=0, keepdims=True)
        out_ref[ROW_FORWARD + kind : ROW_FORWARD + kind + 1, :] = forward
        out_ref[ROW_FORWARD_HEAD + kind : ROW_FORWARD_HEAD + kind + 1, :] = head
    before = lax.broadcasted_iota(jnp.int32, (DEVICES, DEVICES), 0)
    after = lax.broadcasted_iota(jnp.int32, (DEVICES, DEVICES), 1)
    earlier = jnp.where((before < after) & (before % 2 == after % 2), 1.0, 0.0)
    rank = jnp.dot(
        jnp.where(waiting > 0, 1.0, 0.0), earlier, preferred_element_type=jnp.float32
    ).astype(jnp.int32)
    spare = jnp.zeros((CHIPS, DEVICES), jnp.int32)
    for index in range(SPARE):
        for core in range(2):
            chosen = (rank == index) & (lane % 2 == core)
            head = jnp.sum(jnp.where(chosen, waiting, 0), axis=1, keepdims=True)
            spare = jnp.where(lane == 2 * index + core, head, spare)
    out_ref[ROW_SPARE : ROW_SPARE + CHIPS, :] = spare
    excess = jnp.where((waiting > 0) & (rank >= SPARE), 1, 0)
    for index in range(SPARE):
        best = jnp.min(jnp.where(waiting > 0, chip, big), axis=0, keepdims=True)
        picked = (waiting > 0) & (chip == best)
        out_ref[ROW_FROM + index : ROW_FROM + index + 1, :] = jnp.where(best < big, best, 0)
        out_ref[ROW_FROM_RANK + index : ROW_FROM_RANK + index + 1, :] = jnp.minimum(
            jnp.sum(jnp.where(picked, rank, 0), axis=0, keepdims=True), SPARE - 1
        )
        out_ref[ROW_FROM_HEAD + index : ROW_FROM_HEAD + index + 1, :] = jnp.sum(
            jnp.where(picked, waiting, 0), axis=0, keepdims=True
        )
        waiting = jnp.where(picked, 0, waiting)
    excess = excess + waiting
    out_ref[ROW_PARTNER : ROW_PARTNER + 1, :] = partner
    left = jnp.max(jnp.max(excess, axis=0, keepdims=True), axis=1, keepdims=True)
    out_ref[ROW_LEFT : ROW_LEFT + 1, :] = jnp.broadcast_to(left, (1, DEVICES))
    out_ref[0:CHIPS, :] = slot
    out_ref[ROW_DIRECT : ROW_DIRECT + CHIPS, :] = direct


def columns(head):
    return pl.ds(pl.multiple_of(head * HEAD, HEAD), HEAD)


def make_table(plan, me, table):
    for entry in range(TABLE):
        table[entry] = 0

    def note(head_plus, code, wave):
        @pl.when(head_plus > 0)
        def _():
            head = head_plus - 1
            at = table[NEED + HEADS + head]
            table[head * 3 + jnp.minimum(at, 2)] = code
            table[NEED + HEADS + head] = at + 1
            table[NEED + head] = jnp.maximum(table[NEED + head], wave)

    def direct(chip, carry):
        note(plan[ROW_DIRECT + chip, me], place(chip), 0)
        return carry

    lax.fori_loop(0, CHIPS, direct, 0)
    note(plan[ROW_PARTNER, me], CODE_PARTNER, 0)
    for kind in range(KINDS):
        note(plan[ROW_FORWARD_HEAD + kind, me], CODE_FORWARD + kind, WAVE_OF[kind])
    for index in range(SPARE):
        note(plan[ROW_FROM_HEAD + index, me], CODE_SPARE + index, WAVES - 1)
    for ready in range(WAVES):

        def put(head, carry):
            @pl.when(table[NEED + head] == ready)
            def _():
                wave, so_far = ready, 0
                for earlier in range(ready):
                    so_far = so_far + table[COUNT + earlier]
                for later in range(ready, WAVES - 1):
                    so_far = so_far + table[COUNT + later]
                    full = (wave == later) & (so_far >= UP_TO[later])
                    wave = jnp.where(full, later + 1, wave)
                at = table[COUNT + wave]
                table[LIST + wave * HEADS + at] = head
                table[COUNT + wave] = at + 1

            return carry

        lax.fori_loop(0, HEADS, put, 0)


def pack_kernel(chosen, me_ref, keys_in, values_in, other_keys_in, other_values_in, *rest):
    plan_out, send, table, plan, keys, values, other_keys, other_values, sem, sems = rest
    loads = []
    pairs = zip(
        (keys_in, values_in, other_keys_in, other_values_in),
        (keys, values, other_keys, other_values),
    )
    for n, (source, into) in enumerate(pairs):
        loads.append(pltpu.make_async_copy(source, into, sems.at[n]))
        loads[-1].start()
    make_plan(chosen, plan_out)
    to_scalars = pltpu.make_async_copy(plan_out, plan, sems.at[4])
    to_scalars.start()
    to_scalars.wait()
    me = me_ref[0]
    chip, core = me >> 1, me & 1
    for load in loads:
        load.wait()

    def one_slot(dest, carry):
        code = plan[chip, 2 * dest + core]
        at = place(dest)
        cut = columns(jnp.maximum(code, 0) & 15)

        def copy(*sources):
            for half, source in enumerate(sources):
                pltpu.make_async_copy(
                    source.at[:, :, cut],
                    send.at[at >> 1, at & 1, pl.ds(half * HALF, HALF)],
                    sem,
                ).start()

        @pl.when(code >> 4 == core)
        def _():
            copy(keys, values)

        @pl.when(code >> 4 == 1 - core)
        def _():
            copy(other_keys, other_values)

        return carry + jnp.where(code >= 0, 2, 0)

    def one_spare(index, started):
        head = plan[ROW_SPARE + chip, 2 * index + core] - 1
        cut = columns(jnp.maximum(head, 0))

        def copy(*sources):
            for half, source in enumerate(sources):
                pltpu.make_async_copy(
                    source.at[:, :, cut], send.at[:, half, 2 * HALF + index], sem
                ).start()

        @pl.when((head >= 0) & (core == 1))
        def _():
            copy(keys, values)

        @pl.when((head >= 0) & (core == 0))
        def _():
            copy(other_keys, other_values)

        return started + jnp.where(head >= 0, 2, 0)

    started = lax.fori_loop(0, CHIPS, one_slot, 0)
    started = lax.fori_loop(0, SPARE, one_spare, started)
    make_table(plan, me, table)

    def wait_one(index, carry):
        pltpu.make_async_copy(
            keys.at[:, :, pl.ds(0, HEAD)], send.at[0, 0, pl.ds(0, HALF)], sem
        ).wait()
        return carry

    lax.fori_loop(0, started, wait_one, 0)


ANY = pl.BlockSpec(memory_space=pl.ANY)
SMEM = pl.BlockSpec(memory_space=pltpu.SMEM)
VMEM = pl.BlockSpec(memory_space=pltpu.VMEM)
BIG = pltpu.CompilerParams(vmem_limit_bytes=60 * 1024 * 1024)


def tiles(count):
    return jax.ShapeDtypeStruct((count, 2 * HALF, PIECE, HEAD), jnp.bfloat16)


def in_pieces(array):
    return array.reshape(HALF, PIECE, -1)


def pack(chosen_all, me, keys, values, other_keys, other_values):
    whole = pltpu.VMEM((HALF, PIECE, HEADS * HEAD), jnp.bfloat16)
    return pl.pallas_call(
        pack_kernel,
        in_specs=[VMEM, SMEM, ANY, ANY, ANY, ANY],
        out_specs=[VMEM, ANY, SMEM],
        out_shape=[
            jax.ShapeDtypeStruct((ROWS, DEVICES), jnp.int32),
            jax.ShapeDtypeStruct((HALF, 2, SLOT_PIECES, PIECE, HEAD), jnp.bfloat16),
            jax.ShapeDtypeStruct((TABLE,), jnp.int32),
        ],
        scratch_shapes=[pltpu.SMEM((ROWS, DEVICES), jnp.int32)]
        + [whole] * 4
        + [pltpu.SemaphoreType.DMA, pltpu.SemaphoreType.DMA((5,))],
        compiler_params=BIG,
        name="pack",
    )(chosen_all, me, *map(in_pieces, (keys, values, other_keys, other_values)))


def forward_kernel(plan, me_ref, arrived, *rest):
    outs, (moving, spare, gathered, sems, out_sems) = rest[:-5], rest[-5:]
    me = me_ref[0]
    core = me & 1
    load_spare = pltpu.make_async_copy(
        arrived.at[:, pl.ds(2 * HALF, SPARE)], spare, sems.at[KINDS]
    )
    load_spare.start()
    steps = []
    for kind in range(KINDS):
        out = outs[1].at[kind] if kind < PARTNER else outs[kind - PARTNER + 2].at[0]
        chip = plan[ROW_FORWARD + kind, me] - 1
        source = arrived.at[place(jnp.maximum(chip, 0)), pl.ds(0, 2 * HALF)]
        load = pltpu.make_async_copy(source, moving.at[kind], sems.at[kind])
        store = pltpu.make_async_copy(moving.at[kind], out, out_sems.at[kind])
        steps.append((chip >= 0, load, store))
    for used, load, _ in steps:

        @pl.when(used)
        def _():
            load.start()

    load_spare.wait()

    def one_dest(dest, carry):
        device = 2 * dest + core

        def move(index):
            @pl.when(plan[ROW_FROM_HEAD + index, device] > 0)
            def _():
                chip = plan[ROW_FROM + index, device]
                rank = plan[ROW_FROM_RANK + index, device]
                gathered[place(dest), index] = spare[place(chip), rank]
                if index + 1 < SPARE:
                    move(index + 1)

        move(0)
        return carry

    lax.fori_loop(0, CHIPS, one_dest, 0)
    last = pltpu.make_async_copy(gathered, outs[0], out_sems.at[KINDS])
    last.start()
    for used, load, store in steps:

        @pl.when(used)
        def _():
            load.wait()
            store.start()

    for used, _, store in steps:

        @pl.when(used)
        def _():
            store.wait()

    last.wait()


def forward(plan, me, arrived):
    return pl.pallas_call(
        forward_kernel,
        in_specs=[SMEM, SMEM, ANY],
        out_specs=[ANY] * (KINDS - PARTNER + 2),
        out_shape=[jax.ShapeDtypeStruct((CHIPS, SPARE, PIECE, HEAD), jnp.bfloat16)]
        + [tiles(PARTNER)]
        + [tiles(1)] * (KINDS - PARTNER),
        scratch_shapes=[
            pltpu.VMEM((KINDS, 2 * HALF, PIECE, HEAD), jnp.bfloat16),
            pltpu.VMEM((CHIPS, SPARE, PIECE, HEAD), jnp.bfloat16),
            pltpu.VMEM((CHIPS, SPARE, PIECE, HEAD), jnp.bfloat16),
            pltpu.SemaphoreType.DMA((KINDS + 1,)),
            pltpu.SemaphoreType.DMA((KINDS + 1,)),
        ],
        compiler_params=BIG,
        name="forward",
    )(plan, me, arrived)


ROWS_AT_ONCE = 256


def scores_of(query, key):
    return lax.dot_general(
        query, key, (((1,), (1,)), ((), ())), preferred_element_type=jnp.float32
    )


def attend_kernel(wave, kinds, table, queries, keys, values, *rest):
    other_keys, other_values, arrived = rest[:3]
    forwarded = dict(zip(kinds, rest[3 : 3 + len(kinds)]))
    pieces = rest[3 + len(kinds)] if wave == WAVES - 1 else None
    out, query_buf, key_buf, value_buf, out_buf, sems, out_sems = rest[-7:]
    count = table[COUNT + wave]

    def head_at(index):
        return table[LIST + wave * HEADS + index]

    def load(index, slot):
        head = head_at(index)

        def start(j, source_key, source_value):
            into_value = value_buf.at[slot, j, :, :, pl.ds(0, HEAD)]
            pltpu.make_async_copy(source_key, key_buf.at[slot, j], sems.at[slot, 2 * j]).start()
            pltpu.make_async_copy(source_value, into_value, sems.at[slot, 2 * j + 1]).start()

        cut = columns(head)
        pltpu.make_async_copy(queries.at[:, :, cut], query_buf.at[slot], sems.at[slot, 8]).start()
        start(3, keys.at[:, :, cut], values.at[:, :, cut])
        for j in range(3):
            code = table[head * 3 + j]

            @pl.when(code < CHIPS)
            def _():
                start(j, arrived.at[code, pl.ds(0, HALF)], arrived.at[code, pl.ds(HALF, HALF)])

            @pl.when(code >= CHIPS)
            def _():
                @pl.when(code == CODE_PARTNER)
                def _():
                    start(j, other_keys.at[:, :, cut], other_values.at[:, :, cut])

                for kind, ref in forwarded.items():
                    last = kind + (PARTNER if kind == 0 else 1)

                    @pl.when((code >= CODE_FORWARD + kind) & (code < CODE_FORWARD + last))
                    def _():
                        tile = ref.at[code - CODE_FORWARD - kind]
                        start(j, tile.at[pl.ds(0, HALF)], tile.at[pl.ds(HALF, HALF)])

                if pieces is not None:

                    @pl.when(code >= CODE_SPARE)
                    def _():
                        start(j, pieces.at[:, 0, code - CODE_SPARE], pieces.at[:, 1, code - CODE_SPARE])

    def store(index, slot):
        return pltpu.make_async_copy(
            out_buf.at[slot], out.at[:, :, columns(head_at(index))], out_sems.at[slot]
        )

    @pl.when(count > 0)
    def _():
        load(0, 0)
        ones = jnp.ones((HALF, PIECE, HEAD), jnp.bfloat16)
        for slot in range(2):
            for j in range(4):
                value_buf[slot, j, :, :, HEAD:] = ones

    def one_head(index, carry):
        slot = index % 2

        @pl.when(index + 1 < count)
        def _():
            load(index + 1, 1 - slot)

        for j in range(4):
            into_value = value_buf.at[slot, j, :, :, pl.ds(0, HEAD)]
            tile = arrived.at[0, pl.ds(0, HALF)]
            pltpu.make_async_copy(tile, key_buf.at[slot, j], sems.at[slot, 2 * j]).wait()
            pltpu.make_async_copy(tile, into_value, sems.at[slot, 2 * j + 1]).wait()
        pltpu.make_async_copy(tile, query_buf.at[slot], sems.at[slot, 8]).wait()

        @pl.when(index >= 2)
        def _():
            store(index - 2, slot).wait()

        query = query_buf[slot].reshape(BLOCK, HEAD)
        for start in range(0, BLOCK, ROWS_AT_ONCE):
            stop = start + ROWS_AT_ONCE
            q = query[start:stop, :]
            total = highest = None
            for j in (3, 0, 1, 2):
                seen = stop if j == 3 else BLOCK
                scores = scores_of(q, key_buf[slot, j, 0 : seen // PIECE].reshape(seen, HEAD))
                if j == 3:
                    row_iota = lax.broadcasted_iota(jnp.int32, scores.shape, 0) + start
                    col_iota = lax.broadcasted_iota(jnp.int32, scores.shape, 1)
                    scores = jnp.where(col_iota <= row_iota, scores, -jnp.inf)
                top = jnp.max(scores, axis=1, keepdims=True)
                if highest is not None:
                    top = jnp.maximum(highest, top)
                weight = jnp.exp2((scores - top) * SCALE).astype(jnp.bfloat16)
                value = value_buf[slot, j, 0 : seen // PIECE].reshape(seen, 2 * HEAD)
                added = jnp.dot(weight, value, preferred_element_type=jnp.float32)
                if highest is None:
                    total = added
                else:
                    total = total * jnp.exp2((highest - top) * SCALE) + added
                highest = top
            result = (total[:, :HEAD] / total[:, HEAD:]).astype(jnp.bfloat16)
            span = slice(start // PIECE, stop // PIECE)
            out_buf[slot, span] = result.reshape(ROWS_AT_ONCE // PIECE, PIECE, HEAD)
        store(index, slot).start()
        return carry

    lax.fori_loop(0, count, one_head, 0)

    @pl.when(count >= 2)
    def _():
        store(count - 2, count % 2).wait()

    @pl.when(count >= 1)
    def _():
        store(count - 1, (count - 1) % 2).wait()


HEADS_EXPECTED = (9, 4, 2, 2)


def attend(wave, before, table, queries, keys, values, others, arrived, forwarded, pieces):
    kinds = [kind for kind in forwarded if WAVE_OF[kind] <= wave]
    operands = [table, *map(in_pieces, (queries, keys, values, *others)), arrived]
    operands += [forwarded[kind] for kind in kinds]
    if wave == WAVES - 1:
        operands.append(pieces.reshape(HALF, 2, SPARE, PIECE, HEAD))
    if before is not None:
        operands.append(before)
    size = HEADS_EXPECTED[wave] * BLOCK * 4 * BLOCK * HEAD
    return pl.pallas_call(
        lambda *refs: attend_kernel(wave, kinds, *refs),
        in_specs=[SMEM] + [ANY] * (len(operands) - 1),
        out_specs=ANY,
        out_shape=jax.ShapeDtypeStruct((HALF, PIECE, HEADS * HEAD), jnp.bfloat16),
        input_output_aliases={} if before is None else {len(operands) - 1: 0},
        scratch_shapes=[
            pltpu.VMEM((2, HALF, PIECE, HEAD), jnp.bfloat16),
            pltpu.VMEM((2, 4, HALF, PIECE, HEAD), jnp.bfloat16),
            pltpu.VMEM((2, 4, HALF, PIECE, 2 * HEAD), jnp.bfloat16),
            pltpu.VMEM((2, HALF, PIECE, HEAD), jnp.bfloat16),
            pltpu.SemaphoreType.DMA((2, 9)),
            pltpu.SemaphoreType.DMA((2,)),
        ],
        cost_estimate=pl.CostEstimate(
            flops=16 * size, bytes_accessed=3 * 2**20, transcendentals=size // HEAD
        ),
        compiler_params=BIG,
        name="attend",
    )(*operands)


LANES = [[2 * place(at) + core for at in range(CHIPS)] for core in range(2)]
SWAP = [(device, device ^ 1) for device in range(DEVICES)]


def exchange(array):
    return lax.all_to_all(array, "ctx", 0, 0, axis_index_groups=LANES, tiled=True)


def full_attention(queries, keys, values, chosen_all, me):
    heads = jnp.arange(3 * HEADS, dtype=jnp.int32) // 3
    mine = lax.dynamic_index_in_dim(chosen_all, me, 0, keepdims=False)
    wants = chosen_all == me
    which = jnp.max(jnp.where(wants, heads[None, :], 0), axis=1)
    key_heads = keys.reshape(BLOCK, HEADS, HEAD).transpose(1, 0, 2)
    value_heads = values.reshape(BLOCK, HEADS, HEAD).transpose(1, 0, 2)
    got_key = lax.all_to_all(jnp.take(key_heads, which, axis=0), "ctx", 0, 0, tiled=True)
    got_value = lax.all_to_all(jnp.take(value_heads, which, axis=0), "ctx", 0, 0, tiled=True)
    q_heads = queries.reshape(BLOCK, HEADS, HEAD).transpose(1, 0, 2)
    allowed = jnp.arange(4 * BLOCK)[None, :] >= BLOCK
    allowed = allowed | (jnp.arange(4 * BLOCK)[None, :] <= jnp.arange(BLOCK)[:, None])

    def one_head(head):
        picks = lax.dynamic_slice(mine, (3 * head,), (3,))
        k = jnp.concatenate([key_heads[head], got_key[picks].reshape(3 * BLOCK, HEAD)], axis=0)
        v = jnp.concatenate([value_heads[head], got_value[picks].reshape(3 * BLOCK, HEAD)], axis=0)
        s = jnp.where(allowed, scores_of(q_heads[head], k), -jnp.inf)
        weight = jnp.exp2((s - jnp.max(s, axis=1, keepdims=True)) * SCALE)
        total = jnp.sum(weight, axis=1, keepdims=True)
        o = jnp.dot(weight.astype(jnp.bfloat16), v, preferred_element_type=jnp.float32)
        return (o / total).astype(jnp.bfloat16)

    out = lax.map(one_head, jnp.arange(HEADS))
    return out.transpose(1, 0, 2).reshape(BLOCK, HEADS * HEAD)


def body(queries, keys, values, chosen):
    me = lax.axis_index("ctx").astype(jnp.int32)
    me_ref = me.reshape(1)
    other_keys = lax.ppermute(keys, "ctx", SWAP)
    other_values = lax.ppermute(values, "ctx", SWAP)
    spread = jnp.broadcast_to(chosen.reshape(1, 3 * HEADS), (DEVICES, 3 * HEADS))
    chosen_all = lax.all_to_all(spread, "ctx", 0, 0, tiled=True)
    plan, send, table = pack(chosen_all.T, me_ref, keys, values, other_keys, other_values)
    sent = exchange(send.reshape(CHIPS, SLOT_ROWS, HEAD))
    held = (sent, plan, table, queries, keys, values, other_keys, other_values, me_ref)
    held = lax.optimization_barrier(held)
    arrived, plan, table, queries, keys, values, other_keys, other_values, me_ref = held
    arrived = arrived.reshape(CHIPS, SLOT_PIECES, PIECE, HEAD)
    pieces, *outgoing = forward(plan, me_ref, arrived)
    pieces = exchange(pieces)
    outgoing = dict(zip([0, *range(PARTNER, KINDS)], outgoing))
    forwarded = {}
    out = None
    for wave in range(WAVES):
        if wave:
            for kind in [kind for kind in outgoing if WAVE_OF[kind] == wave]:
                forwarded[kind] = lax.ppermute(outgoing[kind], "ctx", shift_pairs(SHIFTS[kind]))
        out = attend(
            wave,
            out,
            table,
            queries,
            keys,
            values,
            (other_keys, other_values),
            arrived,
            forwarded,
            pieces,
        )
    out = out.reshape(BLOCK, HEADS * HEAD)
    return lax.cond(
        plan[ROW_LEFT, 0] > 0,
        lambda: full_attention(queries, keys, values, chosen_all, me),
        lambda: out,
    )


def solution(mesh):
    placed = (P("ctx", None), P("ctx", None), P("ctx", None), P("ctx", None, None))
    return jax.shard_map(
        body, mesh=mesh, in_specs=placed, out_specs=P("ctx", None), check_vma=False
    )
```

```python
import math

import jax
import jax.numpy as jnp
from jax import lax
from jax.experimental import pallas as pl
from jax.experimental.pallas import tpu as pltpu
from jax.sharding import PartitionSpec as P

HEAD = 128
HEADS = 16
BLOCK = 512
DEVICES = 128
CHIPS = 64
SCALE = math.log2(math.e) / math.sqrt(HEAD)

ONE = [(1, 0, 0), (3, 0, 0), (0, 1, 0), (0, 3, 0), (0, 0, 1), (0, 0, 3)]
PARTNER = 6
SHIFTS = [(0, 0, 0, 1)] * PARTNER
SHIFTS += [(*s, c) for s in ONE for c in (0, 1)]
KINDS = len(SHIFTS)
SPARE = 5
PIECE = 16
WAVES = 4
UP_TO = (8, 12, 16)
WAVE_OF = [1] * (PARTNER + 4) + [2] * 4 + [3] * 4
CODE_PARTNER = CHIPS
CODE_FORWARD = CODE_PARTNER + 1
CODE_SPARE = CODE_FORWARD + KINDS
LIST = 3 * HEADS
COUNT = LIST + WAVES * HEADS
NEED = COUNT + WAVES
TABLE = NEED + 2 * HEADS
HALF = BLOCK // PIECE
SLOT_PIECES = 2 * HALF + SPARE
SLOT_ROWS = SLOT_PIECES * PIECE

ROW_DIRECT = CHIPS
ROW_SPARE = ROW_DIRECT + CHIPS
ROW_FORWARD = ROW_SPARE + CHIPS
ROW_FORWARD_HEAD = ROW_FORWARD + KINDS
ROW_FROM_HEAD = ROW_FORWARD_HEAD + KINDS
ROW_FROM = ROW_FROM_HEAD + SPARE
ROW_FROM_RANK = ROW_FROM + SPARE
ROW_PARTNER = ROW_FROM_RANK + SPARE
ROW_LEFT = ROW_PARTNER + 1
ROWS = -(-(ROW_LEFT + 1) // 8) * 8


def place(chip):
    return ((chip & 3) << 4) | (chip & 12) | (chip >> 4)


def through(device, shift):
    z, x, y, c = device // 32, device // 8 % 4, device // 2 % 4, device % 2
    dz, dx, dy, dc = shift
    return (((z + dz) % 4 * 4 + (x + dx) % 4) * 4 + (y + dy) % 4) * 2 + (c ^ dc)


def shift_pairs(shift):
    return [(through(b, shift), b) for b in range(DEVICES)]


def roll_lanes(array, amount):
    amount = amount % DEVICES
    return pltpu.roll(array, amount, 1) if amount else array


def permuted(array, shift, lane, inverse=False):
    dz, dx, dy, dc = shift
    if inverse:
        dz, dx, dy = -dz % 4, -dx % 4, -dy % 4
    if dz:
        array = roll_lanes(array, -32 * dz)
    if dx:
        inside = (lane // 8) % 4 + dx < 4
        array = jnp.where(inside, roll_lanes(array, -8 * dx), roll_lanes(array, 32 - 8 * dx))
    if dy:
        inside = (lane // 2) % 4 + dy < 4
        array = jnp.where(inside, roll_lanes(array, -2 * dy), roll_lanes(array, 8 - 2 * dy))
    if dc:
        array = jnp.where(lane % 2 == 0, roll_lanes(array, -1), roll_lanes(array, 1))
    return array


def make_plan(chosen_ref, out_ref):
    chip = lax.broadcasted_iota(jnp.int32, (CHIPS, DEVICES), 0)
    lane = lax.broadcasted_iota(jnp.int32, (CHIPS, DEVICES), 1)
    even = jnp.zeros((CHIPS, DEVICES), jnp.int32)
    odd = jnp.zeros((CHIPS, DEVICES), jnp.int32)
    for entry in range(3 * HEADS):
        owner = chosen_ref[entry : entry + 1, :]
        even = even + jnp.where(owner == 2 * chip, entry // 3 + 1, 0)
        odd = odd + jnp.where(owner == 2 * chip + 1, entry // 3 + 1, 0)
    home = lane // 2 == chip
    partner = jnp.sum(jnp.where(home, even + odd, 0), axis=0, keepdims=True)
    even = jnp.where(home, 0, even)
    odd = jnp.where(home, 0, odd)
    waiting = jnp.where(even > 0, odd, 0)
    slot = jnp.where(even > 0, even - 1, jnp.where(odd > 0, odd + 15, -1))
    direct = jnp.where(even > 0, even, odd)
    free = jnp.where(home, 0, jnp.where(direct > 0, 0, 1))
    options = jnp.zeros((CHIPS, DEVICES), jnp.int32)
    for shift in sorted(set(SHIFTS)):
        options = options + permuted(free, shift, lane)
    score = options * 64 + (chip + 17 * lane) % 64
    big = 1 << 20
    out_ref[...] = jnp.zeros((ROWS, DEVICES), jnp.int32)
    for kind, shift in enumerate(SHIFTS):
        able = (waiting > 0) & (permuted(free, shift, lane) > 0)
        rated = jnp.where(able, score, big)
        best = jnp.min(rated, axis=0, keepdims=True)
        picked = able & (rated == best)
        head = jnp.sum(jnp.where(picked, waiting, 0), axis=0, keepdims=True)
        back = permuted(jnp.where(picked, waiting + 16, 0), shift, lane, inverse=True)
        waiting = jnp.where(picked, 0, waiting)
        slot = jnp.where(back > 0, back - 1, slot)
        free = jnp.where(back > 0, 0, free)
        forward = jnp.sum(jnp.where(back > 0, chip + 1, 0), axis=0, keepdims=True)
        out_ref[ROW_FORWARD + kind : ROW_FORWARD + kind + 1, :] = forward
        out_ref[ROW_FORWARD_HEAD + kind : ROW_FORWARD_HEAD + kind + 1, :] = head
    before = lax.broadcasted_iota(jnp.int32, (DEVICES, DEVICES), 0)
    after = lax.broadcasted_iota(jnp.int32, (DEVICES, DEVICES), 1)
    earlier = jnp.where((before < after) & (before % 2 == after % 2), 1.0, 0.0)
    rank = jnp.dot(
        jnp.where(waiting > 0, 1.0, 0.0), earlier, preferred_element_type=jnp.float32
    ).astype(jnp.int32)
    spare = jnp.zeros((CHIPS, DEVICES), jnp.int32)
    for index in range(SPARE):
        for core in range(2):
            chosen = (rank == index) & (lane % 2 == core)
            head = jnp.sum(jnp.where(chosen, waiting, 0), axis=1, keepdims=True)
            spare = jnp.where(lane == 2 * index + core, head, spare)
    out_ref[ROW_SPARE : ROW_SPARE + CHIPS, :] = spare
    excess = jnp.where((waiting > 0) & (rank >= SPARE), 1, 0)
    for index in range(SPARE):
        best = jnp.min(jnp.where(waiting > 0, chip, big), axis=0, keepdims=True)
        picked = (waiting > 0) & (chip == best)
        out_ref[ROW_FROM + index : ROW_FROM + index + 1, :] = jnp.where(best < big, best, 0)
        out_ref[ROW_FROM_RANK + index : ROW_FROM_RANK + index + 1, :] = jnp.minimum(
            jnp.sum(jnp.where(picked, rank, 0), axis=0, keepdims=True), SPARE - 1
        )
        out_ref[ROW_FROM_HEAD + index : ROW_FROM_HEAD + index + 1, :] = jnp.sum(
            jnp.where(picked, waiting, 0), axis=0, keepdims=True
        )
        waiting = jnp.where(picked, 0, waiting)
    excess = excess + waiting
    out_ref[ROW_PARTNER : ROW_PARTNER + 1, :] = partner
    left = jnp.max(jnp.max(excess, axis=0, keepdims=True), axis=1, keepdims=True)
    out_ref[ROW_LEFT : ROW_LEFT + 1, :] = jnp.broadcast_to(left, (1, DEVICES))
    out_ref[0:CHIPS, :] = slot
    out_ref[ROW_DIRECT : ROW_DIRECT + CHIPS, :] = direct


def columns(head):
    return pl.ds(pl.multiple_of(head * HEAD, HEAD), HEAD)


def make_table(plan, me, table):
    for entry in range(TABLE):
        table[entry] = 0

    def note(head_plus, code, wave):
        @pl.when(head_plus > 0)
        def _():
            head = head_plus - 1
            at = table[NEED + HEADS + head]
            table[head * 3 + jnp.minimum(at, 2)] = code
            table[NEED + HEADS + head] = at + 1
            table[NEED + head] = jnp.maximum(table[NEED + head], wave)

    def direct(chip, carry):
        note(plan[ROW_DIRECT + chip, me], place(chip), 0)
        return carry

    lax.fori_loop(0, CHIPS, direct, 0)
    note(plan[ROW_PARTNER, me], CODE_PARTNER, 0)
    for kind in range(KINDS):
        note(plan[ROW_FORWARD_HEAD + kind, me], CODE_FORWARD + kind, WAVE_OF[kind])
    for index in range(SPARE):
        note(plan[ROW_FROM_HEAD + index, me], CODE_SPARE + index, WAVES - 1)
    for ready in range(WAVES):

        def put(head, carry):
            @pl.when(table[NEED + head] == ready)
            def _():
                wave, so_far = ready, 0
                for earlier in range(ready):
                    so_far = so_far + table[COUNT + earlier]
                for later in range(ready, WAVES - 1):
                    so_far = so_far + table[COUNT + later]
                    full = (wave == later) & (so_far >= UP_TO[later])
                    wave = jnp.where(full, later + 1, wave)
                at = table[COUNT + wave]
                table[LIST + wave * HEADS + at] = head
                table[COUNT + wave] = at + 1

            return carry

        lax.fori_loop(0, HEADS, put, 0)


def pack_kernel(chosen, me_ref, keys_in, values_in, other_keys_in, other_values_in, *rest):
    plan_out, send, table, plan, keys, values, other_keys, other_values, sem, sems = rest
    loads = []
    pairs = zip(
        (keys_in, values_in, other_keys_in, other_values_in),
        (keys, values, other_keys, other_values),
    )
    for n, (source, into) in enumerate(pairs):
        loads.append(pltpu.make_async_copy(source, into, sems.at[n]))
        loads[-1].start()
    make_plan(chosen, plan_out)
    to_scalars = pltpu.make_async_copy(plan_out, plan, sems.at[4])
    to_scalars.start()
    to_scalars.wait()
    me = me_ref[0]
    chip, core = me >> 1, me & 1
    for load in loads:
        load.wait()

    def one_slot(dest, carry):
        code = plan[chip, 2 * dest + core]
        at = place(dest)
        cut = columns(jnp.maximum(code, 0) & 15)

        def copy(*sources):
            for half, source in enumerate(sources):
                pltpu.make_async_copy(
                    source.at[:, :, cut],
                    send.at[at >> 1, at & 1, pl.ds(half * HALF, HALF)],
                    sem,
                ).start()

        @pl.when(code >> 4 == core)
        def _():
            copy(keys, values)

        @pl.when(code >> 4 == 1 - core)
        def _():
            copy(other_keys, other_values)

        return carry + jnp.where(code >= 0, 2, 0)

    def one_spare(index, started):
        head = plan[ROW_SPARE + chip, 2 * index + core] - 1
        cut = columns(jnp.maximum(head, 0))

        def copy(*sources):
            for half, source in enumerate(sources):
                pltpu.make_async_copy(
                    source.at[:, :, cut], send.at[:, half, 2 * HALF + index], sem
                ).start()

        @pl.when((head >= 0) & (core == 1))
        def _():
            copy(keys, values)

        @pl.when((head >= 0) & (core == 0))
        def _():
            copy(other_keys, other_values)

        return started + jnp.where(head >= 0, 2, 0)

    started = lax.fori_loop(0, CHIPS, one_slot, 0)
    started = lax.fori_loop(0, SPARE, one_spare, started)
    make_table(plan, me, table)

    def wait_one(index, carry):
        pltpu.make_async_copy(
            keys.at[:, :, pl.ds(0, HEAD)], send.at[0, 0, pl.ds(0, HALF)], sem
        ).wait()
        return carry

    lax.fori_loop(0, started, wait_one, 0)


ANY = pl.BlockSpec(memory_space=pl.ANY)
SMEM = pl.BlockSpec(memory_space=pltpu.SMEM)
VMEM = pl.BlockSpec(memory_space=pltpu.VMEM)
BIG = pltpu.CompilerParams(vmem_limit_bytes=60 * 1024 * 1024)


def tiles(count):
    return jax.ShapeDtypeStruct((count, 2 * HALF, PIECE, HEAD), jnp.bfloat16)


def in_pieces(array):
    return array.reshape(HALF, PIECE, -1)


def pack(chosen_all, me, keys, values, other_keys, other_values):
    whole = pltpu.VMEM((HALF, PIECE, HEADS * HEAD), jnp.bfloat16)
    return pl.pallas_call(
        pack_kernel,
        in_specs=[VMEM, SMEM, ANY, ANY, ANY, ANY],
        out_specs=[VMEM, ANY, SMEM],
        out_shape=[
            jax.ShapeDtypeStruct((ROWS, DEVICES), jnp.int32),
            jax.ShapeDtypeStruct((HALF, 2, SLOT_PIECES, PIECE, HEAD), jnp.bfloat16),
            jax.ShapeDtypeStruct((TABLE,), jnp.int32),
        ],
        scratch_shapes=[pltpu.SMEM((ROWS, DEVICES), jnp.int32)]
        + [whole] * 4
        + [pltpu.SemaphoreType.DMA, pltpu.SemaphoreType.DMA((5,))],
        compiler_params=BIG,
        name="pack",
    )(chosen_all, me, *map(in_pieces, (keys, values, other_keys, other_values)))


def forward_kernel(plan, me_ref, arrived, *rest):
    outs, (moving, spare, gathered, sems, out_sems) = rest[:-5], rest[-5:]
    me = me_ref[0]
    core = me & 1
    load_spare = pltpu.make_async_copy(
        arrived.at[:, pl.ds(2 * HALF, SPARE)], spare, sems.at[KINDS]
    )
    load_spare.start()
    steps = []
    for kind in range(KINDS):
        out = outs[1].at[kind] if kind < PARTNER else outs[kind - PARTNER + 2].at[0]
        chip = plan[ROW_FORWARD + kind, me] - 1
        source = arrived.at[place(jnp.maximum(chip, 0)), pl.ds(0, 2 * HALF)]
        load = pltpu.make_async_copy(source, moving.at[kind], sems.at[kind])
        store = pltpu.make_async_copy(moving.at[kind], out, out_sems.at[kind])
        steps.append((chip >= 0, load, store))
    for used, load, _ in steps:

        @pl.when(used)
        def _():
            load.start()

    load_spare.wait()

    def one_dest(dest, carry):
        device = 2 * dest + core

        def move(index):
            @pl.when(plan[ROW_FROM_HEAD + index, device] > 0)
            def _():
                chip = plan[ROW_FROM + index, device]
                rank = plan[ROW_FROM_RANK + index, device]
                gathered[place(dest), index] = spare[place(chip), rank]
                if index + 1 < SPARE:
                    move(index + 1)

        move(0)
        return carry

    lax.fori_loop(0, CHIPS, one_dest, 0)
    last = pltpu.make_async_copy(gathered, outs[0], out_sems.at[KINDS])
    last.start()
    for used, load, store in steps:

        @pl.when(used)
        def _():
            load.wait()
            store.start()

    for used, _, store in steps:

        @pl.when(used)
        def _():
            store.wait()

    last.wait()


def forward(plan, me, arrived):
    return pl.pallas_call(
        forward_kernel,
        in_specs=[SMEM, SMEM, ANY],
        out_specs=[ANY] * (KINDS - PARTNER + 2),
        out_shape=[jax.ShapeDtypeStruct((CHIPS, SPARE, PIECE, HEAD), jnp.bfloat16)]
        + [tiles(PARTNER)]
        + [tiles(1)] * (KINDS - PARTNER),
        scratch_shapes=[
            pltpu.VMEM((KINDS, 2 * HALF, PIECE, HEAD), jnp.bfloat16),
            pltpu.VMEM((CHIPS, SPARE, PIECE, HEAD), jnp.bfloat16),
            pltpu.VMEM((CHIPS, SPARE, PIECE, HEAD), jnp.bfloat16),
            pltpu.SemaphoreType.DMA((KINDS + 1,)),
            pltpu.SemaphoreType.DMA((KINDS + 1,)),
        ],
        compiler_params=BIG,
        name="forward",
    )(plan, me, arrived)


ROWS_AT_ONCE = 256


def scores_of(query, key):
    return lax.dot_general(
        query, key, (((1,), (1,)), ((), ())), preferred_element_type=jnp.float32
    )


def attend_kernel(wave, kinds, table, queries, keys, values, *rest):
    other_keys, other_values, arrived = rest[:3]
    forwarded = dict(zip(kinds, rest[3 : 3 + len(kinds)]))
    pieces = rest[3 + len(kinds)] if wave == WAVES - 1 else None
    out, query_buf, key_buf, value_buf, out_buf, sems, out_sems = rest[-7:]
    count = table[COUNT + wave]

    def head_at(index):
        return table[LIST + wave * HEADS + index]

    def load(index, slot):
        head = head_at(index)

        def start(j, source_key, source_value):
            into_value = value_buf.at[slot, j, :, :, pl.ds(0, HEAD)]
            pltpu.make_async_copy(source_key, key_buf.at[slot, j], sems.at[slot, 2 * j]).start()
            pltpu.make_async_copy(source_value, into_value, sems.at[slot, 2 * j + 1]).start()

        cut = columns(head)
        pltpu.make_async_copy(queries.at[:, :, cut], query_buf.at[slot], sems.at[slot, 8]).start()
        start(3, keys.at[:, :, cut], values.at[:, :, cut])
        for j in range(3):
            code = table[head * 3 + j]

            @pl.when(code < CHIPS)
            def _():
                start(j, arrived.at[code, pl.ds(0, HALF)], arrived.at[code, pl.ds(HALF, HALF)])

            @pl.when(code >= CHIPS)
            def _():
                @pl.when(code == CODE_PARTNER)
                def _():
                    start(j, other_keys.at[:, :, cut], other_values.at[:, :, cut])

                for kind, ref in forwarded.items():
                    last = kind + (PARTNER if kind == 0 else 1)

                    @pl.when((code >= CODE_FORWARD + kind) & (code < CODE_FORWARD + last))
                    def _():
                        tile = ref.at[code - CODE_FORWARD - kind]
                        start(j, tile.at[pl.ds(0, HALF)], tile.at[pl.ds(HALF, HALF)])

                if pieces is not None:

                    @pl.when(code >= CODE_SPARE)
                    def _():
                        start(j, pieces.at[:, 0, code - CODE_SPARE], pieces.at[:, 1, code - CODE_SPARE])

    def store(index, slot):
        return pltpu.make_async_copy(
            out_buf.at[slot], out.at[:, :, columns(head_at(index))], out_sems.at[slot]
        )

    @pl.when(count > 0)
    def _():
        load(0, 0)
        ones = jnp.ones((HALF, PIECE, HEAD), jnp.bfloat16)
        for slot in range(2):
            for j in range(4):
                value_buf[slot, j, :, :, HEAD:] = ones

    def one_head(index, carry):
        slot = index % 2

        @pl.when(index + 1 < count)
        def _():
            load(index + 1, 1 - slot)

        for j in range(4):
            into_value = value_buf.at[slot, j, :, :, pl.ds(0, HEAD)]
            tile = arrived.at[0, pl.ds(0, HALF)]
            pltpu.make_async_copy(tile, key_buf.at[slot, j], sems.at[slot, 2 * j]).wait()
            pltpu.make_async_copy(tile, into_value, sems.at[slot, 2 * j + 1]).wait()
        pltpu.make_async_copy(tile, query_buf.at[slot], sems.at[slot, 8]).wait()

        @pl.when(index >= 2)
        def _():
            store(index - 2, slot).wait()

        query = query_buf[slot].reshape(BLOCK, HEAD)
        for start in range(0, BLOCK, ROWS_AT_ONCE):
            stop = start + ROWS_AT_ONCE
            q = query[start:stop, :]
            total = highest = None
            for j in (3, 0, 1, 2):
                seen = stop if j == 3 else BLOCK
                scores = scores_of(q, key_buf[slot, j, 0 : seen // PIECE].reshape(seen, HEAD))
                if j == 3:
                    row_iota = lax.broadcasted_iota(jnp.int32, scores.shape, 0) + start
                    col_iota = lax.broadcasted_iota(jnp.int32, scores.shape, 1)
                    scores = jnp.where(col_iota <= row_iota, scores, -jnp.inf)
                top = jnp.max(scores, axis=1, keepdims=True)
                if highest is not None:
                    top = jnp.maximum(highest, top)
                weight = jnp.exp2((scores - top) * SCALE).astype(jnp.bfloat16)
                value = value_buf[slot, j, 0 : seen // PIECE].reshape(seen, 2 * HEAD)
                added = jnp.dot(weight, value, preferred_element_type=jnp.float32)
                if highest is None:
                    total = added
                else:
                    total = total * jnp.exp2((highest - top) * SCALE) + added
                highest = top
            result = (total[:, :HEAD] / total[:, HEAD:]).astype(jnp.bfloat16)
            span = slice(start // PIECE, stop // PIECE)
            out_buf[slot, span] = result.reshape(ROWS_AT_ONCE // PIECE, PIECE, HEAD)
        store(index, slot).start()
        return carry

    lax.fori_loop(0, count, one_head, 0)

    @pl.when(count >= 2)
    def _():
        store(count - 2, count % 2).wait()

    @pl.when(count >= 1)
    def _():
        store(count - 1, (count - 1) % 2).wait()


HEADS_EXPECTED = (9, 4, 2, 2)


def attend(wave, before, table, queries, keys, values, others, arrived, forwarded, pieces):
    kinds = [kind for kind in forwarded if WAVE_OF[kind] <= wave]
    operands = [table, *map(in_pieces, (queries, keys, values, *others)), arrived]
    operands += [forwarded[kind] for kind in kinds]
    if wave == WAVES - 1:
        operands.append(pieces.reshape(HALF, 2, SPARE, PIECE, HEAD))
    if before is not None:
        operands.append(before)
    size = HEADS_EXPECTED[wave] * BLOCK * 4 * BLOCK * HEAD
    return pl.pallas_call(
        lambda *refs: attend_kernel(wave, kinds, *refs),
        in_specs=[SMEM] + [ANY] * (len(operands) - 1),
        out_specs=ANY,
        out_shape=jax.ShapeDtypeStruct((HALF, PIECE, HEADS * HEAD), jnp.bfloat16),
        input_output_aliases={} if before is None else {len(operands) - 1: 0},
        scratch_shapes=[
            pltpu.VMEM((2, HALF, PIECE, HEAD), jnp.bfloat16),
            pltpu.VMEM((2, 4, HALF, PIECE, HEAD), jnp.bfloat16),
            pltpu.VMEM((2, 4, HALF, PIECE, 2 * HEAD), jnp.bfloat16),
            pltpu.VMEM((2, HALF, PIECE, HEAD), jnp.bfloat16),
            pltpu.SemaphoreType.DMA((2, 9)),
            pltpu.SemaphoreType.DMA((2,)),
        ],
        cost_estimate=pl.CostEstimate(
            flops=16 * size, bytes_accessed=3 * 2**20, transcendentals=size // HEAD
        ),
        compiler_params=BIG,
        name="attend",
    )(*operands)


LANES = [[2 * place(at) + core for at in range(CHIPS)] for core in range(2)]
SWAP = [(device, device ^ 1) for device in range(DEVICES)]


def exchange(array):
    return lax.all_to_all(array, "ctx", 0, 0, axis_index_groups=LANES, tiled=True)


def full_attention(queries, keys, values, chosen_all, me):
    heads = jnp.arange(3 * HEADS, dtype=jnp.int32) // 3
    mine = lax.dynamic_index_in_dim(chosen_all, me, 0, keepdims=False)
    wants = chosen_all == me
    which = jnp.max(jnp.where(wants, heads[None, :], 0), axis=1)
    key_heads = keys.reshape(BLOCK, HEADS, HEAD).transpose(1, 0, 2)
    value_heads = values.reshape(BLOCK, HEADS, HEAD).transpose(1, 0, 2)
    got_key = lax.all_to_all(jnp.take(key_heads, which, axis=0), "ctx", 0, 0, tiled=True)
    got_value = lax.all_to_all(jnp.take(value_heads, which, axis=0), "ctx", 0, 0, tiled=True)
    q_heads = queries.reshape(BLOCK, HEADS, HEAD).transpose(1, 0, 2)
    allowed = jnp.arange(4 * BLOCK)[None, :] >= BLOCK
    allowed = allowed | (jnp.arange(4 * BLOCK)[None, :] <= jnp.arange(BLOCK)[:, None])

    def one_head(head):
        picks = lax.dynamic_slice(mine, (3 * head,), (3,))
        k = jnp.concatenate([key_heads[head], got_key[picks].reshape(3 * BLOCK, HEAD)], axis=0)
        v = jnp.concatenate([value_heads[head], got_value[picks].reshape(3 * BLOCK, HEAD)], axis=0)
        s = jnp.where(allowed, scores_of(q_heads[head], k), -jnp.inf)
        weight = jnp.exp2((s - jnp.max(s, axis=1, keepdims=True)) * SCALE)
        total = jnp.sum(weight, axis=1, keepdims=True)
        o = jnp.dot(weight.astype(jnp.bfloat16), v, preferred_element_type=jnp.float32)
        return (o / total).astype(jnp.bfloat16)

    out = lax.map(one_head, jnp.arange(HEADS))
    return out.transpose(1, 0, 2).reshape(BLOCK, HEADS * HEAD)


def body(queries, keys, values, chosen):
    me = lax.axis_index("ctx").astype(jnp.int32)
    me_ref = me.reshape(1)
    other_keys = lax.ppermute(keys, "ctx", SWAP)
    other_values = lax.ppermute(values, "ctx", SWAP)
    spread = jnp.broadcast_to(chosen.reshape(1, 3 * HEADS), (DEVICES, 3 * HEADS))
    chosen_all = lax.all_to_all(spread, "ctx", 0, 0, tiled=True)
    plan, send, table = pack(chosen_all.T, me_ref, keys, values, other_keys, other_values)
    sent = exchange(send.reshape(CHIPS, SLOT_ROWS, HEAD))
    held = (sent, plan, table, queries, keys, values, other_keys, other_values, me_ref)
    held = lax.optimization_barrier(held)
    arrived, plan, table, queries, keys, values, other_keys, other_values, me_ref = held
    arrived = arrived.reshape(CHIPS, SLOT_PIECES, PIECE, HEAD)
    pieces, *outgoing = forward(plan, me_ref, arrived)
    pieces = exchange(pieces)
    outgoing = dict(zip([0, *range(PARTNER, KINDS)], outgoing))
    forwarded = {}
    out = None
    for wave in range(WAVES):
        if wave:
            for kind in [kind for kind in outgoing if WAVE_OF[kind] == wave]:
                forwarded[kind] = lax.ppermute(outgoing[kind], "ctx", shift_pairs(SHIFTS[kind]))
        out = attend(
            wave,
            out,
            table,
            queries,
            keys,
            values,
            (other_keys, other_values),
            arrived,
            forwarded,
            pieces,
        )
    out = out.reshape(BLOCK, HEADS * HEAD)
    return lax.cond(
        plan[ROW_LEFT, 0] > 0,
        lambda: full_attention(queries, keys, values, chosen_all, me),
        lambda: out,
    )


def solution(mesh):
    placed = (P("ctx", None), P("ctx", None), P("ctx", None), P("ctx", None, None))
    return jax.shard_map(
        body, mesh=mesh, in_specs=placed, out_specs=P("ctx", None), check_vma=False
    )
```

```python
import math

import jax
import jax.numpy as jnp
from jax import lax
from jax.experimental import pallas as pl
from jax.experimental.pallas import tpu as pltpu
from jax.sharding import PartitionSpec as P

HEAD = 128
HEADS = 16
BLOCK = 512
DEVICES = 128
CHIPS = 64
SCALE = math.log2(math.e) / math.sqrt(HEAD)

ONE = [(1, 0, 0), (3, 0, 0), (0, 1, 0), (0, 3, 0), (0, 0, 1), (0, 0, 3)]
PARTNER = 6
SHIFTS = [(0, 0, 0, 1)] * PARTNER
SHIFTS += [(*s, c) for c in (0, 1) for s in ONE]
KINDS = len(SHIFTS)
SPARE = 5
PIECE = 16
WAVES = 4
UP_TO = (8, 12, 16)
WAVE_OF = [1] * (PARTNER + 4) + [2] * 4 + [3] * 4
CODE_PARTNER = CHIPS
CODE_FORWARD = CODE_PARTNER + 1
CODE_SPARE = CODE_FORWARD + KINDS
LIST = 3 * HEADS
COUNT = LIST + WAVES * HEADS
NEED = COUNT + WAVES
TABLE = NEED + 2 * HEADS
HALF = BLOCK // PIECE
SLOT_PIECES = 2 * HALF + SPARE
SLOT_ROWS = SLOT_PIECES * PIECE

ROW_DIRECT = CHIPS
ROW_SPARE = ROW_DIRECT + CHIPS
ROW_FORWARD = ROW_SPARE + CHIPS
ROW_FORWARD_HEAD = ROW_FORWARD + KINDS
ROW_FROM_HEAD = ROW_FORWARD_HEAD + KINDS
ROW_FROM = ROW_FROM_HEAD + SPARE
ROW_FROM_RANK = ROW_FROM + SPARE
ROW_PARTNER = ROW_FROM_RANK + SPARE
ROW_LEFT = ROW_PARTNER + 1
ROWS = -(-(ROW_LEFT + 1) // 8) * 8


def place(chip):
    return ((chip & 3) << 4) | (chip & 12) | (chip >> 4)


def through(device, shift):
    z, x, y, c = device // 32, device // 8 % 4, device // 2 % 4, device % 2
    dz, dx, dy, dc = shift
    return (((z + dz) % 4 * 4 + (x + dx) % 4) * 4 + (y + dy) % 4) * 2 + (c ^ dc)


def shift_pairs(shift):
    return [(through(b, shift), b) for b in range(DEVICES)]


def roll_lanes(array, amount):
    amount = amount % DEVICES
    return pltpu.roll(array, amount, 1) if amount else array


def permuted(array, shift, lane, inverse=False):
    dz, dx, dy, dc = shift
    if inverse:
        dz, dx, dy = -dz % 4, -dx % 4, -dy % 4
    if dz:
        array = roll_lanes(array, -32 * dz)
    if dx:
        inside = (lane // 8) % 4 + dx < 4
        array = jnp.where(inside, roll_lanes(array, -8 * dx), roll_lanes(array, 32 - 8 * dx))
    if dy:
        inside = (lane // 2) % 4 + dy < 4
        array = jnp.where(inside, roll_lanes(array, -2 * dy), roll_lanes(array, 8 - 2 * dy))
    if dc:
        array = jnp.where(lane % 2 == 0, roll_lanes(array, -1), roll_lanes(array, 1))
    return array


def make_plan(chosen_ref, out_ref):
    chip = lax.broadcasted_iota(jnp.int32, (CHIPS, DEVICES), 0)
    lane = lax.broadcasted_iota(jnp.int32, (CHIPS, DEVICES), 1)
    even = jnp.zeros((CHIPS, DEVICES), jnp.int32)
    odd = jnp.zeros((CHIPS, DEVICES), jnp.int32)
    for entry in range(3 * HEADS):
        owner = chosen_ref[entry : entry + 1, :]
        even = even + jnp.where(owner == 2 * chip, entry // 3 + 1, 0)
        odd = odd + jnp.where(owner == 2 * chip + 1, entry // 3 + 1, 0)
    home = lane // 2 == chip
    partner = jnp.sum(jnp.where(home, even + odd, 0), axis=0, keepdims=True)
    even = jnp.where(home, 0, even)
    odd = jnp.where(home, 0, odd)
    waiting = jnp.where(even > 0, odd, 0)
    slot = jnp.where(even > 0, even - 1, jnp.where(odd > 0, odd + 15, -1))
    direct = jnp.where(even > 0, even, odd)
    free = jnp.where(home, 0, jnp.where(direct > 0, 0, 1))
    options = jnp.zeros((CHIPS, DEVICES), jnp.int32)
    for shift in sorted(set(SHIFTS)):
        options = options + permuted(free, shift, lane)
    score = options * 64 + (chip + 17 * lane) % 64
    big = 1 << 20
    out_ref[...] = jnp.zeros((ROWS, DEVICES), jnp.int32)
    for kind, shift in enumerate(SHIFTS):
        able = (waiting > 0) & (permuted(free, shift, lane) > 0)
        rated = jnp.where(able, score, big)
        best = jnp.min(rated, axis=0, keepdims=True)
        picked = able & (rated == best)
        head = jnp.sum(jnp.where(picked, waiting, 0), axis=0, keepdims=True)
        back = permuted(jnp.where(picked, waiting + 16, 0), shift, lane, inverse=True)
        waiting = jnp.where(picked, 0, waiting)
        slot = jnp.where(back > 0, back - 1, slot)
        free = jnp.where(back > 0, 0, free)
        forward = jnp.sum(jnp.where(back > 0, chip + 1, 0), axis=0, keepdims=True)
        out_ref[ROW_FORWARD + kind : ROW_FORWARD + kind + 1, :] = forward
        out_ref[ROW_FORWARD_HEAD + kind : ROW_FORWARD_HEAD + kind + 1, :] = head
    before = lax.broadcasted_iota(jnp.int32, (DEVICES, DEVICES), 0)
    after = lax.broadcasted_iota(jnp.int32, (DEVICES, DEVICES), 1)
    earlier = jnp.where((before < after) & (before % 2 == after % 2), 1.0, 0.0)
    rank = jnp.dot(
        jnp.where(waiting > 0, 1.0, 0.0), earlier, preferred_element_type=jnp.float32
    ).astype(jnp.int32)
    spare = jnp.zeros((CHIPS, DEVICES), jnp.int32)
    for index in range(SPARE):
        for core in range(2):
            chosen = (rank == index) & (lane % 2 == core)
            head = jnp.sum(jnp.where(chosen, waiting, 0), axis=1, keepdims=True)
            spare = jnp.where(lane == 2 * index + core, head, spare)
    out_ref[ROW_SPARE : ROW_SPARE + CHIPS, :] = spare
    excess = jnp.where((waiting > 0) & (rank >= SPARE), 1, 0)
    for index in range(SPARE):
        best = jnp.min(jnp.where(waiting > 0, chip, big), axis=0, keepdims=True)
        picked = (waiting > 0) & (chip == best)
        out_ref[ROW_FROM + index : ROW_FROM + index + 1, :] = jnp.where(best < big, best, 0)
        out_ref[ROW_FROM_RANK + index : ROW_FROM_RANK + index + 1, :] = jnp.minimum(
            jnp.sum(jnp.where(picked, rank, 0), axis=0, keepdims=True), SPARE - 1
        )
        out_ref[ROW_FROM_HEAD + index : ROW_FROM_HEAD + index + 1, :] = jnp.sum(
            jnp.where(picked, waiting, 0), axis=0, keepdims=True
        )
        waiting = jnp.where(picked, 0, waiting)
    excess = excess + waiting
    out_ref[ROW_PARTNER : ROW_PARTNER + 1, :] = partner
    left = jnp.max(jnp.max(excess, axis=0, keepdims=True), axis=1, keepdims=True)
    out_ref[ROW_LEFT : ROW_LEFT + 1, :] = jnp.broadcast_to(left, (1, DEVICES))
    out_ref[0:CHIPS, :] = slot
    out_ref[ROW_DIRECT : ROW_DIRECT + CHIPS, :] = direct


def columns(head):
    return pl.ds(pl.multiple_of(head * HEAD, HEAD), HEAD)


def make_table(plan, me, table):
    for entry in range(TABLE):
        table[entry] = 0

    def note(head_plus, code, wave):
        @pl.when(head_plus > 0)
        def _():
            head = head_plus - 1
            at = table[NEED + HEADS + head]
            table[head * 3 + jnp.minimum(at, 2)] = code
            table[NEED + HEADS + head] = at + 1
            table[NEED + head] = jnp.maximum(table[NEED + head], wave)

    def direct(chip, carry):
        note(plan[ROW_DIRECT + chip, me], place(chip), 0)
        return carry

    lax.fori_loop(0, CHIPS, direct, 0)
    note(plan[ROW_PARTNER, me], CODE_PARTNER, 0)
    for kind in range(KINDS):
        note(plan[ROW_FORWARD_HEAD + kind, me], CODE_FORWARD + kind, WAVE_OF[kind])
    for index in range(SPARE):
        note(plan[ROW_FROM_HEAD + index, me], CODE_SPARE + index, WAVES - 1)
    for ready in range(WAVES):

        def put(head, carry):
            @pl.when(table[NEED + head] == ready)
            def _():
                wave, so_far = ready, 0
                for earlier in range(ready):
                    so_far = so_far + table[COUNT + earlier]
                for later in range(ready, WAVES - 1):
                    so_far = so_far + table[COUNT + later]
                    full = (wave == later) & (so_far >= UP_TO[later])
                    wave = jnp.where(full, later + 1, wave)
                at = table[COUNT + wave]
                table[LIST + wave * HEADS + at] = head
                table[COUNT + wave] = at + 1

            return carry

        lax.fori_loop(0, HEADS, put, 0)


def pack_kernel(chosen, me_ref, keys_in, values_in, other_keys_in, other_values_in, *rest):
    plan_out, send, table, plan, keys, values, other_keys, other_values, sem, sems = rest
    loads = []
    pairs = zip(
        (keys_in, values_in, other_keys_in, other_values_in),
        (keys, values, other_keys, other_values),
    )
    for n, (source, into) in enumerate(pairs):
        loads.append(pltpu.make_async_copy(source, into, sems.at[n]))
        loads[-1].start()
    make_plan(chosen, plan_out)
    to_scalars = pltpu.make_async_copy(plan_out, plan, sems.at[4])
    to_scalars.start()
    to_scalars.wait()
    me = me_ref[0]
    chip, core = me >> 1, me & 1
    for load in loads:
        load.wait()

    def one_slot(dest, carry):
        code = plan[chip, 2 * dest + core]
        at = place(dest)
        cut = columns(jnp.maximum(code, 0) & 15)

        def copy(*sources):
            for half, source in enumerate(sources):
                pltpu.make_async_copy(
                    source.at[:, :, cut],
                    send.at[at >> 1, at & 1, pl.ds(half * HALF, HALF)],
                    sem,
                ).start()

        @pl.when(code >> 4 == core)
        def _():
            copy(keys, values)

        @pl.when(code >> 4 == 1 - core)
        def _():
            copy(other_keys, other_values)

        return carry + jnp.where(code >= 0, 2, 0)

    def one_spare(index, started):
        head = plan[ROW_SPARE + chip, 2 * index + core] - 1
        cut = columns(jnp.maximum(head, 0))

        def copy(*sources):
            for half, source in enumerate(sources):
                pltpu.make_async_copy(
                    source.at[:, :, cut], send.at[:, half, 2 * HALF + index], sem
                ).start()

        @pl.when((head >= 0) & (core == 1))
        def _():
            copy(keys, values)

        @pl.when((head >= 0) & (core == 0))
        def _():
            copy(other_keys, other_values)

        return started + jnp.where(head >= 0, 2, 0)

    started = lax.fori_loop(0, CHIPS, one_slot, 0)
    started = lax.fori_loop(0, SPARE, one_spare, started)
    make_table(plan, me, table)

    def wait_one(index, carry):
        pltpu.make_async_copy(
            keys.at[:, :, pl.ds(0, HEAD)], send.at[0, 0, pl.ds(0, HALF)], sem
        ).wait()
        return carry

    lax.fori_loop(0, started, wait_one, 0)


ANY = pl.BlockSpec(memory_space=pl.ANY)
SMEM = pl.BlockSpec(memory_space=pltpu.SMEM)
VMEM = pl.BlockSpec(memory_space=pltpu.VMEM)
BIG = pltpu.CompilerParams(vmem_limit_bytes=60 * 1024 * 1024)


def tiles(count):
    return jax.ShapeDtypeStruct((count, 2 * HALF, PIECE, HEAD), jnp.bfloat16)


def in_pieces(array):
    return array.reshape(HALF, PIECE, -1)


def pack(chosen_all, me, keys, values, other_keys, other_values):
    whole = pltpu.VMEM((HALF, PIECE, HEADS * HEAD), jnp.bfloat16)
    return pl.pallas_call(
        pack_kernel,
        in_specs=[VMEM, SMEM, ANY, ANY, ANY, ANY],
        out_specs=[VMEM, ANY, SMEM],
        out_shape=[
            jax.ShapeDtypeStruct((ROWS, DEVICES), jnp.int32),
            jax.ShapeDtypeStruct((HALF, 2, SLOT_PIECES, PIECE, HEAD), jnp.bfloat16),
            jax.ShapeDtypeStruct((TABLE,), jnp.int32),
        ],
        scratch_shapes=[pltpu.SMEM((ROWS, DEVICES), jnp.int32)]
        + [whole] * 4
        + [pltpu.SemaphoreType.DMA, pltpu.SemaphoreType.DMA((5,))],
        compiler_params=BIG,
        name="pack",
    )(chosen_all, me, *map(in_pieces, (keys, values, other_keys, other_values)))


def forward_kernel(plan, me_ref, arrived, *rest):
    outs, (moving, spare, gathered, sems, out_sems) = rest[:-5], rest[-5:]
    me = me_ref[0]
    core = me & 1
    load_spare = pltpu.make_async_copy(
        arrived.at[:, pl.ds(2 * HALF, SPARE)], spare, sems.at[KINDS]
    )
    load_spare.start()
    steps = []
    for kind in range(KINDS):
        out = outs[1].at[kind] if kind < PARTNER else outs[kind - PARTNER + 2].at[0]
        chip = plan[ROW_FORWARD + kind, me] - 1
        source = arrived.at[place(jnp.maximum(chip, 0)), pl.ds(0, 2 * HALF)]
        load = pltpu.make_async_copy(source, moving.at[kind], sems.at[kind])
        store = pltpu.make_async_copy(moving.at[kind], out, out_sems.at[kind])
        steps.append((chip >= 0, load, store))
    for used, load, _ in steps:

        @pl.when(used)
        def _():
            load.start()

    load_spare.wait()

    def one_dest(dest, carry):
        device = 2 * dest + core

        def move(index):
            @pl.when(plan[ROW_FROM_HEAD + index, device] > 0)
            def _():
                chip = plan[ROW_FROM + index, device]
                rank = plan[ROW_FROM_RANK + index, device]
                gathered[place(dest), index] = spare[place(chip), rank]
                if index + 1 < SPARE:
                    move(index + 1)

        move(0)
        return carry

    lax.fori_loop(0, CHIPS, one_dest, 0)
    last = pltpu.make_async_copy(gathered, outs[0], out_sems.at[KINDS])
    last.start()
    for used, load, store in steps:

        @pl.when(used)
        def _():
            load.wait()
            store.start()

    for used, _, store in steps:

        @pl.when(used)
        def _():
            store.wait()

    last.wait()


def forward(plan, me, arrived):
    return pl.pallas_call(
        forward_kernel,
        in_specs=[SMEM, SMEM, ANY],
        out_specs=[ANY] * (KINDS - PARTNER + 2),
        out_shape=[jax.ShapeDtypeStruct((CHIPS, SPARE, PIECE, HEAD), jnp.bfloat16)]
        + [tiles(PARTNER)]
        + [tiles(1)] * (KINDS - PARTNER),
        scratch_shapes=[
            pltpu.VMEM((KINDS, 2 * HALF, PIECE, HEAD), jnp.bfloat16),
            pltpu.VMEM((CHIPS, SPARE, PIECE, HEAD), jnp.bfloat16),
            pltpu.VMEM((CHIPS, SPARE, PIECE, HEAD), jnp.bfloat16),
            pltpu.SemaphoreType.DMA((KINDS + 1,)),
            pltpu.SemaphoreType.DMA((KINDS + 1,)),
        ],
        compiler_params=BIG,
        name="forward",
    )(plan, me, arrived)


ROWS_AT_ONCE = 256


def scores_of(query, key):
    return lax.dot_general(
        query, key, (((1,), (1,)), ((), ())), preferred_element_type=jnp.float32
    )


def attend_kernel(wave, kinds, table, queries, keys, values, *rest):
    other_keys, other_values, arrived = rest[:3]
    forwarded = dict(zip(kinds, rest[3 : 3 + len(kinds)]))
    pieces = rest[3 + len(kinds)] if wave == WAVES - 1 else None
    out, query_buf, key_buf, value_buf, out_buf, sems, out_sems = rest[-7:]
    count = table[COUNT + wave]

    def head_at(index):
        return table[LIST + wave * HEADS + index]

    def load(index, slot):
        head = head_at(index)

        def start(j, source_key, source_value):
            into_value = value_buf.at[slot, j, :, :, pl.ds(0, HEAD)]
            pltpu.make_async_copy(source_key, key_buf.at[slot, j], sems.at[slot, 2 * j]).start()
            pltpu.make_async_copy(source_value, into_value, sems.at[slot, 2 * j + 1]).start()

        cut = columns(head)
        pltpu.make_async_copy(queries.at[:, :, cut], query_buf.at[slot], sems.at[slot, 8]).start()
        start(3, keys.at[:, :, cut], values.at[:, :, cut])
        for j in range(3):
            code = table[head * 3 + j]

            @pl.when(code < CHIPS)
            def _():
                start(j, arrived.at[code, pl.ds(0, HALF)], arrived.at[code, pl.ds(HALF, HALF)])

            @pl.when(code >= CHIPS)
            def _():
                @pl.when(code == CODE_PARTNER)
                def _():
                    start(j, other_keys.at[:, :, cut], other_values.at[:, :, cut])

                for kind, ref in forwarded.items():
                    last = kind + (PARTNER if kind == 0 else 1)

                    @pl.when((code >= CODE_FORWARD + kind) & (code < CODE_FORWARD + last))
                    def _():
                        tile = ref.at[code - CODE_FORWARD - kind]
                        start(j, tile.at[pl.ds(0, HALF)], tile.at[pl.ds(HALF, HALF)])

                if pieces is not None:

                    @pl.when(code >= CODE_SPARE)
                    def _():
                        start(j, pieces.at[:, 0, code - CODE_SPARE], pieces.at[:, 1, code - CODE_SPARE])

    def store(index, slot):
        return pltpu.make_async_copy(
            out_buf.at[slot], out.at[:, :, columns(head_at(index))], out_sems.at[slot]
        )

    @pl.when(count > 0)
    def _():
        load(0, 0)
        ones = jnp.ones((HALF, PIECE, HEAD), jnp.bfloat16)
        for slot in range(2):
            for j in range(4):
                value_buf[slot, j, :, :, HEAD:] = ones

    def one_head(index, carry):
        slot = index % 2

        @pl.when(index + 1 < count)
        def _():
            load(index + 1, 1 - slot)

        for j in range(4):
            into_value = value_buf.at[slot, j, :, :, pl.ds(0, HEAD)]
            tile = arrived.at[0, pl.ds(0, HALF)]
            pltpu.make_async_copy(tile, key_buf.at[slot, j], sems.at[slot, 2 * j]).wait()
            pltpu.make_async_copy(tile, into_value, sems.at[slot, 2 * j + 1]).wait()
        pltpu.make_async_copy(tile, query_buf.at[slot], sems.at[slot, 8]).wait()

        @pl.when(index >= 2)
        def _():
            store(index - 2, slot).wait()

        query = query_buf[slot].reshape(BLOCK, HEAD)
        for start in range(0, BLOCK, ROWS_AT_ONCE):
            stop = start + ROWS_AT_ONCE
            q = query[start:stop, :]
            total = highest = None
            for j in (3, 0, 1, 2):
                seen = stop if j == 3 else BLOCK
                scores = scores_of(q, key_buf[slot, j, 0 : seen // PIECE].reshape(seen, HEAD))
                if j == 3:
                    row_iota = lax.broadcasted_iota(jnp.int32, scores.shape, 0) + start
                    col_iota = lax.broadcasted_iota(jnp.int32, scores.shape, 1)
                    scores = jnp.where(col_iota <= row_iota, scores, -jnp.inf)
                top = jnp.max(scores, axis=1, keepdims=True)
                if highest is not None:
                    top = jnp.maximum(highest, top)
                weight = jnp.exp2((scores - top) * SCALE).astype(jnp.bfloat16)
                value = value_buf[slot, j, 0 : seen // PIECE].reshape(seen, 2 * HEAD)
                added = jnp.dot(weight, value, preferred_element_type=jnp.float32)
                if highest is None:
                    total = added
                else:
                    total = total * jnp.exp2((highest - top) * SCALE) + added
                highest = top
            result = (total[:, :HEAD] / total[:, HEAD:]).astype(jnp.bfloat16)
            span = slice(start // PIECE, stop // PIECE)
            out_buf[slot, span] = result.reshape(ROWS_AT_ONCE // PIECE, PIECE, HEAD)
        store(index, slot).start()
        return carry

    lax.fori_loop(0, count, one_head, 0)

    @pl.when(count >= 2)
    def _():
        store(count - 2, count % 2).wait()

    @pl.when(count >= 1)
    def _():
        store(count - 1, (count - 1) % 2).wait()


HEADS_EXPECTED = (9, 4, 2, 2)


def attend(wave, before, table, queries, keys, values, others, arrived, forwarded, pieces):
    kinds = [kind for kind in forwarded if WAVE_OF[kind] <= wave]
    operands = [table, *map(in_pieces, (queries, keys, values, *others)), arrived]
    operands += [forwarded[kind] for kind in kinds]
    if wave == WAVES - 1:
        operands.append(pieces.reshape(HALF, 2, SPARE, PIECE, HEAD))
    if before is not None:
        operands.append(before)
    size = HEADS_EXPECTED[wave] * BLOCK * 4 * BLOCK * HEAD
    return pl.pallas_call(
        lambda *refs: attend_kernel(wave, kinds, *refs),
        in_specs=[SMEM] + [ANY] * (len(operands) - 1),
        out_specs=ANY,
        out_shape=jax.ShapeDtypeStruct((HALF, PIECE, HEADS * HEAD), jnp.bfloat16),
        input_output_aliases={} if before is None else {len(operands) - 1: 0},
        scratch_shapes=[
            pltpu.VMEM((2, HALF, PIECE, HEAD), jnp.bfloat16),
            pltpu.VMEM((2, 4, HALF, PIECE, HEAD), jnp.bfloat16),
            pltpu.VMEM((2, 4, HALF, PIECE, 2 * HEAD), jnp.bfloat16),
            pltpu.VMEM((2, HALF, PIECE, HEAD), jnp.bfloat16),
            pltpu.SemaphoreType.DMA((2, 9)),
            pltpu.SemaphoreType.DMA((2,)),
        ],
        cost_estimate=pl.CostEstimate(
            flops=16 * size, bytes_accessed=3 * 2**20, transcendentals=size // HEAD
        ),
        compiler_params=BIG,
        name="attend",
    )(*operands)


LANES = [[2 * place(at) + core for at in range(CHIPS)] for core in range(2)]
SWAP = [(device, device ^ 1) for device in range(DEVICES)]


def exchange(array):
    return lax.all_to_all(array, "ctx", 0, 0, axis_index_groups=LANES, tiled=True)


def full_attention(queries, keys, values, chosen_all, me):
    heads = jnp.arange(3 * HEADS, dtype=jnp.int32) // 3
    mine = lax.dynamic_index_in_dim(chosen_all, me, 0, keepdims=False)
    wants = chosen_all == me
    which = jnp.max(jnp.where(wants, heads[None, :], 0), axis=1)
    key_heads = keys.reshape(BLOCK, HEADS, HEAD).transpose(1, 0, 2)
    value_heads = values.reshape(BLOCK, HEADS, HEAD).transpose(1, 0, 2)
    got_key = lax.all_to_all(jnp.take(key_heads, which, axis=0), "ctx", 0, 0, tiled=True)
    got_value = lax.all_to_all(jnp.take(value_heads, which, axis=0), "ctx", 0, 0, tiled=True)
    q_heads = queries.reshape(BLOCK, HEADS, HEAD).transpose(1, 0, 2)
    allowed = jnp.arange(4 * BLOCK)[None, :] >= BLOCK
    allowed = allowed | (jnp.arange(4 * BLOCK)[None, :] <= jnp.arange(BLOCK)[:, None])

    def one_head(head):
        picks = lax.dynamic_slice(mine, (3 * head,), (3,))
        k = jnp.concatenate([key_heads[head], got_key[picks].reshape(3 * BLOCK, HEAD)], axis=0)
        v = jnp.concatenate([value_heads[head], got_value[picks].reshape(3 * BLOCK, HEAD)], axis=0)
        s = jnp.where(allowed, scores_of(q_heads[head], k), -jnp.inf)
        weight = jnp.exp2((s - jnp.max(s, axis=1, keepdims=True)) * SCALE)
        total = jnp.sum(weight, axis=1, keepdims=True)
        o = jnp.dot(weight.astype(jnp.bfloat16), v, preferred_element_type=jnp.float32)
        return (o / total).astype(jnp.bfloat16)

    out = lax.map(one_head, jnp.arange(HEADS))
    return out.transpose(1, 0, 2).reshape(BLOCK, HEADS * HEAD)


def body(queries, keys, values, chosen):
    me = lax.axis_index("ctx").astype(jnp.int32)
    me_ref = me.reshape(1)
    other_keys = lax.ppermute(keys, "ctx", SWAP)
    other_values = lax.ppermute(values, "ctx", SWAP)
    spread = jnp.broadcast_to(chosen.reshape(1, 3 * HEADS), (DEVICES, 3 * HEADS))
    chosen_all = lax.all_to_all(spread, "ctx", 0, 0, tiled=True)
    plan, send, table = pack(chosen_all.T, me_ref, keys, values, other_keys, other_values)
    sent = exchange(send.reshape(CHIPS, SLOT_ROWS, HEAD))
    held = (sent, plan, table, queries, keys, values, other_keys, other_values, me_ref)
    held = lax.optimization_barrier(held)
    arrived, plan, table, queries, keys, values, other_keys, other_values, me_ref = held
    arrived = arrived.reshape(CHIPS, SLOT_PIECES, PIECE, HEAD)
    pieces, *outgoing = forward(plan, me_ref, arrived)
    pieces = exchange(pieces)
    outgoing = dict(zip([0, *range(PARTNER, KINDS)], outgoing))
    forwarded = {}
    out = None
    for wave in range(WAVES):
        if wave:
            for kind in [kind for kind in outgoing if WAVE_OF[kind] == wave]:
                forwarded[kind] = lax.ppermute(outgoing[kind], "ctx", shift_pairs(SHIFTS[kind]))
        out = attend(
            wave,
            out,
            table,
            queries,
            keys,
            values,
            (other_keys, other_values),
            arrived,
            forwarded,
            pieces,
        )
    out = out.reshape(BLOCK, HEADS * HEAD)
    return lax.cond(
        plan[ROW_LEFT, 0] > 0,
        lambda: full_attention(queries, keys, values, chosen_all, me),
        lambda: out,
    )


def solution(mesh):
    placed = (P("ctx", None), P("ctx", None), P("ctx", None), P("ctx", None, None))
    return jax.shard_map(
        body, mesh=mesh, in_specs=placed, out_specs=P("ctx", None), check_vma=False
    )
```

```python
import math

import jax
import jax.numpy as jnp
from jax import lax
from jax.experimental import pallas as pl
from jax.experimental.pallas import tpu as pltpu
from jax.sharding import PartitionSpec as P

HEAD = 128
HEADS = 16
BLOCK = 512
DEVICES = 128
CHIPS = 64
SCALE = math.log2(math.e) / math.sqrt(HEAD)

ONE = [(1, 0, 0), (3, 0, 0), (0, 1, 0), (0, 3, 0), (0, 0, 1), (0, 0, 3)]
PARTNER = 6
SHIFTS = [(0, 0, 0, 1)] * PARTNER
SHIFTS += [(*s, c) for c in (0, 1) for s in ONE]
KINDS = len(SHIFTS)
SPARE = 5
PIECE = 16
WAVES = 4
UP_TO = (8, 12, 16)
WAVE_OF = [1] * (PARTNER + 4) + [2] * 4 + [3] * 4
CODE_PARTNER = CHIPS
CODE_FORWARD = CODE_PARTNER + 1
CODE_SPARE = CODE_FORWARD + KINDS
LIST = 3 * HEADS
COUNT = LIST + WAVES * HEADS
NEED = COUNT + WAVES
TABLE = NEED + 2 * HEADS
HALF = BLOCK // PIECE
SLOT_PIECES = 2 * HALF + SPARE
SLOT_ROWS = SLOT_PIECES * PIECE

ROW_DIRECT = CHIPS
ROW_SPARE = ROW_DIRECT + CHIPS
ROW_FORWARD = ROW_SPARE + CHIPS
ROW_FORWARD_HEAD = ROW_FORWARD + KINDS
ROW_FROM_HEAD = ROW_FORWARD_HEAD + KINDS
ROW_FROM = ROW_FROM_HEAD + SPARE
ROW_FROM_RANK = ROW_FROM + SPARE
ROW_PARTNER = ROW_FROM_RANK + SPARE
ROW_LEFT = ROW_PARTNER + 1
ROWS = -(-(ROW_LEFT + 1) // 8) * 8


def place(chip):
    return ((chip & 3) << 4) | (chip & 12) | (chip >> 4)


def through(device, shift):
    z, x, y, c = device // 32, device // 8 % 4, device // 2 % 4, device % 2
    dz, dx, dy, dc = shift
    return (((z + dz) % 4 * 4 + (x + dx) % 4) * 4 + (y + dy) % 4) * 2 + (c ^ dc)


def shift_pairs(shift):
    return [(through(b, shift), b) for b in range(DEVICES)]


def roll_lanes(array, amount):
    amount = amount % DEVICES
    return pltpu.roll(array, amount, 1) if amount else array


def permuted(array, shift, lane, inverse=False):
    dz, dx, dy, dc = shift
    if inverse:
        dz, dx, dy = -dz % 4, -dx % 4, -dy % 4
    if dz:
        array = roll_lanes(array, -32 * dz)
    if dx:
        inside = (lane // 8) % 4 + dx < 4
        array = jnp.where(inside, roll_lanes(array, -8 * dx), roll_lanes(array, 32 - 8 * dx))
    if dy:
        inside = (lane // 2) % 4 + dy < 4
        array = jnp.where(inside, roll_lanes(array, -2 * dy), roll_lanes(array, 8 - 2 * dy))
    if dc:
        array = jnp.where(lane % 2 == 0, roll_lanes(array, -1), roll_lanes(array, 1))
    return array


def make_plan(chosen_ref, out_ref):
    chip = lax.broadcasted_iota(jnp.int32, (CHIPS, DEVICES), 0)
    lane = lax.broadcasted_iota(jnp.int32, (CHIPS, DEVICES), 1)
    even = jnp.zeros((CHIPS, DEVICES), jnp.int32)
    odd = jnp.zeros((CHIPS, DEVICES), jnp.int32)
    for entry in range(3 * HEADS):
        owner = chosen_ref[entry : entry + 1, :]
        even = even + jnp.where(owner == 2 * chip, entry // 3 + 1, 0)
        odd = odd + jnp.where(owner == 2 * chip + 1, entry // 3 + 1, 0)
    home = lane // 2 == chip
    partner = jnp.sum(jnp.where(home, even + odd, 0), axis=0, keepdims=True)
    even = jnp.where(home, 0, even)
    odd = jnp.where(home, 0, odd)
    waiting = jnp.where(even > 0, odd, 0)
    slot = jnp.where(even > 0, even - 1, jnp.where(odd > 0, odd + 15, -1))
    direct = jnp.where(even > 0, even, odd)
    free = jnp.where(home, 0, jnp.where(direct > 0, 0, 1))
    options = jnp.zeros((CHIPS, DEVICES), jnp.int32)
    for shift in sorted(set(SHIFTS)):
        options = options + permuted(free, shift, lane)
    score = options * 64 + (chip + 17 * lane) % 64
    big = 1 << 20
    out_ref[...] = jnp.zeros((ROWS, DEVICES), jnp.int32)
    for kind, shift in enumerate(SHIFTS):
        able = (waiting > 0) & (permuted(free, shift, lane) > 0)
        rated = jnp.where(able, score, big)
        best = jnp.min(rated, axis=0, keepdims=True)
        picked = able & (rated == best)
        head = jnp.sum(jnp.where(picked, waiting, 0), axis=0, keepdims=True)
        back = permuted(jnp.where(picked, waiting + 16, 0), shift, lane, inverse=True)
        waiting = jnp.where(picked, 0, waiting)
        slot = jnp.where(back > 0, back - 1, slot)
        free = jnp.where(back > 0, 0, free)
        forward = jnp.sum(jnp.where(back > 0, chip + 1, 0), axis=0, keepdims=True)
        out_ref[ROW_FORWARD + kind : ROW_FORWARD + kind + 1, :] = forward
        out_ref[ROW_FORWARD_HEAD + kind : ROW_FORWARD_HEAD + kind + 1, :] = head
    before = lax.broadcasted_iota(jnp.int32, (DEVICES, DEVICES), 0)
    after = lax.broadcasted_iota(jnp.int32, (DEVICES, DEVICES), 1)
    earlier = jnp.where((before < after) & (before % 2 == after % 2), 1.0, 0.0)
    rank = jnp.dot(
        jnp.where(waiting > 0, 1.0, 0.0), earlier, preferred_element_type=jnp.float32
    ).astype(jnp.int32)
    spare = jnp.zeros((CHIPS, DEVICES), jnp.int32)
    for index in range(SPARE):
        for core in range(2):
            chosen = (rank == index) & (lane % 2 == core)
            head = jnp.sum(jnp.where(chosen, waiting, 0), axis=1, keepdims=True)
            spare = jnp.where(lane == 2 * index + core, head, spare)
    out_ref[ROW_SPARE : ROW_SPARE + CHIPS, :] = spare
    excess = jnp.where((waiting > 0) & (rank >= SPARE), 1, 0)
    for index in range(SPARE):
        best = jnp.min(jnp.where(waiting > 0, chip, big), axis=0, keepdims=True)
        picked = (waiting > 0) & (chip == best)
        out_ref[ROW_FROM + index : ROW_FROM + index + 1, :] = jnp.where(best < big, best, 0)
        out_ref[ROW_FROM_RANK + index : ROW_FROM_RANK + index + 1, :] = jnp.minimum(
            jnp.sum(jnp.where(picked, rank, 0), axis=0, keepdims=True), SPARE - 1
        )
        out_ref[ROW_FROM_HEAD + index : ROW_FROM_HEAD + index + 1, :] = jnp.sum(
            jnp.where(picked, waiting, 0), axis=0, keepdims=True
        )
        waiting = jnp.where(picked, 0, waiting)
    excess = excess + waiting
    out_ref[ROW_PARTNER : ROW_PARTNER + 1, :] = partner
    left = jnp.max(jnp.max(excess, axis=0, keepdims=True), axis=1, keepdims=True)
    out_ref[ROW_LEFT : ROW_LEFT + 1, :] = jnp.broadcast_to(left, (1, DEVICES))
    out_ref[0:CHIPS, :] = slot
    out_ref[ROW_DIRECT : ROW_DIRECT + CHIPS, :] = direct


def columns(head):
    return pl.ds(pl.multiple_of(head * HEAD, HEAD), HEAD)


def make_table(plan, me, table):
    for entry in range(TABLE):
        table[entry] = 0

    def note(head_plus, code, wave):
        @pl.when(head_plus > 0)
        def _():
            head = head_plus - 1
            at = table[NEED + HEADS + head]
            table[head * 3 + jnp.minimum(at, 2)] = code
            table[NEED + HEADS + head] = at + 1
            table[NEED + head] = jnp.maximum(table[NEED + head], wave)

    def direct(chip, carry):
        note(plan[ROW_DIRECT + chip, me], place(chip), 0)
        return carry

    lax.fori_loop(0, CHIPS, direct, 0)
    note(plan[ROW_PARTNER, me], CODE_PARTNER, 0)
    for kind in range(KINDS):
        note(plan[ROW_FORWARD_HEAD + kind, me], CODE_FORWARD + kind, WAVE_OF[kind])
    for index in range(SPARE):
        note(plan[ROW_FROM_HEAD + index, me], CODE_SPARE + index, WAVES - 1)
    for ready in range(WAVES):

        def put(head, carry):
            @pl.when(table[NEED + head] == ready)
            def _():
                wave, so_far = ready, 0
                for earlier in range(ready):
                    so_far = so_far + table[COUNT + earlier]
                for later in range(ready, WAVES - 1):
                    so_far = so_far + table[COUNT + later]
                    full = (wave == later) & (so_far >= UP_TO[later])
                    wave = jnp.where(full, later + 1, wave)
                at = table[COUNT + wave]
                table[LIST + wave * HEADS + at] = head
                table[COUNT + wave] = at + 1

            return carry

        lax.fori_loop(0, HEADS, put, 0)


def pack_kernel(chosen, me_ref, keys_in, values_in, other_keys_in, other_values_in, *rest):
    plan_out, send, table, left, plan, keys, values, other_keys, other_values, sem, sems = rest
    loads = []
    pairs = zip(
        (keys_in, values_in, other_keys_in, other_values_in),
        (keys, values, other_keys, other_values),
    )
    for n, (source, into) in enumerate(pairs):
        loads.append(pltpu.make_async_copy(source, into, sems.at[n]))
        loads[-1].start()
    make_plan(chosen, plan_out)
    to_scalars = pltpu.make_async_copy(plan_out, plan, sems.at[4])
    to_scalars.start()
    to_scalars.wait()
    me = me_ref[0]
    chip, core = me >> 1, me & 1
    for load in loads:
        load.wait()

    def one_slot(dest, carry):
        code = plan[chip, 2 * dest + core]
        at = place(dest)
        cut = columns(jnp.maximum(code, 0) & 15)

        def copy(*sources):
            for half, source in enumerate(sources):
                pltpu.make_async_copy(
                    source.at[:, :, cut],
                    send.at[at >> 1, at & 1, pl.ds(half * HALF, HALF)],
                    sem,
                ).start()

        @pl.when(code >> 4 == core)
        def _():
            copy(keys, values)

        @pl.when(code >> 4 == 1 - core)
        def _():
            copy(other_keys, other_values)

        return carry + jnp.where(code >= 0, 2, 0)

    def one_spare(index, started):
        head = plan[ROW_SPARE + chip, 2 * index + core] - 1
        cut = columns(jnp.maximum(head, 0))

        def copy(*sources):
            for half, source in enumerate(sources):
                pltpu.make_async_copy(
                    source.at[:, :, cut], send.at[:, half, 2 * HALF + index], sem
                ).start()

        @pl.when((head >= 0) & (core == 1))
        def _():
            copy(keys, values)

        @pl.when((head >= 0) & (core == 0))
        def _():
            copy(other_keys, other_values)

        return started + jnp.where(head >= 0, 2, 0)

    started = lax.fori_loop(0, CHIPS, one_slot, 0)
    started = lax.fori_loop(0, SPARE, one_spare, started)
    make_table(plan, me, table)
    left[0] = plan[ROW_LEFT, 0]

    def wait_one(index, carry):
        pltpu.make_async_copy(
            keys.at[:, :, pl.ds(0, HEAD)], send.at[0, 0, pl.ds(0, HALF)], sem
        ).wait()
        return carry

    lax.fori_loop(0, started, wait_one, 0)


ANY = pl.BlockSpec(memory_space=pl.ANY)
SMEM = pl.BlockSpec(memory_space=pltpu.SMEM)
VMEM = pl.BlockSpec(memory_space=pltpu.VMEM)
BIG = pltpu.CompilerParams(vmem_limit_bytes=60 * 1024 * 1024)


def tiles(count):
    return jax.ShapeDtypeStruct((count, 2 * HALF, PIECE, HEAD), jnp.bfloat16)


def in_pieces(array):
    return array.reshape(HALF, PIECE, -1)


def pack(chosen_all, me, keys, values, other_keys, other_values):
    whole = pltpu.VMEM((HALF, PIECE, HEADS * HEAD), jnp.bfloat16)
    return pl.pallas_call(
        pack_kernel,
        in_specs=[VMEM, SMEM, ANY, ANY, ANY, ANY],
        out_specs=[VMEM, ANY, SMEM, SMEM],
        out_shape=[
            jax.ShapeDtypeStruct((ROWS, DEVICES), jnp.int32),
            jax.ShapeDtypeStruct((HALF, 2, SLOT_PIECES, PIECE, HEAD), jnp.bfloat16),
            jax.ShapeDtypeStruct((TABLE,), jnp.int32),
            jax.ShapeDtypeStruct((1,), jnp.int32),
        ],
        scratch_shapes=[pltpu.SMEM((ROWS, DEVICES), jnp.int32)]
        + [whole] * 4
        + [pltpu.SemaphoreType.DMA, pltpu.SemaphoreType.DMA((5,))],
        compiler_params=BIG,
        name="pack",
    )(chosen_all, me, *map(in_pieces, (keys, values, other_keys, other_values)))


def forward_kernel(plan, me_ref, arrived, *rest):
    outs, (moving, spare, gathered, sems, out_sems) = rest[:-5], rest[-5:]
    me = me_ref[0]
    core = me & 1
    load_spare = pltpu.make_async_copy(
        arrived.at[:, pl.ds(2 * HALF, SPARE)], spare, sems.at[KINDS]
    )
    load_spare.start()
    steps = []
    for kind in range(KINDS):
        out = outs[1].at[kind] if kind < PARTNER else outs[kind - PARTNER + 2].at[0]
        chip = plan[ROW_FORWARD + kind, me] - 1
        source = arrived.at[place(jnp.maximum(chip, 0)), pl.ds(0, 2 * HALF)]
        load = pltpu.make_async_copy(source, moving.at[kind], sems.at[kind])
        store = pltpu.make_async_copy(moving.at[kind], out, out_sems.at[kind])
        steps.append((chip >= 0, load, store))
    for used, load, _ in steps:

        @pl.when(used)
        def _():
            load.start()

    load_spare.wait()

    def one_dest(dest, carry):
        device = 2 * dest + core

        def move(index):
            @pl.when(plan[ROW_FROM_HEAD + index, device] > 0)
            def _():
                chip = plan[ROW_FROM + index, device]
                rank = plan[ROW_FROM_RANK + index, device]
                gathered[place(dest), index] = spare[place(chip), rank]
                if index + 1 < SPARE:
                    move(index + 1)

        move(0)
        return carry

    lax.fori_loop(0, CHIPS, one_dest, 0)
    last = pltpu.make_async_copy(gathered, outs[0], out_sems.at[KINDS])
    last.start()
    for used, load, store in steps:

        @pl.when(used)
        def _():
            load.wait()
            store.start()

    for used, _, store in steps:

        @pl.when(used)
        def _():
            store.wait()

    last.wait()


def forward(plan, me, arrived):
    return pl.pallas_call(
        forward_kernel,
        in_specs=[SMEM, SMEM, ANY],
        out_specs=[ANY] * (KINDS - PARTNER + 2),
        out_shape=[jax.ShapeDtypeStruct((CHIPS, SPARE, PIECE, HEAD), jnp.bfloat16)]
        + [tiles(PARTNER)]
        + [tiles(1)] * (KINDS - PARTNER),
        scratch_shapes=[
            pltpu.VMEM((KINDS, 2 * HALF, PIECE, HEAD), jnp.bfloat16),
            pltpu.VMEM((CHIPS, SPARE, PIECE, HEAD), jnp.bfloat16),
            pltpu.VMEM((CHIPS, SPARE, PIECE, HEAD), jnp.bfloat16),
            pltpu.SemaphoreType.DMA((KINDS + 1,)),
            pltpu.SemaphoreType.DMA((KINDS + 1,)),
        ],
        compiler_params=BIG,
        name="forward",
    )(plan, me, arrived)


ROWS_AT_ONCE = 256


def scores_of(query, key):
    return lax.dot_general(
        query, key, (((1,), (1,)), ((), ())), preferred_element_type=jnp.float32
    )


def attend_kernel(wave, kinds, table, queries, keys, values, *rest):
    other_keys, other_values, arrived = rest[:3]
    forwarded = dict(zip(kinds, rest[3 : 3 + len(kinds)]))
    pieces = rest[3 + len(kinds)] if wave == WAVES - 1 else None
    out, query_buf, key_buf, value_buf, out_buf, sems, out_sems = rest[-7:]
    count = table[COUNT + wave]

    def head_at(index):
        return table[LIST + wave * HEADS + index]

    def load(index, slot):
        head = head_at(index)

        def start(j, source_key, source_value):
            into_value = value_buf.at[slot, j, :, :, pl.ds(0, HEAD)]
            pltpu.make_async_copy(source_key, key_buf.at[slot, j], sems.at[slot, 2 * j]).start()
            pltpu.make_async_copy(source_value, into_value, sems.at[slot, 2 * j + 1]).start()

        cut = columns(head)
        pltpu.make_async_copy(queries.at[:, :, cut], query_buf.at[slot], sems.at[slot, 8]).start()
        start(3, keys.at[:, :, cut], values.at[:, :, cut])
        for j in range(3):
            code = table[head * 3 + j]

            @pl.when(code < CHIPS)
            def _():
                start(j, arrived.at[code, pl.ds(0, HALF)], arrived.at[code, pl.ds(HALF, HALF)])

            @pl.when(code >= CHIPS)
            def _():
                @pl.when(code == CODE_PARTNER)
                def _():
                    start(j, other_keys.at[:, :, cut], other_values.at[:, :, cut])

                for kind, ref in forwarded.items():
                    last = kind + (PARTNER if kind == 0 else 1)

                    @pl.when((code >= CODE_FORWARD + kind) & (code < CODE_FORWARD + last))
                    def _():
                        tile = ref.at[code - CODE_FORWARD - kind]
                        start(j, tile.at[pl.ds(0, HALF)], tile.at[pl.ds(HALF, HALF)])

                if pieces is not None:

                    @pl.when(code >= CODE_SPARE)
                    def _():
                        start(j, pieces.at[:, 0, code - CODE_SPARE], pieces.at[:, 1, code - CODE_SPARE])

    def store(index, slot):
        return pltpu.make_async_copy(
            out_buf.at[slot], out.at[:, :, columns(head_at(index))], out_sems.at[slot]
        )

    @pl.when(count > 0)
    def _():
        load(0, 0)
        ones = jnp.ones((HALF, PIECE, HEAD), jnp.bfloat16)
        for slot in range(2):
            for j in range(4):
                value_buf[slot, j, :, :, HEAD:] = ones

    def one_head(index, carry):
        slot = index % 2

        @pl.when(index + 1 < count)
        def _():
            load(index + 1, 1 - slot)

        for j in range(4):
            into_value = value_buf.at[slot, j, :, :, pl.ds(0, HEAD)]
            tile = arrived.at[0, pl.ds(0, HALF)]
            pltpu.make_async_copy(tile, key_buf.at[slot, j], sems.at[slot, 2 * j]).wait()
            pltpu.make_async_copy(tile, into_value, sems.at[slot, 2 * j + 1]).wait()
        pltpu.make_async_copy(tile, query_buf.at[slot], sems.at[slot, 8]).wait()

        @pl.when(index >= 2)
        def _():
            store(index - 2, slot).wait()

        query = query_buf[slot].reshape(BLOCK, HEAD)
        for start in range(0, BLOCK, ROWS_AT_ONCE):
            stop = start + ROWS_AT_ONCE
            q = query[start:stop, :]
            total = highest = None
            for j in (3, 0, 1, 2):
                seen = stop if j == 3 else BLOCK
                scores = scores_of(q, key_buf[slot, j, 0 : seen // PIECE].reshape(seen, HEAD))
                if j == 3:
                    row_iota = lax.broadcasted_iota(jnp.int32, scores.shape, 0) + start
                    col_iota = lax.broadcasted_iota(jnp.int32, scores.shape, 1)
                    scores = jnp.where(col_iota <= row_iota, scores, -jnp.inf)
                top = jnp.max(scores, axis=1, keepdims=True)
                if highest is not None:
                    top = jnp.maximum(highest, top)
                weight = jnp.exp2((scores - top) * SCALE).astype(jnp.bfloat16)
                value = value_buf[slot, j, 0 : seen // PIECE].reshape(seen, 2 * HEAD)
                added = jnp.dot(weight, value, preferred_element_type=jnp.float32)
                if highest is None:
                    total = added
                else:
                    total = total * jnp.exp2((highest - top) * SCALE) + added
                highest = top
            result = (total[:, :HEAD] / total[:, HEAD:]).astype(jnp.bfloat16)
            span = slice(start // PIECE, stop // PIECE)
            out_buf[slot, span] = result.reshape(ROWS_AT_ONCE // PIECE, PIECE, HEAD)
        store(index, slot).start()
        return carry

    lax.fori_loop(0, count, one_head, 0)

    @pl.when(count >= 2)
    def _():
        store(count - 2, count % 2).wait()

    @pl.when(count >= 1)
    def _():
        store(count - 1, (count - 1) % 2).wait()


HEADS_EXPECTED = (9, 4, 2, 2)


def attend(wave, before, table, queries, keys, values, others, arrived, forwarded, pieces):
    kinds = [kind for kind in forwarded if WAVE_OF[kind] <= wave]
    operands = [table, *map(in_pieces, (queries, keys, values, *others)), arrived]
    operands += [forwarded[kind] for kind in kinds]
    if wave == WAVES - 1:
        operands.append(pieces.reshape(HALF, 2, SPARE, PIECE, HEAD))
    if before is not None:
        operands.append(before)
    size = HEADS_EXPECTED[wave] * BLOCK * 4 * BLOCK * HEAD
    return pl.pallas_call(
        lambda *refs: attend_kernel(wave, kinds, *refs),
        in_specs=[SMEM] + [ANY] * (len(operands) - 1),
        out_specs=ANY,
        out_shape=jax.ShapeDtypeStruct((HALF, PIECE, HEADS * HEAD), jnp.bfloat16),
        input_output_aliases={} if before is None else {len(operands) - 1: 0},
        scratch_shapes=[
            pltpu.VMEM((2, HALF, PIECE, HEAD), jnp.bfloat16),
            pltpu.VMEM((2, 4, HALF, PIECE, HEAD), jnp.bfloat16),
            pltpu.VMEM((2, 4, HALF, PIECE, 2 * HEAD), jnp.bfloat16),
            pltpu.VMEM((2, HALF, PIECE, HEAD), jnp.bfloat16),
            pltpu.SemaphoreType.DMA((2, 9)),
            pltpu.SemaphoreType.DMA((2,)),
        ],
        cost_estimate=pl.CostEstimate(
            flops=16 * size, bytes_accessed=3 * 2**20, transcendentals=size // HEAD
        ),
        compiler_params=BIG,
        name="attend",
    )(*operands)


LANES = [[2 * place(at) + core for at in range(CHIPS)] for core in range(2)]
SWAP = [(device, device ^ 1) for device in range(DEVICES)]


def exchange(array):
    return lax.all_to_all(array, "ctx", 0, 0, axis_index_groups=LANES, tiled=True)


def full_attention(queries, keys, values, chosen_all, me):
    heads = jnp.arange(3 * HEADS, dtype=jnp.int32) // 3
    mine = lax.dynamic_index_in_dim(chosen_all, me, 0, keepdims=False)
    wants = chosen_all == me
    which = jnp.max(jnp.where(wants, heads[None, :], 0), axis=1)
    key_heads = keys.reshape(BLOCK, HEADS, HEAD).transpose(1, 0, 2)
    value_heads = values.reshape(BLOCK, HEADS, HEAD).transpose(1, 0, 2)
    got_key = lax.all_to_all(jnp.take(key_heads, which, axis=0), "ctx", 0, 0, tiled=True)
    got_value = lax.all_to_all(jnp.take(value_heads, which, axis=0), "ctx", 0, 0, tiled=True)
    q_heads = queries.reshape(BLOCK, HEADS, HEAD).transpose(1, 0, 2)
    allowed = jnp.arange(4 * BLOCK)[None, :] >= BLOCK
    allowed = allowed | (jnp.arange(4 * BLOCK)[None, :] <= jnp.arange(BLOCK)[:, None])

    def one_head(head):
        picks = lax.dynamic_slice(mine, (3 * head,), (3,))
        k = jnp.concatenate([key_heads[head], got_key[picks].reshape(3 * BLOCK, HEAD)], axis=0)
        v = jnp.concatenate([value_heads[head], got_value[picks].reshape(3 * BLOCK, HEAD)], axis=0)
        s = jnp.where(allowed, scores_of(q_heads[head], k), -jnp.inf)
        weight = jnp.exp2((s - jnp.max(s, axis=1, keepdims=True)) * SCALE)
        total = jnp.sum(weight, axis=1, keepdims=True)
        o = jnp.dot(weight.astype(jnp.bfloat16), v, preferred_element_type=jnp.float32)
        return (o / total).astype(jnp.bfloat16)

    out = lax.map(one_head, jnp.arange(HEADS))
    return out.transpose(1, 0, 2).reshape(BLOCK, HEADS * HEAD)


def body(queries, keys, values, chosen):
    me = lax.axis_index("ctx").astype(jnp.int32)
    me_ref = me.reshape(1)
    other_keys = lax.ppermute(keys, "ctx", SWAP)
    other_values = lax.ppermute(values, "ctx", SWAP)
    spread = jnp.broadcast_to(chosen.reshape(1, 3 * HEADS), (DEVICES, 3 * HEADS))
    chosen_all = lax.all_to_all(spread, "ctx", 0, 0, tiled=True)
    plan, send, table, left = pack(chosen_all.T, me_ref, keys, values, other_keys, other_values)
    sent = exchange(send.reshape(CHIPS, SLOT_ROWS, HEAD))
    held = (sent, left, plan, table, queries, keys, values, other_keys, other_values, me_ref)
    held = lax.optimization_barrier(held)
    arrived, left, plan, table, queries, keys, values, other_keys, other_values, me_ref = held
    arrived = arrived.reshape(CHIPS, SLOT_PIECES, PIECE, HEAD)
    pieces, *outgoing = forward(plan, me_ref, arrived)
    pieces = exchange(pieces)
    outgoing = dict(zip([0, *range(PARTNER, KINDS)], outgoing))
    forwarded = {}
    out = None
    for wave in range(WAVES):
        if wave:
            for kind in [kind for kind in outgoing if WAVE_OF[kind] == wave]:
                forwarded[kind] = lax.ppermute(outgoing[kind], "ctx", shift_pairs(SHIFTS[kind]))
        out = attend(
            wave,
            out,
            table,
            queries,
            keys,
            values,
            (other_keys, other_values),
            arrived,
            forwarded,
            pieces,
        )
    out = out.reshape(BLOCK, HEADS * HEAD)
    return lax.cond(
        left[0] > 0,
        lambda: full_attention(queries, keys, values, chosen_all, me),
        lambda: out,
    )


def solution(mesh):
    placed = (P("ctx", None), P("ctx", None), P("ctx", None), P("ctx", None, None))
    return jax.shard_map(
        body, mesh=mesh, in_specs=placed, out_specs=P("ctx", None), check_vma=False
    )
```
